32 devices in a mesh: expert: 8 (over z, core), shard: 4 (over y, x).
Axes of the slice: x: 2, y: 2, z: 4, core: 2. Of those that a mesh axis runs over, the one named last changes fastest.
Arguments:
- tokens: bfloat16 [25216, 768], P(('expert', 'shard')), may hold values from -6 to 6
- routes: int32 [25216, 2], P(('expert', 'shard')), may hold values from 0 to 15, all different within a row; in each aligned block of 788 rows (0 to 787, 788 to 1575, ...) at most 152 rows name the same one
- cotangent: bfloat16 [25216, 768], P(('expert', 'shard')), may hold values from -6 to 6
- gain_attn: bfloat16 [768], P('shard'), may hold values from 0.5 to 1.5
- w_qkv: bfloat16 [768, 2304], P('shard'), may hold values from -0.21875 to 0.21875
- w_proj: bfloat16 [768, 768], P('shard'), may hold values from -0.875 to 0.875
- gain_moe: bfloat16 [768], P('shard'), may hold values from 0.5 to 1.5
- w_router: bfloat16 [768, 16], P('shard'), may hold values from -0.4375 to 0.4375
- w_in: bfloat16 [16, 768, 3072], P('expert', None, 'shard'), may hold values from -0.21875 to 0.21875
- w_out: bfloat16 [16, 3072, 768], P('expert', 'shard'), may hold values from -0.15625 to 0.15625
- v_attn: float32 [768], P('shard'), may hold values from 4300.8 to 17203.2
- v_moe: float32 [768], P('shard'), may hold values from 26476.8 to 105907.2
- row_qkv: float32 [768], P('shard'), may hold values from 1433.6 to 5734.4
- col_qkv: float32 [2304], replicated, may hold values from 1433.6 to 5734.4
- row_proj: float32 [768], P('shard'), may hold values from 358.4 to 1433.6
- col_proj: float32 [768], replicated, may hold values from 358.4 to 1433.6
- row_router: float32 [768], P('shard'), may hold values from 211814.4 to 847257.6
- col_router: float32 [16], replicated, may hold values from 211814.4 to 847257.6
- row_in: float32 [16, 768], P('expert'), may hold values from 96.6 to 386.4
- col_in: float32 [16, 3072], P('expert', 'shard'), may hold values from 96.6 to 386.4
- row_out: float32 [16, 3072], P('expert', 'shard'), may hold values from 198.8 to 795.2
- col_out: float32 [16, 768], P('expert'), may hold values from 198.8 to 795.2
Outputs:
- block_out: bfloat16 [25216, 768], P(('expert', 'shard'))
- grad_tokens: float32 [25216, 768], P(('expert', 'shard'))
- dense_rms: float32 [5], replicated
- expert_rms: float32 [16, 2], P('expert')
- grad_gain_attn: float32 [768], P('shard')
- new_gain_attn: float32 [768], P('shard')
- v_attn_new: float32 [768], P('shard')
- grad_gain_moe: float32 [768], P('shard')
- new_gain_moe: float32 [768], P('shard')
- v_moe_new: float32 [768], P('shard')
- grad_w_qkv: float32 [768, 2304], P('shard')
- new_w_qkv: float32 [768, 2304], P('shard')
- row_qkv_new: float32 [768], P('shard')
- col_qkv_new: float32 [2304], replicated
- grad_w_proj: float32 [768, 768], P('shard')
- new_w_proj: float32 [768, 768], P('shard')
- row_proj_new: float32 [768], P('shard')
- col_proj_new: float32 [768], replicated
- grad_w_router: float32 [768, 16], P('shard')
- new_w_router: float32 [768, 16], P('shard')
- row_router_new: float32 [768], P('shard')
- col_router_new: float32 [16], replicated
- grad_w_in: float32 [16, 768, 3072], P('expert', None, 'shard')
- new_w_in: float32 [16, 768, 3072], P('expert', None, 'shard')
- row_in_new: float32 [16, 768], P('expert')
- col_in_new: float32 [16, 3072], P('expert', 'shard')
- grad_w_out: float32 [16, 3072, 768], P('expert', 'shard')
- new_w_out: float32 [16, 3072, 768], P('expert', 'shard')
- row_out_new: float32 [16, 3072], P('expert', 'shard')
- col_out_new: float32 [16, 768], P('expert')
The draws below stay inside these ranges and needn't reach their ends.
Inputs may be any that keep to these rules, and one draw needn't show every extreme that they name: `routes`: each row names two different experts; within each aligned block of 788 rows (the rows of one device) no expert is named by more than 152 rows.
All inputs are finite; a program needn't handle non-finite values.
Results may differ from the reference program's by a relative error of at most 0.015.
Values may be sent and summed in bfloat16 or wider, within the bound.
A program may use at most 256 MiB of HBM per device.

```python
import math
import jax
import jax.numpy as jnp
import numpy as np
from jax import lax

D = 768
HEADS = 12
HEAD = 64
FF = 3072
SEQ = 197
IMG_DEV = 4
EXPERTS = 16
TOK_DEV = 788
TOKENS = 25216
CAP = 152
DEVICES = 32


def block_levels(key, shape, shards, smallest, top_value):
    def one(dim, blocks):
        heights = jax.random.uniform(jax.random.fold_in(jax.random.fold_in(key, 6), dim), (blocks,), jnp.float32, smallest / len(shards), top_value / len(shards))
        return jnp.repeat(jnp.exp(heights), shape[dim] // blocks).reshape((-1,) + (1,) * (len(shape) - dim - 1))

    factor_of = one(*shards[0])
    for cut in shards[1:]:
        factor_of = factor_of * one(*cut)
    return factor_of


def assign_block(stream_key, own, number, rows, count, top, most, skew):
    sequence = jax.random.permutation(stream_key, count)
    heavy_load, usual = load_shares(count, rows * top, most, skew, True), load_shares(count, rows * top, most, skew, False)
    places = jnp.arange(count)

    def named(lengths, rotation):
        used = int((lengths > 0).sum())
        fixed = max(1, used // 4)
        moved = fixed + (places - fixed + rotation * (used - fixed)) % max(1, count - fixed)
        return jnp.zeros((count,), jnp.int32).at[sequence[jnp.where(places < fixed, places, moved)]].set(jnp.asarray(lengths, jnp.int32))

    lengths = jnp.where(number % 4 == 0, named(heavy_load, number // 4), named(usual, number - number // 4 - 1))
    mixed = jax.random.permutation(jax.random.fold_in(own, 3), count)
    source_of, taker = mixed[0:count // 2 * 2:2], mixed[1:count // 2 * 2:2]
    room = jnp.minimum(lengths[source_of] - 1, most - lengths[taker]) // 2
    room = jnp.where((source_of == sequence[0]) | (taker == sequence[0]) | (lengths[taker] == 0), 0, jnp.maximum(room, 0))
    moved = jax.random.randint(jax.random.fold_in(own, 4), (count // 2,), 0, 1 << 20) % (room + 1)
    lengths = lengths.at[source_of].add(-moved).at[taker].add(moved)
    items = jnp.searchsorted(jnp.cumsum(lengths), jnp.arange(rows * top), side="right").astype(jnp.int32)
    listing = items.reshape(top, rows).T
    listing = listing[jax.random.permutation(jax.random.fold_in(own, 1), rows)]
    rotation = jax.random.randint(jax.random.fold_in(own, 2), (rows, 1), 0, top)
    return jnp.take_along_axis(listing, (jnp.arange(top)[None, :] + rotation) % top, axis=1)


def load_shares(number_of, total, reach, skew, full):
    loads = [(1 << 20) // math.isqrt(rank ** skew) + 1 for rank in range(1, number_of + 1)]
    largest = reach if full else min(reach, max(-(-total // number_of), total * loads[0] // sum(loads)))
    least = 1 if total - largest >= number_of - 1 else 0
    holding, rest = [largest] + [least] * (number_of - 1), total - largest - least * (number_of - 1)
    while rest > 0:
        candidates = [i for i in range(1, number_of) if holding[i] < largest] or [i for i in range(1, number_of) if holding[i] < reach]
        mass, budget = sum([loads[i] for i in candidates]), rest
        for i in candidates:
            addition = min(reach - holding[i], max(1, budget * loads[i] // mass), rest)
            holding[i] = holding[i] + addition
            rest = rest - addition
    return np.array(holding)


def scatter_about(own_key, extent, deviation, reach, pieces=(), held_as=jnp.bfloat16):
    values = deviation * jax.random.normal(own_key, extent, jnp.float32)
    if pieces:
        values = values * block_levels(own_key, extent, pieces, -0.22, 0.18)
    return jnp.clip(values, -reach, reach).astype(held_as)


def setup_inputs(seed: int = 0) -> dict:
    keys = jax.random.split(jax.random.key(seed), 23)
    tokens = scatter_about(keys[0], (TOKENS, D), 1.0, 6.0, ((0, 32),))
    routes_keys = jax.random.split(jax.random.fold_in(keys[1], 1), TOKENS // TOK_DEV)
    routes_turns = jax.random.permutation(jax.random.fold_in(keys[1], 3), TOKENS // TOK_DEV)
    routes = jax.vmap(lambda own, number: assign_block(jax.random.fold_in(keys[1], 2), own, number, TOK_DEV, EXPERTS, 2, CAP, 1))(routes_keys, routes_turns).reshape((TOKENS, 2))
    cotangent = scatter_about(keys[2], (TOKENS, D), 1.0, 6.0, ((0, 32),))
    gain_attn = jnp.clip(1.0 + 0.1 * jax.random.normal(keys[3], (D,), jnp.float32), 0.5, 1.5).astype(jnp.bfloat16)
    w_qkv = scatter_about(keys[4], (D, 3 * D), D ** -0.5, 0.21875, ((0, 4),))
    w_proj = scatter_about(keys[5], (D, D), (D // 16) ** -0.5, 0.875, ((0, 4),))
    gain_moe = jnp.clip(1.0 + 0.1 * jax.random.normal(keys[6], (D,), jnp.float32), 0.5, 1.5).astype(jnp.bfloat16)
    w_router = scatter_about(keys[7], (D, EXPERTS), (D // 4) ** -0.5, 0.4375, ((0, 4),))
    w_in = scatter_about(keys[8], (EXPERTS, D, FF), D ** -0.5, 0.21875, ((0, 8), (2, 4)))
    w_out = scatter_about(keys[9], (EXPERTS, FF, D), (FF // 2) ** -0.5, 0.15625, ((0, 8), (1, 4)))
    v_attn = jnp.clip(jnp.exp(math.log(17203.2) - 1.3862944 * jax.random.uniform(keys[10], (D,), jnp.float32) ** block_levels(keys[10], (D,), ((0, 4),), -0.2, 0.2)), 4300.8, 17203.2)
    v_moe = jnp.clip(jnp.exp(math.log(105907.2) - 1.3862944 * jax.random.uniform(keys[11], (D,), jnp.float32) ** block_levels(keys[11], (D,), ((0, 4),), -0.2, 0.2)), 26476.8, 105907.2)
    row_qkv = jnp.clip(jnp.exp(math.log(5734.4) - 1.3862944 * jax.random.uniform(keys[12], (D,), jnp.float32) ** block_levels(keys[12], (D,), ((0, 4),), -0.2, 0.2)), 1433.6, 5734.4)
    col_qkv = jnp.clip(jnp.exp(jax.random.uniform(keys[13], (3 * D,), jnp.float32, math.log(1433.6), math.log(5734.4))), 1433.6, 5734.4)
    row_proj = jnp.clip(jnp.exp(math.log(1433.6) - 1.3862944 * jax.random.uniform(keys[14], (D,), jnp.float32) ** block_levels(keys[14], (D,), ((0, 4),), -0.2, 0.2)), 358.4, 1433.6)
    col_proj = jnp.clip(jnp.exp(jax.random.uniform(keys[15], (D,), jnp.float32, math.log(358.4), math.log(1433.6))), 358.4, 1433.6)
    row_router = jnp.clip(jnp.exp(math.log(847257.6) - 1.3862944 * jax.random.uniform(keys[16], (D,), jnp.float32) ** block_levels(keys[16], (D,), ((0, 4),), -0.2, 0.2)), 211814.4, 847257.6)
    col_router = jnp.clip(jnp.exp(jax.random.uniform(keys[17], (EXPERTS,), jnp.float32, math.log(211814.4), math.log(847257.6))), 211814.4, 847257.6)
    row_in = jnp.clip(jnp.exp(math.log(386.4) - 1.3862944 * jax.random.uniform(keys[18], (EXPERTS, D), jnp.float32) ** block_levels(keys[18], (EXPERTS, D), ((0, 8),), -0.2, 0.2)), 96.6, 386.4)
    col_in = jnp.clip(jnp.exp(math.log(386.4) - 1.3862944 * jax.random.uniform(keys[19], (EXPERTS, FF), jnp.float32) ** block_levels(keys[19], (EXPERTS, FF), ((0, 8), (1, 4)), -0.2, 0.2)), 96.6, 386.4)
    row_out = jnp.clip(jnp.exp(math.log(795.2) - 1.3862944 * jax.random.uniform(keys[20], (EXPERTS, FF), jnp.float32) ** block_levels(keys[20], (EXPERTS, FF), ((0, 8), (1, 4)), -0.2, 0.2)), 198.8, 795.2)
    col_out = jnp.clip(jnp.exp(math.log(795.2) - 1.3862944 * jax.random.uniform(keys[21], (EXPERTS, D), jnp.float32) ** block_levels(keys[21], (EXPERTS, D), ((0, 8),), -0.2, 0.2)), 198.8, 795.2)
    return {"tokens": tokens, "routes": routes, "cotangent": cotangent, "gain_attn": gain_attn, "w_qkv": w_qkv, "w_proj": w_proj, "gain_moe": gain_moe, "w_router": w_router, "w_in": w_in, "w_out": w_out, "v_attn": v_attn, "v_moe": v_moe, "row_qkv": row_qkv, "col_qkv": col_qkv, "row_proj": row_proj, "col_proj": col_proj, "row_router": row_router, "col_router": col_router, "row_in": row_in, "col_in": col_in, "row_out": row_out, "col_out": col_out}


@jax.custom_vjp
def low(v):
    return lax.optimization_barrier(v.astype(jnp.bfloat16)).astype(jnp.float32)

@jax.custom_vjp
def low_back(v):
    return v

def low_keep(v):
    return (low(v), None)

def low_pass(kept, grad):
    return (grad,)

def back_keep(v):
    return (v, None)

def back_low(kept, grad):
    return (low(grad),)
low.defvjp(low_keep, low_pass)
low_back.defvjp(back_keep, back_low)
PRECISE = lax.Precision.HIGHEST
EPS_NORM = 1e-06
EPS_SQUARE = 1e-30
RATE = 0.3
DECAY = 0.5
CLIP = 0.05

def matmul(left, right):
    return jnp.dot(left, right, precision=PRECISE)

def layer_norm(values, gain):
    center = values - lax.optimization_barrier(jnp.mean(values, axis=-1, keepdims=True))
    spread = lax.optimization_barrier(jnp.mean(center * center, axis=-1, keepdims=True))
    return center * lax.rsqrt(spread + EPS_NORM) * gain

def attention_group(group_rows, gain_attn, w_qkv, w_proj):
    normed = low(layer_norm(group_rows, gain_attn))
    qkv_all = low(low_back(matmul(normed, w_qkv)))
    qkv_all = qkv_all.reshape(IMG_DEV, SEQ, 3, HEADS, HEAD)
    query_part = qkv_all[:, :, 0]
    key_part = qkv_all[:, :, 1]
    value_part = qkv_all[:, :, 2]
    scores = jnp.einsum('ishd,ithd->ihst', query_part, key_part, precision=PRECISE) * HEAD ** (-0.5)
    scores = low_back(scores)
    weights_soft = low(jax.nn.softmax(scores, axis=-1))
    attended = jnp.einsum('ihst,ithd->ishd', weights_soft, value_part, precision=PRECISE).reshape(TOK_DEV, D)
    attended = low(low_back(attended))
    return group_rows + low_back(matmul(attended, w_proj))

def slot_tables(routes):
    flat_routes = routes.reshape(DEVICES, TOK_DEV * 2)
    labels = jnp.arange(EXPERTS, dtype=jnp.int32)
    route_hits = (flat_routes[:, :, None] == labels[None, None, :]).astype(jnp.int32)
    slot_rank = lax.optimization_barrier(jnp.sum((jnp.cumsum(route_hits, axis=1) - 1) * route_hits, axis=2))
    blocks = jnp.arange(DEVICES, dtype=jnp.int32)[:, None]
    slot_dest = (flat_routes * (DEVICES * CAP) + blocks * CAP + slot_rank).reshape(-1)
    owners = jnp.arange(TOKENS * 2, dtype=jnp.int32) // 2
    slot_token = jnp.full((EXPERTS * DEVICES * CAP,), TOKENS, jnp.int32).at[slot_dest].set(owners)
    return (slot_token.reshape(EXPERTS, DEVICES * CAP), slot_dest)

def forward(tok_float, gain_attn, w_qkv, w_proj, gain_moe, w_router, w_in, w_out, routes, slot_token, slot_dest):
    groups = tok_float.reshape(DEVICES, TOK_DEV, D)
    attend = jax.checkpoint(lambda group_rows: attention_group(group_rows, gain_attn, w_qkv, w_proj))
    hidden = lax.map(attend, groups).reshape(TOKENS, D)
    moe_in = low(layer_norm(hidden, gain_moe))
    logits = matmul(moe_in, w_router)
    chosen = jnp.take_along_axis(logits, routes, axis=1)
    gates = jax.nn.softmax(chosen, axis=-1)
    padded = jnp.concatenate([moe_in, jnp.zeros((1, D), jnp.float32)], axis=0)

    def expert_apply(inputs):
        token_rows, first_weight, second_weight = inputs
        expert_in = low_back(padded[token_rows])
        pre_gelu = low_back(matmul(expert_in, first_weight))
        activated = low(jax.nn.gelu(pre_gelu, approximate=True))
        return low(low_back(matmul(activated, second_weight)))
    expert_out = lax.map(jax.checkpoint(expert_apply), (slot_token, w_in, w_out))
    picked = expert_out.reshape(-1, D)[slot_dest].reshape(TOKENS, 2, D)
    return hidden + lax.optimization_barrier(jnp.sum(gates[:, :, None] * picked, axis=1))

def factored(grad, weight, row_old, col_old):
    squares = grad * grad + EPS_SQUARE
    row_new = DECAY * row_old + (1.0 - DECAY) * lax.optimization_barrier(jnp.mean(squares, axis=-1))
    col_new = DECAY * col_old + (1.0 - DECAY) * lax.optimization_barrier(jnp.mean(squares, axis=-2))
    row_mean = lax.optimization_barrier(jnp.mean(row_new, axis=-1))
    estimate = row_new[..., :, None] * col_new[..., None, :] / row_mean[..., None, None]
    raw_step = grad * lax.rsqrt(estimate)
    step_rms = jnp.sqrt(lax.optimization_barrier(jnp.mean(raw_step * raw_step, axis=(-2, -1))))
    weight_rms = jnp.sqrt(lax.optimization_barrier(jnp.mean(weight * weight, axis=(-2, -1))))
    factor = -RATE * weight_rms / jnp.maximum(CLIP, step_rms)
    return (weight + factor[..., None, None] * raw_step, row_new, col_new, step_rms)

def unfactored(grad, weight, moment_old):
    moment_new = DECAY * moment_old + (1.0 - DECAY) * (grad * grad + EPS_SQUARE)
    raw_step = grad * lax.rsqrt(moment_new)
    step_rms = jnp.sqrt(jnp.mean(raw_step * raw_step))
    weight_rms = jnp.sqrt(jnp.mean(weight * weight))
    factor = -RATE * weight_rms / jnp.maximum(CLIP, step_rms)
    return (weight + factor * raw_step, moment_new, step_rms)

def reference(tokens, routes, cotangent, gain_attn, w_qkv, w_proj, gain_moe, w_router, w_in, w_out, v_attn, v_moe, row_qkv, col_qkv, row_proj, col_proj, row_router, col_router, row_in, col_in, row_out, col_out):
    slot_token, slot_dest = slot_tables(routes)
    params = tuple((item.astype(jnp.float32) for item in (tokens, gain_attn, w_qkv, w_proj, gain_moe, w_router, w_in, w_out)))

    def run_block(tok_float, gain_one, qkv_weight, proj_weight, gain_two, router_weight, first_weight, second_weight):
        return forward(tok_float, gain_one, qkv_weight, proj_weight, gain_two, router_weight, first_weight, second_weight, routes, slot_token, slot_dest)
    result, pullback = jax.vjp(run_block, *params)
    grads = pullback(cotangent.astype(jnp.float32))
    grad_tokens, grad_g1, grad_qkv, grad_proj, grad_g2, grad_router, grad_first, grad_second = grads
    new_g1, v_attn_new, rms_g1 = unfactored(grad_g1, params[1], v_attn)
    new_g2, v_moe_new, rms_g2 = unfactored(grad_g2, params[4], v_moe)
    new_qkv, row_qkv_new, col_qkv_new, rms_qkv = factored(grad_qkv, params[2], row_qkv, col_qkv)
    new_proj, row_proj_new, col_proj_new, rms_proj = factored(grad_proj, params[3], row_proj, col_proj)
    new_router, row_router_new, col_router_new, rms_router = factored(grad_router, params[5], row_router, col_router)
    new_first, row_in_new, col_in_new, rms_first = factored(grad_first, params[6], row_in, col_in)
    new_second, row_out_new, col_out_new, rms_second = factored(grad_second, params[7], row_out, col_out)
    dense_rms = jnp.stack([rms_g1, rms_g2, rms_qkv, rms_proj, rms_router])
    expert_rms = jnp.stack([rms_first, rms_second], axis=1)
    return (result.astype(jnp.bfloat16), grad_tokens, dense_rms, expert_rms, grad_g1, new_g1, v_attn_new, grad_g2, new_g2, v_moe_new, grad_qkv, new_qkv, row_qkv_new, col_qkv_new, grad_proj, new_proj, row_proj_new, col_proj_new, grad_router, new_router, row_router_new, col_router_new, grad_first, new_first, row_in_new, col_in_new, grad_second, new_second, row_out_new, col_out_new)
```

```python
import functools

import jax
import jax.numpy as jnp
from jax import lax
from jax.experimental import pallas as pl
from jax.experimental.pallas import tpu as pltpu
from jax.sharding import PartitionSpec as P

D = 768
HEADS = 12
HEAD = 64
FF = 3072
SEQ = 197


PRECISE = lax.Precision.HIGHEST
EPS_NORM = 1e-06
EPS_SQUARE = 1e-30
RATE = 0.3
DECAY = 0.5
CLIP = 0.05


GELU_A = 0.7978845608028654
GELU_B = 0.044715


def normalize(values):
    center = values - jnp.mean(values, axis=-1, keepdims=True)
    inv_root = lax.rsqrt(jnp.mean(center * center, axis=-1, keepdims=True) + EPS_NORM)
    return (center * inv_root, inv_root)


def norm_back(grad, normed, inv_root, gain):
    scaled = grad * gain
    grad_in = inv_root * (
        scaled
        - jnp.mean(scaled, axis=-1, keepdims=True)
        - normed * jnp.mean(scaled * normed, axis=-1, keepdims=True)
    )
    return (grad_in, jnp.sum(grad * normed, axis=0))


def gelu_tanh(values):
    return jax.nn.gelu(values, approximate=True)


def general(
    tokens,
    routes,
    cotangent,
    gain_attn,
    w_qkv,
    w_proj,
    gain_moe,
    w_router,
    w_in,
    w_out,
):
    gain_first, qkv_full, proj_full, gain_second, router_full = (
        lax.all_gather(gain_attn, "shard", axis=0, tiled=True),
        lax.all_gather(w_qkv, "shard", axis=0, tiled=True),
        lax.all_gather(w_proj, "shard", axis=0, tiled=True),
        lax.all_gather(gain_moe, "shard", axis=0, tiled=True),
        lax.all_gather(w_router, "shard", axis=0, tiled=True),
    )
    first_full, second_full = (
        lax.all_gather(w_in, "shard", axis=2, tiled=True),
        lax.all_gather(w_out, "shard", axis=1, tiled=True),
    )
    row_count = tokens.shape[0]
    image_count = row_count // SEQ
    expert_count = router_full.shape[1]
    per_device = w_in.shape[0]
    axis_count = lax.axis_size("expert")
    capacity = ((3 * row_count + expert_count - 1) // expert_count + 7) // 8 * 8
    score_scale = HEAD ** (-0.5)
    tok_float = tokens.astype(jnp.float32)
    gain_one = gain_first.astype(jnp.float32)
    gain_two = gain_second.astype(jnp.float32)
    attn_hat, attn_inv = normalize(tok_float)
    attn_low = (attn_hat * gain_one).astype(jnp.bfloat16)
    qkv_low = jnp.dot(attn_low, qkv_full, preferred_element_type=jnp.float32).astype(jnp.bfloat16)
    qkv_split = qkv_low.reshape(image_count, SEQ, 3, HEADS, HEAD)
    query_part = qkv_split[:, :, 0]
    key_part = qkv_split[:, :, 1]
    value_part = qkv_split[:, :, 2]
    scores = (
        jnp.einsum("ishd,ithd->ihst", query_part, key_part, preferred_element_type=jnp.float32)
        * score_scale
    )
    log_total = jax.nn.logsumexp(scores, axis=-1, keepdims=True)
    soft_low = jnp.exp(scores - log_total).astype(jnp.bfloat16)
    attended = (
        jnp.einsum("ihst,ithd->ishd", soft_low, value_part, preferred_element_type=jnp.float32)
        .reshape(row_count, D)
        .astype(jnp.bfloat16)
    )
    hidden = tok_float + jnp.dot(attended, proj_full, preferred_element_type=jnp.float32)
    moe_hat, moe_inv = normalize(hidden)
    moe_low = (moe_hat * gain_two).astype(jnp.bfloat16)
    logits = jnp.dot(moe_low, router_full, preferred_element_type=jnp.float32)
    labels = jnp.arange(expert_count, dtype=jnp.int32)
    route_hits = (routes[:, :, None] == labels[None, None, :]).astype(jnp.float32)
    chosen = jnp.sum(route_hits * logits[:, None, :], axis=2)
    gates = jax.nn.softmax(chosen, axis=-1)
    flat_routes = routes.reshape(-1)
    earlier = (jnp.arange(row_count)[:, None] > jnp.arange(row_count)[None, :]).astype(jnp.bfloat16)
    before = jnp.dot(
        earlier, jnp.sum(route_hits, axis=1).astype(jnp.bfloat16), preferred_element_type=jnp.float32
    )
    slot_rank = jnp.sum(route_hits * before[:, None, :], axis=2).astype(jnp.int32).reshape(-1)
    slot_dest = flat_routes * capacity + slot_rank
    pair_index = jnp.arange(2 * row_count, dtype=jnp.int32)
    slot_pair = (
        jnp.full((expert_count * capacity,), 2 * row_count, jnp.int32).at[slot_dest].set(pair_index)
    )
    slot_token = slot_pair // 2
    zero_row = jnp.zeros((1, D), jnp.bfloat16)
    send_rows = jnp.concatenate([moe_low, zero_row], axis=0)[slot_token].reshape(
        axis_count, per_device, capacity, D
    )
    received = lax.all_to_all(send_rows, "expert", split_axis=0, concat_axis=0, tiled=True)
    pre_gelu = jnp.einsum(
        "sekd,edf->sekf", received, first_full, preferred_element_type=jnp.float32
    )
    activated = gelu_tanh(pre_gelu).astype(jnp.bfloat16)
    expert_out = jnp.einsum(
        "sekf,efd->sekd", activated, second_full, preferred_element_type=jnp.float32
    ).astype(jnp.bfloat16)
    back_rows = lax.all_to_all(expert_out, "expert", split_axis=0, concat_axis=0, tiled=True)
    back_rows, received, pre_gelu, activated = (back_rows, received, pre_gelu, activated)
    picked = (
        back_rows.reshape(expert_count * capacity, D)[slot_dest]
        .reshape(row_count, 2, D)
        .astype(jnp.float32)
    )
    block_out = (hidden + jnp.sum(gates[:, :, None] * picked, axis=1)).astype(jnp.bfloat16)
    grad_out = cotangent.astype(jnp.float32)
    grad_picked = (gates[:, :, None] * grad_out[:, None, :]).astype(jnp.bfloat16)
    grad_gates = jnp.sum(grad_out[:, None, :] * picked, axis=2)
    grad_chosen = gates * (grad_gates - jnp.sum(gates * grad_gates, axis=1, keepdims=True))
    grad_logits = jnp.sum(route_hits * grad_chosen[:, :, None], axis=1)
    grad_send = jnp.concatenate([grad_picked.reshape(2 * row_count, D), zero_row], axis=0)[
        slot_pair
    ].reshape(axis_count, per_device, capacity, D)
    grad_recv = lax.all_to_all(grad_send, "expert", split_axis=0, concat_axis=0, tiled=True)
    grad_act = jnp.einsum(
        "sekd,efd->sekf", grad_recv, second_full, preferred_element_type=jnp.float32
    )
    unused, gelu_pull = jax.vjp(gelu_tanh, pre_gelu)
    grad_pre = gelu_pull(grad_act)[0].astype(jnp.bfloat16)
    grad_rows = jnp.einsum(
        "sekf,edf->sekd", grad_pre, first_full, preferred_element_type=jnp.float32
    ).astype(jnp.bfloat16)
    grad_back = lax.all_to_all(grad_rows, "expert", split_axis=0, concat_axis=0, tiled=True)
    grad_first = jnp.einsum(
        "sekd,sekf->edf", received, grad_pre, preferred_element_type=jnp.float32
    )
    grad_second = jnp.einsum(
        "sekf,sekd->efd", activated, grad_recv, preferred_element_type=jnp.float32
    )
    grad_first, grad_second = (
        lax.psum_scatter(grad_first, "shard", scatter_dimension=2, tiled=True),
        lax.psum_scatter(grad_second, "shard", scatter_dimension=1, tiled=True),
    )
    returned = (
        grad_back.reshape(expert_count * capacity, D)[slot_dest]
        .reshape(row_count, 2, D)
        .astype(jnp.float32)
    )
    router_float = router_full.astype(jnp.float32)
    grad_moe = jnp.sum(returned, axis=1) + jnp.einsum(
        "te,de->td", grad_logits, router_float, precision=PRECISE
    )
    grad_router = jnp.einsum(
        "td,te->de", moe_low.astype(jnp.float32), grad_logits, precision=PRECISE
    )
    grad_from_moe, grad_g2 = norm_back(grad_moe, moe_hat, moe_inv, gain_two)
    grad_hidden = grad_out + grad_from_moe
    grad_low = grad_hidden.astype(jnp.bfloat16)
    grad_proj = jnp.einsum("tc,td->cd", attended, grad_low, preferred_element_type=jnp.float32)
    grad_att = (
        jnp.einsum("td,cd->tc", grad_low, proj_full, preferred_element_type=jnp.float32)
        .astype(jnp.bfloat16)
        .reshape(image_count, SEQ, HEADS, HEAD)
    )
    scores_again = (
        jnp.einsum("ishd,ithd->ihst", query_part, key_part, preferred_element_type=jnp.float32)
        * score_scale
    )
    soft_again = jnp.exp(scores_again - log_total)
    soft_again_low = soft_again.astype(jnp.bfloat16)
    grad_soft = jnp.einsum(
        "ishd,ithd->ihst", grad_att, value_part, preferred_element_type=jnp.float32
    )
    grad_value = jnp.einsum(
        "ihst,ishd->ithd", soft_again_low, grad_att, preferred_element_type=jnp.float32
    )
    row_delta = jnp.sum(soft_again * grad_soft, axis=-1, keepdims=True)
    grad_scores = (soft_again * (grad_soft - row_delta)).astype(jnp.bfloat16)
    grad_query = (
        jnp.einsum("ihst,ithd->ishd", grad_scores, key_part, preferred_element_type=jnp.float32)
        * score_scale
    )
    grad_key = (
        jnp.einsum("ihst,ishd->ithd", grad_scores, query_part, preferred_element_type=jnp.float32)
        * score_scale
    )
    grad_qkv_low = (
        jnp.stack([grad_query, grad_key, grad_value], axis=2)
        .reshape(row_count, 3 * D)
        .astype(jnp.bfloat16)
    )
    grad_qkv = jnp.einsum("tc,td->cd", attn_low, grad_qkv_low, preferred_element_type=jnp.float32)
    grad_attn_in = jnp.einsum(
        "td,cd->tc", grad_qkv_low, qkv_full, preferred_element_type=jnp.float32
    )
    grad_from_attn, grad_g1 = norm_back(grad_attn_in, attn_hat, attn_inv, gain_one)
    grad_tokens = grad_hidden + grad_from_attn
    dense_grads = (grad_g1, grad_qkv, grad_proj, grad_g2, grad_router)
    dense_total = lax.psum(
        (dense_grads[0], dense_grads[1], dense_grads[2], dense_grads[3], dense_grads[4]), "expert"
    )
    dense_parts = (
        lax.psum_scatter(dense_total[0], "shard", scatter_dimension=0, tiled=True),
        lax.psum_scatter(dense_total[1], "shard", scatter_dimension=0, tiled=True),
        lax.psum_scatter(dense_total[2], "shard", scatter_dimension=0, tiled=True),
        lax.psum_scatter(dense_total[3], "shard", scatter_dimension=0, tiled=True),
        lax.psum_scatter(dense_total[4], "shard", scatter_dimension=0, tiled=True),
    )
    return block_out, grad_tokens, dense_parts, (grad_first, grad_second)


SEQ_PAD = 224
MESH = pl.DeviceIdType.MESH
VMEM_LIMIT = 62 * 1024 * 1024
BF = jnp.bfloat16
F32 = jnp.float32


def mm(a, b):
    return lax.dot_general(a, b, (((1,), (0,)), ((), ())), preferred_element_type=F32)


def mm_nt(a, b):
    return lax.dot_general(a, b, (((1,), (1,)), ((), ())), preferred_element_type=F32)


def mm_tn(a, b):
    return lax.dot_general(a, b, (((0,), (0,)), ((), ())), preferred_element_type=F32)


def remote(src, dst, send, recv, device):
    return pltpu.make_async_remote_copy(
        src_ref=src, dst_ref=dst, send_sem=send, recv_sem=recv, device_id=device, device_id_type=MESH
    )


def greet(devices):
    barrier = pltpu.get_barrier_semaphore()
    for device in devices:
        pl.semaphore_signal(barrier, inc=1, device_id=device, device_id_type=MESH)
    pl.semaphore_wait(barrier, len(devices))


class Place:
    def __init__(self):
        expert = lax.axis_index("expert")
        self.shard = lax.axis_index("shard")
        self.z, self.core = expert // 2, expert % 2
        self.number = self.z * 4 + self.shard
        self.sibling = (self.z * 2 + 1 - self.core, self.shard)

    def plane(self, step):
        return (self.z // 2 + step // 2) % 2 * 2 + (self.z + step) % 2

    def peer(self, number):
        return (number // 4 * 2 + self.core, number % 4)

    def peers(self):
        return [self.peer((self.number + d) % 16) for d in range(1, 16)]

    def mates(self):
        return [(self.z * 2 + self.core, (self.shard + d) % 4) for d in range(1, 4)]


def split3(rows):
    high = rows.astype(BF)
    rest = rows - high.astype(F32)
    low = rest.astype(BF)
    last = (rest - low.astype(F32)).astype(BF)
    return high, low, last


def three_rows(row):
    high, low, last = split3(row)
    index = lax.broadcasted_iota(jnp.int32, (8, row.shape[1]), 0)
    out = jnp.where(index == 0, high.astype(F32), 0.0)
    out = jnp.where(index == 1, low.astype(F32), out)
    return jnp.where(index == 2, last.astype(F32), out).astype(BF)


def norm_stats(values):
    center = values - jnp.mean(values, axis=-1, keepdims=True)
    inv = lax.rsqrt(jnp.mean(center * center, axis=-1, keepdims=True) + EPS_NORM)
    return center * inv, inv


def fill_hits(ranks, plane, hits, cap):
    slot = lax.broadcasted_iota(jnp.int32, (cap, hits.shape[1]), 0)
    for k in range(4):
        row = ranks[pl.ds(plane * 4 + k, 1), :]
        hits[k * cap : (k + 1) * cap, :] = jnp.where(slot == row, 1.0, 0.0).astype(BF)


def kernel_a(
    cap, tok, cot, rt, dsh, w1, w2,
    qkv, att, hid, lse, gate_t, ranks, aux, dense, xsend, gsend, cotr, wfull,
    csend, low, hits, tri, dsem, dfsem, csem, wsem, wloc, wrecv, fsem, osem,
):
    me = Place()
    z, c, s = me.z, me.core, me.shard
    rows = tok.shape[0]
    images = rows // SEQ_PAD
    other = [(z * 2 + 1 - c, t) for t in range(4)]
    greet(me.peers() + other)

    quarter = dsh.shape[0]
    half = quarter // 2
    dense_out = []
    for d in range(1, 4):
        cp = remote(
            dsh.at[pl.ds(pl.multiple_of(c * half, half), half)],
            dense.at[pl.ds(pl.multiple_of(s * quarter + c * half, half), half)],
            dsem.at[0, d], dsem.at[1, d], (z * 2 + c, (s + d) % 4),
        )
        cp.start()
        dense_out.append(cp)
    dense[pl.ds(pl.multiple_of(s * quarter, quarter), quarter), :] = dsh[...]

    expert_row = lax.broadcasted_iota(jnp.int32, (16, rows), 0)
    hit = (expert_row == rt[0:1, :]) | (expert_row == rt[1:2, :])
    earlier = lax.broadcasted_iota(jnp.int32, (rows, rows), 0) < lax.broadcasted_iota(jnp.int32, (rows, rows), 1)
    tri[...] = jnp.where(earlier, 1.0, 0.0).astype(BF)
    before = mm(jnp.where(hit, 1.0, 0.0).astype(BF), tri[...])
    ranks[...] = jnp.where(hit, before, -1.0).astype(jnp.int32)

    def cot_copy(p):
        return remote(
            csend.at[pl.ds(pl.multiple_of(p * cap, cap), cap)],
            cotr.at[pl.ds(pl.multiple_of(me.number * cap, cap), cap)],
            csem.at[0, p], csem.at[1, me.number], me.peer(p),
        )

    own = pl.multiple_of(me.number * cap, cap)
    own_copy = pltpu.make_async_copy(csend.at[pl.ds(own, cap)], cotr.at[pl.ds(own, cap)], osem)

    @pl.loop(0, 4)
    def _(step):
        plane = me.plane(3 - step)
        fill_hits(ranks, plane, hits, cap)
        csend[pl.ds(pl.multiple_of(plane * 4 * cap, 4 * cap), 4 * cap), :] = mm(hits[...], cot[...]).astype(BF)
        for k in range(4):
            p = plane * 4 + k

            @pl.when(p != me.number)
            def _():
                cot_copy(p).start()

            @pl.when(p == me.number)
            def _():
                own_copy.start()

    forwards = []
    for d in range(1, 4):
        dense_out[d - 1].wait()
        source = (s - d + 4) % 4
        place = pl.ds(pl.multiple_of(source * quarter + c * half, half), half)
        cp = remote(dense.at[place], dense.at[place], dfsem.at[0, d], dfsem.at[1, d], me.sibling)
        cp.start()
        forwards.append(cp)

    def quarters(act, own=True):
        for i in range(2):
            for a, w in ((0, w1), (1, w2)):
                target = 2 * c + i
                self_target = (a == c) & (target == s)

                @pl.when(jnp.logical_not(self_target))
                def _():
                    act(remote(w.at[i], wfull.at[a, s], wsem.at[i, a], wrecv.at[s], (z * 2 + a, target)), False)

                if own:

                    @pl.when(self_target)
                    def _():
                        act(pltpu.make_async_copy(w.at[i], wfull.at[a, s], wloc), True)

    for cp in forwards:
        cp.wait()
    quarters(lambda cp, local_copy: cp.start())

    flat = jnp.transpose(dense[:, 3072:3200].astype(F32))
    aux[...] = flat[0:32, :]

    @pl.loop(0, images)
    def _(i):
        r = pl.ds(pl.multiple_of(i * SEQ_PAD, SEQ_PAD), SEQ_PAD)
        hat, _unused = norm_stats(tok[r, :].astype(F32))
        low[r, :] = (hat * aux[16:17, :]).astype(BF)

    @pl.loop(0, 3)
    def _(n):
        columns = pl.ds(pl.multiple_of(n * D, D), D)
        qkv[:, columns] = mm(low[...], dense[:, columns]).astype(BF)

    attention_forward(qkv, att, lse, images)

    wproj = dense.at[:, 2304:3072]
    @pl.loop(0, images)
    def _(i):
        r = pl.ds(pl.multiple_of(i * SEQ_PAD, SEQ_PAD), SEQ_PAD)
        hidden = tok[r, :].astype(F32) + mm(att[r, :], wproj[...])
        hid[r, :] = hidden
        hat, _unused = norm_stats(hidden)
        low[r, :] = (hat * aux[17:18, :]).astype(BF)

    logits = mm_nt(aux[0:16, :].astype(BF), low[...])
    masked = jnp.where(hit, logits, -1e30)
    weights = jnp.where(hit, jnp.exp(masked - jnp.max(masked, axis=0, keepdims=True)), 0.0)
    gate_t[...] = weights / jnp.maximum(jnp.sum(weights, axis=0, keepdims=True), 0.5)
    gsend[...] = jnp.zeros_like(gsend)

    @pl.loop(0, 4)
    def _(plane):
        fill_hits(ranks, plane, hits, cap)
        xsend[pl.ds(pl.multiple_of(plane * 4 * cap, 4 * cap), 4 * cap), :] = mm(hits[...], low[...]).astype(BF)
        for k in range(4):
            row = mm_nt(three_rows(gate_t[pl.ds(plane * 4 + k, 1), :]), hits[k * cap : (k + 1) * cap, :])
            gsend[plane * 4 + k, :, 0:cap] = jnp.broadcast_to(jnp.sum(row, axis=0, keepdims=True), (8, cap))

    source_core = s // 2
    for t in range(4):
        arrives_here = (source_core == c) & (s == t)

        @pl.when(jnp.logical_not(arrives_here))
        def _():
            remote(w1.at[0], wfull.at[c, t], wsem.at[0, 0], wrecv.at[t], me.sibling).wait_recv()

        @pl.when(arrives_here)
        def _():
            pltpu.make_async_copy(w1.at[0], wfull.at[c, t], wloc).wait()

        remote(wfull.at[c, t], wfull.at[c, t], fsem.at[0, t], fsem.at[1, t], me.sibling).start()
    quarters(lambda cp, local_copy: cp.wait_send(), own=False)
    for t in range(4):
        remote(wfull.at[c, t], wfull.at[c, t], fsem.at[0, t], fsem.at[1, t], me.sibling).wait_send()
        remote(wfull.at[1 - c, t], wfull.at[1 - c, t], fsem.at[0, t], fsem.at[1, t], me.sibling).wait_recv()
    for d in range(1, 16):
        p = (me.number + d) % 16
        cot_copy(p).wait_send()
        remote(
            csend.at[pl.ds(0, cap)], cotr.at[pl.ds(0, cap)], csem.at[0, p], csem.at[1, p], me.peer(p)
        ).wait_recv()
    own_copy.wait()


def attention_forward(qkv, att, lse, images):
    first = lax.broadcasted_iota(jnp.int32, (SEQ_PAD, 128), 1) < HEAD
    lane = lax.broadcasted_iota(jnp.int32, (SEQ_PAD, 128), 1)
    real = lax.broadcasted_iota(jnp.int32, (SEQ_PAD, SEQ_PAD), 1) < SEQ
    lse[...] = jnp.zeros_like(lse)

    @pl.loop(0, HEADS // 2)
    def _(pair):
        for i in range(images):
            r = slice(i * SEQ_PAD, (i + 1) * SEQ_PAD)
            cols = [pl.ds(pl.multiple_of(part * D + pair * 128, 128), 128) for part in range(3)]
            q, k, v = (qkv[r, cols[part]] for part in range(3))
            outs, lses = [], []
            for h in range(2):
                mine = first if h == 0 else jnp.logical_not(first)
                qh = (jnp.where(mine, q.astype(F32), 0.0) * 0.125).astype(BF)
                scores = jnp.where(real, mm_nt(qh, k), -1e30)
                top = jnp.max(scores, axis=1, keepdims=True)
                weights = jnp.exp(scores - top)
                total = jnp.sum(weights, axis=1, keepdims=True)
                lses.append(top + jnp.log(total))
                outs.append(mm((weights * (1.0 / total)).astype(BF), v))
            att[r, pl.ds(pl.multiple_of(pair * 128, 128), 128)] = jnp.where(first, outs[0], outs[1]).astype(BF)
            old = lse[r, :]
            lse[r, :] = jnp.where(lane == 2 * pair, lses[0], jnp.where(lane == 2 * pair + 1, lses[1], old))


def kernel_e(
    cap, xsend, gsend, cotr, wfull,
    outs, ginh, ginb, ggb, gw,
    w1v, w2v, xr, gcot, gater, act, gpre, acc, stage, ggs, gcol,
    xsem, gsem, rsem, ggsem, lsem, wlsem, stsem,
):
    me = Place()
    z, c, s = me.z, me.core, me.shard
    greet(me.peers())
    block = 4 * cap

    def part(ref, p):
        return ref.at[pl.ds(pl.multiple_of(p * cap, cap), cap)]

    def x_copy(p):
        return remote(part(xsend, p), part(xr, me.number), xsem.at[0, p], xsem.at[1, me.number], me.peer(p))

    def g_copy(p):
        return remote(gsend.at[p], gater.at[me.number], gsem.at[0, p], gsem.at[1, me.number], me.peer(p))

    def r_copy(p):
        return remote(part(ginh, p), part(ginb, me.number), rsem.at[0, p], rsem.at[1, me.number], me.peer(p))

    def gg_copy(p):
        return remote(ggs.at[p], ggb.at[me.number], ggsem.at[0, p], ggsem.at[1, me.number], me.peer(p))

    local_copies = [
        pltpu.make_async_copy(part(xsend, me.number), part(xr, me.number), lsem.at[0]),
        pltpu.make_async_copy(gsend.at[me.number], gater.at[me.number], lsem.at[1]),
        pltpu.make_async_copy(cotr, gcot, lsem.at[2]),
    ]
    own_r = pltpu.make_async_copy(part(ginh, me.number), part(ginb, me.number), lsem.at[3])
    own_g = pltpu.make_async_copy(ggs.at[me.number], ggb.at[me.number], lsem.at[4])
    w_copies = [pltpu.make_async_copy(wfull.at[0], w1v, wlsem.at[0])] + [
        pltpu.make_async_copy(wfull.at[1, f], w2v.at[pl.ds(f * D, D)], wlsem.at[1 + f]) for f in range(4)
    ]
    for d in range(1, 16):
        g_copy((me.number + d) % 16).start()
    for cp in local_copies + w_copies:
        cp.start()
    for step in range(4):
        for k in range(4):
            p = me.plane(step) * 4 + k

            @pl.when(p != me.number)
            def _():
                x_copy(p).start()

    ggs[...] = jnp.zeros_like(ggs)
    for cp in local_copies + w_copies:
        cp.wait()

    eye = lax.broadcasted_iota(jnp.int32, (cap, cap), 0) == lax.broadcasted_iota(jnp.int32, (cap, cap), 1)

    def recv_block(plane):
        for k in range(4):
            p = plane * 4 + k

            @pl.when(p != me.number)
            def _():
                remote(part(xsend, p), part(xr, p), xsem.at[0, p], xsem.at[1, p], me.peer(p)).wait_recv()
                remote(gsend.at[p], gater.at[p], gsem.at[0, p], gsem.at[1, p], me.peer(p)).wait_recv()

    def stage_out(plane, which):
        return pltpu.make_async_copy(
            stage.at[which], (outs if which == 0 else ginh).at[pl.ds(pl.multiple_of(plane * block, block), block)],
            stsem.at[which],
        )

    @pl.loop(0, 4)
    def _(step):
        plane = me.plane(step)
        recv_block(plane)
        r = pl.ds(pl.multiple_of(plane * block, block), block)

        @pl.loop(0, 4)
        def _(f):
            for n in range(3):
                cols = pl.ds(pl.multiple_of(f * D + n * 256, 256), 256)
                pre = mm(xr[r, :], w1v[f, :, n * 256 : (n + 1) * 256])
                square = pre * pre
                t = jnp.tanh(pre * (GELU_A + GELU_A * GELU_B * square))
                half = 0.5 + 0.5 * t
                act[r, cols] = (pre * half).astype(BF)
                slope = half + (0.5 * pre) * (1.0 - t * t) * (GELU_A + 3.0 * GELU_A * GELU_B * square)
                gpre[r, cols] = slope.astype(BF)

        acc[...] = mm(act[r, :], w2v[...])

        for k in range(4):
            row = gater[plane * 4 + k, 0:1, 0:cap]
            column = jnp.sum(jnp.where(eye, row, 0.0), axis=1, keepdims=True)
            gcol[k * cap : (k + 1) * cap, :] = jnp.broadcast_to(column, (cap, 128))

        @pl.when(step > 0)
        def _():
            stage_out(plane, 0).wait()

        for k in range(4):
            rk = pl.ds(pl.multiple_of(plane * block + k * cap, cap), cap)
            kk = slice(k * cap, (k + 1) * cap)
            out = acc[kk, :].astype(BF).astype(F32)
            gate = gcol[kk, 0:1]
            g = gcot[rk, :].astype(F32)
            dots = jnp.sum(g * out, axis=1, keepdims=True)
            row = jnp.sum(jnp.where(eye, dots, 0.0), axis=0, keepdims=True)
            ggs[plane * 4 + k, :, 0:cap] = jnp.broadcast_to(row, (8, cap))
            stage[0, kk, :] = (gate * out).astype(BF)
            gcot[rk, :] = (gate * g).astype(BF)
        stage_out(plane, 0).start()

        @pl.loop(0, 4)
        def _(f):
            for n in range(3):
                cols = pl.ds(pl.multiple_of(f * D + n * 256, 256), 256)
                ga = mm_nt(gcot[r, :], w2v[cols, :])
                gpre[r, cols] = (ga * gpre[r, cols].astype(F32)).astype(BF)

        acc[...] = mm_nt(gpre[r, 0:D], w1v[0])
        for f in range(1, 4):
            acc[...] += mm_nt(gpre[r, f * D : (f + 1) * D], w1v[f])
        stage[1] = acc[...].astype(BF)
        stage_out(plane, 1).start()
        stage_out(plane, 1).wait()
        for k in range(4):
            p = plane * 4 + k

            @pl.when(p != me.number)
            def _():
                r_copy(p).start()
                gg_copy(p).start()

            @pl.when(p == me.number)
            def _():
                own_r.start()
                own_g.start()

    stage_out(0, 0).wait()

    @pl.loop(0, 4)
    def _(f):
        cols = pl.ds(pl.multiple_of(f * D, D), D)
        w1v[f] = mm_tn(xr[...], gpre[:, cols]).astype(BF)
        w2v[cols, :] = mm_tn(act[:, cols], gcot[...]).astype(BF)

    out_w = [pltpu.make_async_copy(w1v, gw.at[0], wlsem.at[0])] + [
        pltpu.make_async_copy(w2v.at[pl.ds(f * D, D)], gw.at[1, f], wlsem.at[1 + f]) for f in range(4)
    ]
    for cp in out_w:
        cp.start()
    for d in range(1, 16):
        p = (me.number + d) % 16
        x_copy(p).wait_send()
        g_copy(p).wait_send()
        r_copy(p).wait_send()
        gg_copy(p).wait_send()
        remote(part(ginh, p), part(ginb, p), rsem.at[0, p], rsem.at[1, p], me.peer(p)).wait_recv()
        remote(ggs.at[p], ggb.at[p], ggsem.at[0, p], ggsem.at[1, p], me.peer(p)).wait_recv()
    own_r.wait()
    own_g.wait()
    for cp in out_w:
        cp.wait()


def attention_backward(qkv, gatt, lse, gqkv, images):
    first = lax.broadcasted_iota(jnp.int32, (SEQ_PAD, 128), 1) < HEAD
    lane = lax.broadcasted_iota(jnp.int32, (SEQ_PAD, 128), 1)
    real = lax.broadcasted_iota(jnp.int32, (SEQ_PAD, SEQ_PAD), 1) < SEQ

    @pl.loop(0, HEADS // 2)
    def _(pair):
        for i in range(images):
            r = slice(i * SEQ_PAD, (i + 1) * SEQ_PAD)
            cols = [pl.ds(pl.multiple_of(part * D + pair * 128, 128), 128) for part in range(3)]
            q, k, v = (qkv[r, cols[part]] for part in range(3))
            g = gatt[r, pl.ds(pl.multiple_of(pair * 128, 128), 128)]
            logs = lse[r, :]
            parts = []
            for h in range(2):
                mine = first if h == 0 else jnp.logical_not(first)
                qh = (jnp.where(mine, q.astype(F32), 0.0) * 0.125).astype(BF)
                gh = jnp.where(mine, g.astype(F32), 0.0).astype(BF)
                log = jnp.sum(jnp.where(lane == 2 * pair + h, logs, 0.0), axis=1, keepdims=True)
                probs = jnp.where(real, jnp.exp(mm_nt(qh, k) - log), 0.0)
                grad_probs = mm_nt(gh, v)
                low = probs.astype(BF)
                delta = jnp.sum(probs * grad_probs, axis=1, keepdims=True)
                grad_scores = (probs * (grad_probs - delta)).astype(BF)
                parts.append((mm(grad_scores, k) * 0.125, mm_tn(grad_scores, q) * 0.125, mm_tn(low, g)))
            for part in range(3):
                gqkv[r, cols[part]] = jnp.where(first, parts[0][part], parts[1][part]).astype(BF)


def kernel_b(
    cap, tok, cot, dense, aux, qkv, att, hid, lse, gate_t, ranks, ggb, ginb, outs, gw,
    block_out, gtok, ghat, extra, outb, eg,
    rowsv, hits, gmoe, low, glow, gatt, gqkv, gd, ra, rb, sc, rc, exs, exl, gx, own_w, ggt,
    osem, lsem, wxsem, wsem, wload, wlocal, asem, bsem, zsem, fsem, esem, xsem,
):
    me = Place()
    z, c, s = me.z, me.core, me.shard
    rows = tok.shape[0]
    images = rows // SEQ_PAD
    block = 4 * cap
    half = D // 8
    greet(me.peers() + [(z * 2 + 1 - c, t) for t in range(4)])

    def part(ref, p):
        return ref.at[pl.ds(pl.multiple_of(p * cap, cap), cap)]

    def o_copy(p):
        return remote(part(outs, p), part(outb, me.number), osem.at[0, p], osem.at[1, me.number], me.peer(p))

    load_in = pltpu.make_async_copy(ginb, rowsv, lsem.at[0])
    load_in.start()
    swap = [remote(gw.at[1 - c, t], gx.at[t], wxsem.at[0, t], wxsem.at[1, t], me.sibling) for t in range(4)]
    for cp in swap:
        cp.start()
    own_o = pltpu.make_async_copy(part(outs, me.number), part(outb, me.number), lsem.at[1])
    own_o.start()
    for d in range(1, 16):
        o_copy((me.number + d) % 16).start()

    load_in.wait()
    gmoe[...] = jnp.zeros_like(gmoe)

    @pl.loop(0, 4)
    def _(plane):
        fill_hits(ranks, plane, hits, cap)
        for k in range(4):
            rows8 = three_rows(ggb[plane * 4 + k, 0:1, 0:cap])
            row = mm(rows8, hits[k * cap : (k + 1) * cap, :])
            ggt[pl.ds(plane * 4 + k, 1), :] = jnp.sum(row, axis=0, keepdims=True)
        r = pl.ds(pl.multiple_of(plane * block, block), block)
        gmoe[...] += mm_tn(hits[...], rowsv[r, :])

    gates = gate_t[...]
    grad_gates = ggt[...]
    grad_logits = gates * (grad_gates - jnp.sum(gates * grad_gates, axis=0, keepdims=True))
    gl_high = grad_logits.astype(BF)
    gl_low = (grad_logits - gl_high.astype(F32)).astype(BF)

    @pl.loop(0, images)
    def _(i):
        r = pl.ds(pl.multiple_of(i * SEQ_PAD, SEQ_PAD), SEQ_PAD)
        hat, _unused = norm_stats(hid[r, :])
        low[r, :] = (hat * aux[17:18, :]).astype(BF)

    router = aux[0:16, :].astype(BF)
    gmoe[...] += mm_tn(gl_high, router) + mm_tn(gl_low, router)
    exs[0, 0:16, :] = mm(gl_high, low[...]) + mm(gl_low, low[...])
    exs[0, 16:32, :] = jnp.zeros((16, D), F32)

    @pl.loop(0, images)
    def _(i):
        r = pl.ds(pl.multiple_of(i * SEQ_PAD, SEQ_PAD), SEQ_PAD)
        hat, inv = norm_stats(hid[r, :])
        w = gmoe[r, :]
        scaled = w * aux[17:18, :]
        back = inv * (
            scaled - jnp.mean(scaled, axis=-1, keepdims=True) - hat * jnp.mean(scaled * hat, axis=-1, keepdims=True)
        )
        grad = cot[r, :].astype(F32) + back
        gtok[r, :] = grad
        glow[r, :] = grad.astype(BF)
        exs[0, 17:18, :] += jnp.sum(w * hat, axis=0, keepdims=True)
        hat, _unused = norm_stats(tok[r, :].astype(F32))
        low[r, :] = (hat * aux[16:17, :]).astype(BF)

    def put(group, value):
        for t in range(4):
            for h in range(2):
                gd[t, h, group] = value[t * 2 * half + h * half : t * 2 * half + (h + 1) * half, :].astype(BF)

    put(3, mm_tn(att[...], glow[...]))
    gatt[...] = mm_nt(glow[...], dense[:, 2304:3072]).astype(BF)

    def owner_copy(t):
        return remote(
            gx.at[t], eg.at[s % 2, c], wsem.at[0, t], wsem.at[1, s % 2 * 2 + c], (z * 2 + s // 2, t)
        )

    mine_local = s // 2 == c
    owner_local = pltpu.make_async_copy(gx.at[s], eg.at[s % 2, c], wlocal)
    for t in range(4):
        load = pltpu.make_async_copy(gw.at[c, t], own_w, wload)
        load.start()
        load.wait()
        swap[t].wait()
        gx[t] = (gx[t].astype(F32) + own_w[...].astype(F32)).astype(BF)

        @pl.when(jnp.logical_not(mine_local & (s == t)))
        def _():
            owner_copy(t).start()

        @pl.when(mine_local & (s == t))
        def _():
            owner_local.start()

    attention_backward(qkv, gatt, lse, gqkv, images)

    for group in range(3):
        put(group, mm_tn(low[...], gqkv[:, group * D : (group + 1) * D]))

    a_copies = [remote(gd.at[t, 1 - c], ra.at[t], asem.at[0, t], asem.at[1, t], me.sibling) for t in range(4)]
    for cp in a_copies:
        cp.start()

    gmoe[...] = mm_nt(gqkv[...], dense[:, 0:2304])

    @pl.loop(0, images)
    def _(i):
        r = pl.ds(pl.multiple_of(i * SEQ_PAD, SEQ_PAD), SEQ_PAD)
        hat, inv = norm_stats(tok[r, :].astype(F32))
        w = gmoe[r, :]
        scaled = w * aux[16:17, :]
        gtok[r, :] += inv * (
            scaled - jnp.mean(scaled, axis=-1, keepdims=True) - hat * jnp.mean(scaled * hat, axis=-1, keepdims=True)
        )
        exs[0, 16:17, :] += jnp.sum(w * hat, axis=0, keepdims=True)

    x_first = remote(exs.at[0], exl.at[0], xsem.at[0, 0], xsem.at[1, 0], me.sibling)
    x_first.start()
    b_copies = []
    for d in range(1, 4):
        t = (s + d) % 4
        b_copies.append(remote(gd.at[t, c], rb.at[d], bsem.at[0, d], bsem.at[1, d], (z * 2 + c, t)))
    for t in range(4):
        a_copies[t].wait()
        gd[t, c] = (gd[t, c].astype(F32) + ra[t].astype(F32)).astype(BF)
    for cp in b_copies:
        cp.start()
    x_first.wait()
    exs[1] = exs[0] + exl[0]
    exl[1 + s] = exs[1]
    x_second = [
        remote(exs.at[1], exl.at[1 + s], xsem.at[0, d], xsem.at[1, d], (z * 2 + c, (s + d) % 4)) for d in range(1, 4)
    ]
    for cp in x_second:
        cp.start()
    for cp in x_second:
        cp.wait()
    exs[2] = (exl[1] + exl[2]) + (exl[3] + exl[4])
    exl[5 + z] = exs[2]
    x_third = [
        remote(exs.at[2], exl.at[5 + z], xsem.at[0, 3 + d], xsem.at[1, 3 + d], ((z + d) % 4 * 2 + c, s))
        for d in range(1, 4)
    ]
    for cp in x_third:
        cp.start()
    for cp in b_copies:
        cp.wait()
    for g in range(4):
        sc[g] = (
            (gd[s, c, g].astype(F32) + rb[1, g].astype(F32)) + (rb[2, g].astype(F32) + rb[3, g].astype(F32))
        ).astype(BF)
    z_copies = []
    for d in range(1, 4):
        t = (z + d) % 4
        cp = remote(sc.at[t], rc.at[d], zsem.at[0, d], zsem.at[1, d], (t * 2 + c, s))
        cp.start()
        z_copies.append(cp)
    for cp in z_copies:
        cp.wait()
    ghat[c, z] = (
        (sc[z].astype(F32) + rc[1].astype(F32)) + (rc[2].astype(F32) + rc[3].astype(F32))
    ).astype(BF)
    f_copies = []
    for d in range(1, 4):
        t = (z + d) % 4
        cp = remote(ghat.at[c, z], ghat.at[c, z], fsem.at[0, d], fsem.at[1, d], (t * 2 + c, s))
        cp.start()
        f_copies.append(cp)
    for cp in f_copies:
        cp.wait()
    e_copy = remote(ghat.at[c], ghat.at[c], esem.at[0], esem.at[1], me.sibling)
    e_copy.start()
    for cp in x_third:
        cp.wait()
    extra[...] = (exl[5] + exl[6]) + (exl[7] + exl[8])

    own_o.wait()
    for d in range(1, 16):
        p = (me.number + d) % 16
        o_copy(p).wait_send()
        remote(part(outs, p), part(outb, p), osem.at[0, p], osem.at[1, p], me.peer(p)).wait_recv()
    load_out = pltpu.make_async_copy(outb, rowsv, lsem.at[0])
    load_out.start()
    load_out.wait()
    gmoe[...] = hid[...]

    @pl.loop(0, 4)
    def _(plane):
        fill_hits(ranks, plane, hits, cap)
        r = pl.ds(pl.multiple_of(plane * block, block), block)
        gmoe[...] += mm_tn(hits[...], rowsv[r, :])

    block_out[...] = gmoe[...].astype(BF)

    for t in range(4):
        @pl.when(jnp.logical_not(mine_local & (s == t)))
        def _():
            owner_copy(t).wait_send()

        @pl.when(mine_local & (s == t))
        def _():
            owner_local.wait()

    for i in range(2):
        for a in range(2):
            own = (a == c) & (s == 2 * c + i)

            @pl.when(jnp.logical_not(own))
            def _():
                remote(gx.at[0], eg.at[i, a], wsem.at[0, 0], wsem.at[1, i * 2 + a], me.sibling).wait_recv()

    e_copy.wait()


def params(number):
    return pltpu.CompilerParams(collective_id=number, has_side_effects=True, vmem_limit_bytes=VMEM_LIMIT)


def dma(*shape):
    return pltpu.SemaphoreType.DMA(shape)


def fast(tokens, routes, cotangent, gain_attn, w_qkv, w_proj, gain_moe, w_router, w_in, w_out):
    count = tokens.shape[0]
    images = count // SEQ
    rows = images * SEQ_PAD
    experts = w_router.shape[1]
    cap = ((3 * count + experts - 1) // experts + 15) // 16 * 16
    slots = experts * cap
    vmem = pl.BlockSpec(memory_space=pltpu.VMEM)
    hbm = pl.BlockSpec(memory_space=pl.ANY)
    shape = jax.ShapeDtypeStruct

    def padded(array, value=0):
        array = array.reshape(images, SEQ, array.shape[1])
        array = jnp.pad(array, ((0, 0), (0, SEQ_PAD - SEQ), (0, 0)), constant_values=value)
        return array.reshape(rows, array.shape[2])

    tok = padded(tokens)
    cot = padded(cotangent)
    rt = padded(routes, -1).T
    quarter = w_qkv.shape[0]
    small = jnp.concatenate([w_router, gain_attn[:, None], gain_moe[:, None]], axis=1)
    small = jnp.pad(small, ((0, 0), (0, 128 - small.shape[1])))
    dsh = jnp.concatenate([w_qkv, w_proj, small], axis=1)
    wide = dsh.shape[1]

    qkv, att, hid, lse, gate_t, ranks, aux, dense, xsend, gsend, cotr, wfull = pl.pallas_call(
        functools.partial(kernel_a, cap),
        out_shape=(
            shape((rows, 3 * D), BF), shape((rows, D), BF), shape((rows, D), F32), shape((rows, 128), F32),
            shape((16, rows), F32), shape((16, rows), jnp.int32), shape((32, D), F32), shape((D, wide), BF),
            shape((slots, D), BF), shape((16, 8, 256), F32), shape((slots, D), BF), shape((2, 4, D, D), BF),
        ),
        in_specs=[vmem] * 4 + [hbm] * 2,
        out_specs=(vmem,) * 10 + (hbm,) * 2,
        scratch_shapes=[
            pltpu.VMEM((slots, D), BF), pltpu.VMEM((rows, D), BF), pltpu.VMEM((4 * cap, rows), BF),
            pltpu.VMEM((rows, rows), BF), dma(2, 4), dma(2, 4), dma(2, 16), dma(2, 2), dma(), dma(4), dma(2, 4), dma(),
        ],
        compiler_params=params(1),
        name="forward",
    )(tok, cot, rt, dsh, w_in, w_out)

    outs, ginh, ginb, ggb, gw = pl.pallas_call(
        functools.partial(kernel_e, cap),
        out_shape=(
            shape((slots, D), BF), shape((slots, D), BF), shape((slots, D), BF), shape((16, 8, 256), F32),
            shape((2, 4, D, D), BF),
        ),
        in_specs=[hbm, vmem, hbm, hbm],
        out_specs=(hbm, hbm, hbm, vmem, hbm),
        scratch_shapes=[
            pltpu.VMEM((4, D, D), BF), pltpu.VMEM((FF, D), BF), pltpu.VMEM((slots, D), BF), pltpu.VMEM((slots, D), BF),
            pltpu.VMEM((16, 8, 256), F32), pltpu.VMEM((slots, FF), BF), pltpu.VMEM((slots, FF), BF),
            pltpu.VMEM((4 * cap, D), F32), pltpu.VMEM((2, 4 * cap, D), BF),
            pltpu.VMEM((16, 8, 256), F32), pltpu.VMEM((4 * cap, 128), F32),
            dma(2, 16), dma(2, 16), dma(2, 16), dma(2, 16), dma(5), dma(5), dma(2),
        ],
        compiler_params=params(2),
        name="experts",
    )(xsend, gsend, cotr, wfull)

    half = D // 8
    block_out, gtok, ghat, extra, outb, eg = pl.pallas_call(
        functools.partial(kernel_b, cap),
        out_shape=(
            shape((rows, D), BF), shape((rows, D), F32), shape((2, 4, half, D), BF), shape((32, D), F32),
            shape((slots, D), BF), shape((2, 2, D, D), BF),
        ),
        in_specs=[vmem] * 11 + [hbm] * 3,
        out_specs=(vmem,) * 4 + (hbm,) * 2,
        scratch_shapes=[
            pltpu.VMEM((slots, D), BF), pltpu.VMEM((4 * cap, rows), BF), pltpu.VMEM((rows, D), F32),
            pltpu.VMEM((rows, D), BF), pltpu.VMEM((rows, D), BF), pltpu.VMEM((rows, D), BF),
            pltpu.VMEM((rows, 3 * D), BF), pltpu.VMEM((4, 2, 4, half, D), BF), pltpu.VMEM((4, 4, half, D), BF),
            pltpu.VMEM((4, 4, half, D), BF), pltpu.VMEM((4, half, D), BF), pltpu.VMEM((4, half, D), BF),
            pltpu.VMEM((3, 32, D), F32), pltpu.VMEM((9, 32, D), F32), pltpu.VMEM((4, D, D), BF),
            pltpu.VMEM((D, D), BF), pltpu.VMEM((16, rows), F32),
            dma(2, 16), dma(2), dma(2, 4), dma(2, 4), dma(), dma(), dma(2, 4), dma(2, 4), dma(2, 4), dma(2, 4),
            dma(2), dma(2, 7),
        ],
        compiler_params=params(3),
        name="backward",
    )(tok, cot, dense, aux, qkv, att, hid, lse, gate_t, ranks, ggb, ginb, outs, gw)

    def unpadded(array):
        return array.reshape(images, SEQ_PAD, D)[:, :SEQ].reshape(count, D)

    part_dense = jnp.swapaxes(ghat, 1, 2).reshape(quarter, 4 * D).astype(F32)
    mine = lax.dynamic_slice_in_dim(extra, lax.axis_index("shard") * quarter, quarter, axis=1)
    dense_parts = (mine[16], part_dense[:, : 3 * D], part_dense[:, 3 * D :], mine[17], mine[:16].T)
    eg = eg.astype(F32)
    return unpadded(block_out), unpadded(gtok), dense_parts, (eg[:, 0], eg[:, 1])


def local(
    tokens, routes, cotangent, gain_attn, w_qkv, w_proj, gain_moe, w_router, w_in, w_out,
    v_attn, v_moe, row_qkv, col_qkv, row_proj, col_proj, row_router, col_router, row_in, col_in, row_out, col_out,
):
    fits = (
        lax.axis_size("shard") == 4 and lax.axis_size("expert") == 8 and w_in.shape[0] == 2 and tokens.shape[0] % SEQ == 0
    )
    block_out, grad_tokens, dense_parts, expert_parts = (fast if fits else general)(
        tokens, routes, cotangent, gain_attn, w_qkv, w_proj, gain_moe, w_router, w_in, w_out
    )
    part_g1, part_qkv, part_proj, part_g2, part_router = dense_parts
    grad_first, grad_second = expert_parts
    expert_count = part_router.shape[1]
    weight_g1 = gain_attn.astype(jnp.float32)
    weight_g2 = gain_moe.astype(jnp.float32)
    dense = (
        (part_qkv, w_qkv.astype(jnp.float32), row_qkv, col_qkv),
        (part_proj, w_proj.astype(jnp.float32), row_proj, col_proj),
        (part_router, w_router.astype(jnp.float32), row_router, col_router),
    )
    weight_first = w_in.astype(jnp.float32)
    weight_second = w_out.astype(jnp.float32)
    v_attn_new = DECAY * v_attn + (1.0 - DECAY) * (part_g1 * part_g1 + EPS_SQUARE)
    v_moe_new = DECAY * v_moe + (1.0 - DECAY) * (part_g2 * part_g2 + EPS_SQUARE)
    raw_g1 = part_g1 * lax.rsqrt(v_attn_new)
    raw_g2 = part_g2 * lax.rsqrt(v_moe_new)
    dense_rows, dense_sums = [], []
    for grad, weight, row, col in dense:
        square = grad * grad
        row_new = DECAY * row + (1.0 - DECAY) * jnp.mean(square + EPS_SQUARE, axis=1)
        dense_rows.append(row_new)
        dense_sums.append(
            (
                jnp.sum(square + EPS_SQUARE, axis=0),
                jnp.sum(square / row_new[:, None], axis=0),
                jnp.stack([jnp.sum(row_new), jnp.sum(weight * weight)]),
            )
        )
    square_first = grad_first * grad_first
    square_second = grad_second * grad_second
    col_in_new = DECAY * col_in + (1.0 - DECAY) * jnp.mean(square_first + EPS_SQUARE, axis=1)
    row_out_new = DECAY * row_out + (1.0 - DECAY) * jnp.mean(square_second + EPS_SQUARE, axis=2)
    gain_sums = jnp.stack(
        [
            jnp.sum(raw_g1 * raw_g1),
            jnp.sum(raw_g2 * raw_g2),
            jnp.sum(weight_g1 * weight_g1),
            jnp.sum(weight_g2 * weight_g2),
        ]
    )
    expert_sums = (
        jnp.sum(square_first + EPS_SQUARE, axis=2),
        jnp.sum(square_first / col_in_new[:, None, :], axis=2),
        jnp.sum(square_second + EPS_SQUARE, axis=1),
        jnp.sum(square_second / row_out_new[:, :, None], axis=1),
        jnp.stack(
            [
                jnp.sum(weight_first * weight_first, axis=(1, 2)),
                jnp.sum(row_out_new, axis=1),
                jnp.sum(weight_second * weight_second, axis=(1, 2)),
            ]
        ),
    )
    expert_sums = lax.psum(expert_sums, "shard")
    dense_sums, gain_sums = lax.psum((dense_sums, gain_sums), "shard")

    def step(square_sum, weight_sum, size):
        rms = jnp.sqrt(square_sum / size)
        return rms, -RATE * jnp.sqrt(weight_sum / size) / jnp.maximum(CLIP, rms)

    rms_g1, factor_g1 = step(gain_sums[0], gain_sums[2], D)
    rms_g2, factor_g2 = step(gain_sums[1], gain_sums[3], D)
    new_g1 = weight_g1 + factor_g1 * raw_g1
    new_g2 = weight_g2 + factor_g2 * raw_g2
    dense_new, dense_cols, dense_rms = [], [], [rms_g1, rms_g2]
    for (grad, weight, _, col), row_new, (col_sum, ratio_sum, both) in zip(dense, dense_rows, dense_sums):
        col_new = DECAY * col + (1.0 - DECAY) * (col_sum / D)
        row_mean = both[0] / D
        rms, factor = step(row_mean * jnp.sum(ratio_sum / col_new), both[1], grad.shape[1] * D)
        raw = grad * lax.rsqrt(row_new[:, None] * col_new[None, :] / row_mean)
        dense_new.append(weight + factor * raw)
        dense_cols.append(col_new)
        dense_rms.append(rms)
    new_qkv, new_proj, new_router = dense_new
    row_qkv_new, row_proj_new, row_router_new = dense_rows
    col_qkv_new, col_proj_new, col_router_new = dense_cols
    row_in_sum, ratio_in, col_out_sum, ratio_out, expert_scalars = expert_sums
    row_in_new = DECAY * row_in + (1.0 - DECAY) * (row_in_sum / FF)
    col_out_new = DECAY * col_out + (1.0 - DECAY) * (col_out_sum / FF)
    mean_in = jnp.mean(row_in_new, axis=1)
    mean_out = expert_scalars[1] / FF
    rms_first, factor_first = step(mean_in * jnp.sum(ratio_in / row_in_new, axis=1), expert_scalars[0], D * FF)
    rms_second, factor_second = step(mean_out * jnp.sum(ratio_out / col_out_new, axis=1), expert_scalars[2], D * FF)
    new_first = weight_first + factor_first[:, None, None] * grad_first * lax.rsqrt(
        row_in_new[:, :, None] * col_in_new[:, None, :] / mean_in[:, None, None]
    )
    new_second = weight_second + factor_second[:, None, None] * grad_second * lax.rsqrt(
        row_out_new[:, :, None] * col_out_new[:, None, :] / mean_out[:, None, None]
    )
    return (
        block_out,
        grad_tokens,
        jnp.stack(dense_rms),
        jnp.stack([rms_first, rms_second], axis=1),
        part_g1,
        new_g1,
        v_attn_new,
        part_g2,
        new_g2,
        v_moe_new,
        part_qkv,
        new_qkv,
        row_qkv_new,
        col_qkv_new,
        part_proj,
        new_proj,
        row_proj_new,
        col_proj_new,
        part_router,
        new_router,
        row_router_new,
        col_router_new,
        grad_first,
        new_first,
        row_in_new,
        col_in_new,
        grad_second,
        new_second,
        row_out_new,
        col_out_new,
    )


def solution(mesh):
    return jax.shard_map(
        local,
        mesh=mesh,
        in_specs=(
            P(("expert", "shard"), None),
            P(("expert", "shard"), None),
            P(("expert", "shard"), None),
            P("shard"),
            P("shard", None),
            P("shard", None),
            P("shard"),
            P("shard", None),
            P("expert", None, "shard"),
            P("expert", "shard", None),
            P("shard"),
            P("shard"),
            P("shard"),
            P(),
            P("shard"),
            P(),
            P("shard"),
            P(),
            P("expert", None),
            P("expert", "shard"),
            P("expert", "shard"),
            P("expert", None),
        ),
        out_specs=(
            P(("expert", "shard"), None),
            P(("expert", "shard"), None),
            P(),
            P("expert", None),
            P("shard"),
            P("shard"),
            P("shard"),
            P("shard"),
            P("shard"),
            P("shard"),
            P("shard", None),
            P("shard", None),
            P("shard"),
            P(),
            P("shard", None),
            P("shard", None),
            P("shard"),
            P(),
            P("shard", None),
            P("shard", None),
            P("shard"),
            P(),
            P("expert", None, "shard"),
            P("expert", None, "shard"),
            P("expert", None),
            P("expert", "shard"),
            P("expert", "shard", None),
            P("expert", "shard", None),
            P("expert", "shard"),
            P("expert", None),
        ),
        check_vma=False,
    )
```

```python
import functools

import jax
import jax.numpy as jnp
from jax import lax
from jax.experimental import pallas as pl
from jax.experimental.pallas import tpu as pltpu
from jax.sharding import PartitionSpec as P

D = 768
HEADS = 12
HEAD = 64
FF = 3072
SEQ = 197


PRECISE = lax.Precision.HIGHEST
EPS_NORM = 1e-06
EPS_SQUARE = 1e-30
RATE = 0.3
DECAY = 0.5
CLIP = 0.05


GELU_A = 0.7978845608028654
GELU_B = 0.044715


def normalize(values):
    center = values - jnp.mean(values, axis=-1, keepdims=True)
    inv_root = lax.rsqrt(jnp.mean(center * center, axis=-1, keepdims=True) + EPS_NORM)
    return (center * inv_root, inv_root)


def norm_back(grad, normed, inv_root, gain):
    scaled = grad * gain
    grad_in = inv_root * (
        scaled
        - jnp.mean(scaled, axis=-1, keepdims=True)
        - normed * jnp.mean(scaled * normed, axis=-1, keepdims=True)
    )
    return (grad_in, jnp.sum(grad * normed, axis=0))


def gelu_tanh(values):
    return jax.nn.gelu(values, approximate=True)


def general(
    tokens,
    routes,
    cotangent,
    gain_attn,
    w_qkv,
    w_proj,
    gain_moe,
    w_router,
    w_in,
    w_out,
):
    gain_first, qkv_full, proj_full, gain_second, router_full = (
        lax.all_gather(gain_attn, "shard", axis=0, tiled=True),
        lax.all_gather(w_qkv, "shard", axis=0, tiled=True),
        lax.all_gather(w_proj, "shard", axis=0, tiled=True),
        lax.all_gather(gain_moe, "shard", axis=0, tiled=True),
        lax.all_gather(w_router, "shard", axis=0, tiled=True),
    )
    first_full, second_full = (
        lax.all_gather(w_in, "shard", axis=2, tiled=True),
        lax.all_gather(w_out, "shard", axis=1, tiled=True),
    )
    row_count = tokens.shape[0]
    image_count = row_count // SEQ
    expert_count = router_full.shape[1]
    per_device = w_in.shape[0]
    axis_count = lax.axis_size("expert")
    capacity = ((3 * row_count + expert_count - 1) // expert_count + 7) // 8 * 8
    score_scale = HEAD ** (-0.5)
    tok_float = tokens.astype(jnp.float32)
    gain_one = gain_first.astype(jnp.float32)
    gain_two = gain_second.astype(jnp.float32)
    attn_hat, attn_inv = normalize(tok_float)
    attn_low = (attn_hat * gain_one).astype(jnp.bfloat16)
    qkv_low = jnp.dot(attn_low, qkv_full, preferred_element_type=jnp.float32).astype(jnp.bfloat16)
    qkv_split = qkv_low.reshape(image_count, SEQ, 3, HEADS, HEAD)
    query_part = qkv_split[:, :, 0]
    key_part = qkv_split[:, :, 1]
    value_part = qkv_split[:, :, 2]
    scores = (
        jnp.einsum("ishd,ithd->ihst", query_part, key_part, preferred_element_type=jnp.float32)
        * score_scale
    )
    log_total = jax.nn.logsumexp(scores, axis=-1, keepdims=True)
    soft_low = jnp.exp(scores - log_total).astype(jnp.bfloat16)
    attended = (
        jnp.einsum("ihst,ithd->ishd", soft_low, value_part, preferred_element_type=jnp.float32)
        .reshape(row_count, D)
        .astype(jnp.bfloat16)
    )
    hidden = tok_float + jnp.dot(attended, proj_full, preferred_element_type=jnp.float32)
    moe_hat, moe_inv = normalize(hidden)
    moe_low = (moe_hat * gain_two).astype(jnp.bfloat16)
    logits = jnp.dot(moe_low, router_full, preferred_element_type=jnp.float32)
    labels = jnp.arange(expert_count, dtype=jnp.int32)
    route_hits = (routes[:, :, None] == labels[None, None, :]).astype(jnp.float32)
    chosen = jnp.sum(route_hits * logits[:, None, :], axis=2)
    gates = jax.nn.softmax(chosen, axis=-1)
    flat_routes = routes.reshape(-1)
    earlier = (jnp.arange(row_count)[:, None] > jnp.arange(row_count)[None, :]).astype(jnp.bfloat16)
    before = jnp.dot(
        earlier, jnp.sum(route_hits, axis=1).astype(jnp.bfloat16), preferred_element_type=jnp.float32
    )
    slot_rank = jnp.sum(route_hits * before[:, None, :], axis=2).astype(jnp.int32).reshape(-1)
    slot_dest = flat_routes * capacity + slot_rank
    pair_index = jnp.arange(2 * row_count, dtype=jnp.int32)
    slot_pair = (
        jnp.full((expert_count * capacity,), 2 * row_count, jnp.int32).at[slot_dest].set(pair_index)
    )
    slot_token = slot_pair // 2
    zero_row = jnp.zeros((1, D), jnp.bfloat16)
    send_rows = jnp.concatenate([moe_low, zero_row], axis=0)[slot_token].reshape(
        axis_count, per_device, capacity, D
    )
    received = lax.all_to_all(send_rows, "expert", split_axis=0, concat_axis=0, tiled=True)
    pre_gelu = jnp.einsum(
        "sekd,edf->sekf", received, first_full, preferred_element_type=jnp.float32
    )
    activated = gelu_tanh(pre_gelu).astype(jnp.bfloat16)
    expert_out = jnp.einsum(
        "sekf,efd->sekd", activated, second_full, preferred_element_type=jnp.float32
    ).astype(jnp.bfloat16)
    back_rows = lax.all_to_all(expert_out, "expert", split_axis=0, concat_axis=0, tiled=True)
    back_rows, received, pre_gelu, activated = (back_rows, received, pre_gelu, activated)
    picked = (
        back_rows.reshape(expert_count * capacity, D)[slot_dest]
        .reshape(row_count, 2, D)
        .astype(jnp.float32)
    )
    block_out = (hidden + jnp.sum(gates[:, :, None] * picked, axis=1)).astype(jnp.bfloat16)
    grad_out = cotangent.astype(jnp.float32)
    grad_picked = (gates[:, :, None] * grad_out[:, None, :]).astype(jnp.bfloat16)
    grad_gates = jnp.sum(grad_out[:, None, :] * picked, axis=2)
    grad_chosen = gates * (grad_gates - jnp.sum(gates * grad_gates, axis=1, keepdims=True))
    grad_logits = jnp.sum(route_hits * grad_chosen[:, :, None], axis=1)
    grad_send = jnp.concatenate([grad_picked.reshape(2 * row_count, D), zero_row], axis=0)[
        slot_pair
    ].reshape(axis_count, per_device, capacity, D)
    grad_recv = lax.all_to_all(grad_send, "expert", split_axis=0, concat_axis=0, tiled=True)
    grad_act = jnp.einsum(
        "sekd,efd->sekf", grad_recv, second_full, preferred_element_type=jnp.float32
    )
    unused, gelu_pull = jax.vjp(gelu_tanh, pre_gelu)
    grad_pre = gelu_pull(grad_act)[0].astype(jnp.bfloat16)
    grad_rows = jnp.einsum(
        "sekf,edf->sekd", grad_pre, first_full, preferred_element_type=jnp.float32
    ).astype(jnp.bfloat16)
    grad_back = lax.all_to_all(grad_rows, "expert", split_axis=0, concat_axis=0, tiled=True)
    grad_first = jnp.einsum(
        "sekd,sekf->edf", received, grad_pre, preferred_element_type=jnp.float32
    )
    grad_second = jnp.einsum(
        "sekf,sekd->efd", activated, grad_recv, preferred_element_type=jnp.float32
    )
    grad_first, grad_second = (
        lax.psum_scatter(grad_first, "shard", scatter_dimension=2, tiled=True),
        lax.psum_scatter(grad_second, "shard", scatter_dimension=1, tiled=True),
    )
    returned = (
        grad_back.reshape(expert_count * capacity, D)[slot_dest]
        .reshape(row_count, 2, D)
        .astype(jnp.float32)
    )
    router_float = router_full.astype(jnp.float32)
    grad_moe = jnp.sum(returned, axis=1) + jnp.einsum(
        "te,de->td", grad_logits, router_float, precision=PRECISE
    )
    grad_router = jnp.einsum(
        "td,te->de", moe_low.astype(jnp.float32), grad_logits, precision=PRECISE
    )
    grad_from_moe, grad_g2 = norm_back(grad_moe, moe_hat, moe_inv, gain_two)
    grad_hidden = grad_out + grad_from_moe
    grad_low = grad_hidden.astype(jnp.bfloat16)
    grad_proj = jnp.einsum("tc,td->cd", attended, grad_low, preferred_element_type=jnp.float32)
    grad_att = (
        jnp.einsum("td,cd->tc", grad_low, proj_full, preferred_element_type=jnp.float32)
        .astype(jnp.bfloat16)
        .reshape(image_count, SEQ, HEADS, HEAD)
    )
    scores_again = (
        jnp.einsum("ishd,ithd->ihst", query_part, key_part, preferred_element_type=jnp.float32)
        * score_scale
    )
    soft_again = jnp.exp(scores_again - log_total)
    soft_again_low = soft_again.astype(jnp.bfloat16)
    grad_soft = jnp.einsum(
        "ishd,ithd->ihst", grad_att, value_part, preferred_element_type=jnp.float32
    )
    grad_value = jnp.einsum(
        "ihst,ishd->ithd", soft_again_low, grad_att, preferred_element_type=jnp.float32
    )
    row_delta = jnp.sum(soft_again * grad_soft, axis=-1, keepdims=True)
    grad_scores = (soft_again * (grad_soft - row_delta)).astype(jnp.bfloat16)
    grad_query = (
        jnp.einsum("ihst,ithd->ishd", grad_scores, key_part, preferred_element_type=jnp.float32)
        * score_scale
    )
    grad_key = (
        jnp.einsum("ihst,ishd->ithd", grad_scores, query_part, preferred_element_type=jnp.float32)
        * score_scale
    )
    grad_qkv_low = (
        jnp.stack([grad_query, grad_key, grad_value], axis=2)
        .reshape(row_count, 3 * D)
        .astype(jnp.bfloat16)
    )
    grad_qkv = jnp.einsum("tc,td->cd", attn_low, grad_qkv_low, preferred_element_type=jnp.float32)
    grad_attn_in = jnp.einsum(
        "td,cd->tc", grad_qkv_low, qkv_full, preferred_element_type=jnp.float32
    )
    grad_from_attn, grad_g1 = norm_back(grad_attn_in, attn_hat, attn_inv, gain_one)
    grad_tokens = grad_hidden + grad_from_attn
    dense_grads = (grad_g1, grad_qkv, grad_proj, grad_g2, grad_router)
    dense_total = lax.psum(
        (dense_grads[0], dense_grads[1], dense_grads[2], dense_grads[3], dense_grads[4]), "expert"
    )
    dense_parts = (
        lax.psum_scatter(dense_total[0], "shard", scatter_dimension=0, tiled=True),
        lax.psum_scatter(dense_total[1], "shard", scatter_dimension=0, tiled=True),
        lax.psum_scatter(dense_total[2], "shard", scatter_dimension=0, tiled=True),
        lax.psum_scatter(dense_total[3], "shard", scatter_dimension=0, tiled=True),
        lax.psum_scatter(dense_total[4], "shard", scatter_dimension=0, tiled=True),
    )
    return block_out, grad_tokens, dense_parts, (grad_first, grad_second)


SEQ_PAD = 224
MESH = pl.DeviceIdType.MESH
VMEM_LIMIT = 62 * 1024 * 1024
BF = jnp.bfloat16
F32 = jnp.float32


def mm(a, b):
    return lax.dot_general(a, b, (((1,), (0,)), ((), ())), preferred_element_type=F32)


def mm_nt(a, b):
    return lax.dot_general(a, b, (((1,), (1,)), ((), ())), preferred_element_type=F32)


def mm_tn(a, b):
    return lax.dot_general(a, b, (((0,), (0,)), ((), ())), preferred_element_type=F32)


def remote(src, dst, send, recv, device):
    return pltpu.make_async_remote_copy(
        src_ref=src, dst_ref=dst, send_sem=send, recv_sem=recv, device_id=device, device_id_type=MESH
    )


def greet(devices):
    barrier = pltpu.get_barrier_semaphore()
    for device in devices:
        pl.semaphore_signal(barrier, inc=1, device_id=device, device_id_type=MESH)
    pl.semaphore_wait(barrier, len(devices))


class Place:
    def __init__(self):
        expert = lax.axis_index("expert")
        self.shard = lax.axis_index("shard")
        self.z, self.core = expert // 2, expert % 2
        self.number = self.z * 4 + self.shard
        self.sibling = (self.z * 2 + 1 - self.core, self.shard)

    def plane(self, step):
        return (self.z // 2 + step // 2) % 2 * 2 + (self.z + step) % 2

    def peer(self, number):
        return (number // 4 * 2 + self.core, number % 4)

    def peers(self):
        return [self.peer((self.number + d) % 16) for d in range(1, 16)]

    def mates(self):
        return [(self.z * 2 + self.core, (self.shard + d) % 4) for d in range(1, 4)]


class Quarters:
    def __init__(self, me, source, place, send, recv, local, pass_on):
        self.me, self.source, self.place = me, source, place
        self.sems = send, recv, local, pass_on

    def outgoing(self, act):
        me, (send, recv, local, _) = self.me, self.sems
        core = me.shard % 2
        for i in range(2):
            chip = 2 * me.core + i
            own = (core == me.core) & (chip == me.shard)

            @pl.when(jnp.logical_not(own))
            def _():
                act(
                    remote(
                        self.source.at[i], self.place(me.shard), send.at[i], recv.at[me.shard // 2],
                        (me.z * 2 + core, chip),
                    )
                )

            @pl.when(own)
            def _():
                act(pltpu.make_async_copy(self.source.at[i], self.place(me.shard), local))

    def start(self):
        self.outgoing(lambda cp: cp.start())

    def handed_on(self, q):
        pass_on = self.sems[3]
        return remote(self.place(q), self.place(q), pass_on.at[0, q // 2], pass_on.at[1, q // 2], self.me.sibling)

    def forward(self):
        me, (send, recv, local, _) = self.me, self.sems
        for n in range(2):
            q = 2 * n + me.core
            here = (me.shard // 2 == me.core) & (me.shard == q)

            @pl.when(jnp.logical_not(here))
            def _():
                remote(self.source.at[0], self.place(q), send.at[0], recv.at[n], me.sibling).wait_recv()

            @pl.when(here)
            def _():
                pltpu.make_async_copy(self.source.at[0], self.place(q), local).wait()

            self.handed_on(q).start()

    def finish(self):
        me, (send, recv, _, _) = self.me, self.sems
        core = me.shard % 2
        for i in range(2):
            chip = 2 * me.core + i

            @pl.when(jnp.logical_not((core == me.core) & (chip == me.shard)))
            def _():
                remote(self.source.at[i], self.place(me.shard), send.at[i], recv.at[0], me.sibling).wait_send()

        for n in range(2):
            self.handed_on(2 * n + me.core).wait_send()
            self.handed_on(2 * n + 1 - me.core).wait_recv()


def split3(rows):
    high = rows.astype(BF)
    rest = rows - high.astype(F32)
    low = rest.astype(BF)
    last = (rest - low.astype(F32)).astype(BF)
    return high, low, last


def three_rows(row):
    high, low, last = split3(row)
    index = lax.broadcasted_iota(jnp.int32, (8, row.shape[1]), 0)
    out = jnp.where(index == 0, high.astype(F32), 0.0)
    out = jnp.where(index == 1, low.astype(F32), out)
    return jnp.where(index == 2, last.astype(F32), out).astype(BF)


def norm_stats(values):
    center = values - jnp.mean(values, axis=-1, keepdims=True)
    inv = lax.rsqrt(jnp.mean(center * center, axis=-1, keepdims=True) + EPS_NORM)
    return center * inv, inv


def fill_hits(ranks, plane, hits, cap):
    slot = lax.broadcasted_iota(jnp.int32, (cap, hits.shape[1]), 0)
    for k in range(4):
        row = ranks[pl.ds(plane * 4 + k, 1), :]
        hits[k * cap : (k + 1) * cap, :] = jnp.where(slot == row, 1.0, 0.0).astype(BF)


def kernel_a(
    cap, tok, cot, rt, dsh, w1,
    qkv, att, hid, lse, gate_t, ranks, aux, dense, xsend, gsend, cotr, wfull,
    csend, low, hits, tri, dsem, dfsem, csem, wsem, wloc, wrecv, fsem, osem,
):
    me = Place()
    z, c, s = me.z, me.core, me.shard
    rows = tok.shape[0]
    images = rows // SEQ_PAD
    other = [(z * 2 + 1 - c, t) for t in range(4)]
    greet(me.peers() + other)

    quarter = dsh.shape[0]
    half = quarter // 2
    dense_out = []
    for d in range(1, 4):
        cp = remote(
            dsh.at[pl.ds(pl.multiple_of(c * half, half), half)],
            dense.at[pl.ds(pl.multiple_of(s * quarter + c * half, half), half)],
            dsem.at[0, d], dsem.at[1, d], (z * 2 + c, (s + d) % 4),
        )
        cp.start()
        dense_out.append(cp)
    dense[pl.ds(pl.multiple_of(s * quarter, quarter), quarter), :] = dsh[...]

    expert_row = lax.broadcasted_iota(jnp.int32, (16, rows), 0)
    hit = (expert_row == rt[0:1, :]) | (expert_row == rt[1:2, :])
    earlier = lax.broadcasted_iota(jnp.int32, (rows, rows), 0) < lax.broadcasted_iota(jnp.int32, (rows, rows), 1)
    tri[...] = jnp.where(earlier, 1.0, 0.0).astype(BF)
    before = mm(jnp.where(hit, 1.0, 0.0).astype(BF), tri[...])
    ranks[...] = jnp.where(hit, before, -1.0).astype(jnp.int32)

    def cot_copy(p):
        return remote(
            csend.at[pl.ds(pl.multiple_of(p * cap, cap), cap)],
            cotr.at[pl.ds(pl.multiple_of(me.number * cap, cap), cap)],
            csem.at[0, p], csem.at[1, me.number], me.peer(p),
        )

    own = pl.multiple_of(me.number * cap, cap)
    own_copy = pltpu.make_async_copy(csend.at[pl.ds(own, cap)], cotr.at[pl.ds(own, cap)], osem)

    @pl.loop(0, 4)
    def _(step):
        plane = me.plane(3 - step)
        fill_hits(ranks, plane, hits, cap)
        csend[pl.ds(pl.multiple_of(plane * 4 * cap, 4 * cap), 4 * cap), :] = mm(hits[...], cot[...]).astype(BF)
        for k in range(4):
            p = plane * 4 + k

            @pl.when(p != me.number)
            def _():
                cot_copy(p).start()

            @pl.when(p == me.number)
            def _():
                own_copy.start()

    forwards = []
    for d in range(1, 4):
        dense_out[d - 1].wait()
        source = (s - d + 4) % 4
        place = pl.ds(pl.multiple_of(source * quarter + c * half, half), half)
        cp = remote(dense.at[place], dense.at[place], dfsem.at[0, d], dfsem.at[1, d], me.sibling)
        cp.start()
        forwards.append(cp)

    in_quarters = Quarters(me, w1, lambda q: wfull.at[q], wsem, wrecv, wloc, fsem)

    for cp in forwards:
        cp.wait()
    in_quarters.start()

    flat = jnp.transpose(dense[:, 3072:3200].astype(F32))
    aux[...] = flat[0:32, :]

    @pl.loop(0, images)
    def _(i):
        r = pl.ds(pl.multiple_of(i * SEQ_PAD, SEQ_PAD), SEQ_PAD)
        hat, _unused = norm_stats(tok[r, :].astype(F32))
        low[r, :] = (hat * aux[16:17, :]).astype(BF)

    @pl.loop(0, 3)
    def _(n):
        columns = pl.ds(pl.multiple_of(n * D, D), D)
        qkv[:, columns] = mm(low[...], dense[:, columns]).astype(BF)

    attention_forward(qkv, att, lse, images)

    wproj = dense.at[:, 2304:3072]
    @pl.loop(0, images)
    def _(i):
        r = pl.ds(pl.multiple_of(i * SEQ_PAD, SEQ_PAD), SEQ_PAD)
        hidden = tok[r, :].astype(F32) + mm(att[r, :], wproj[...])
        hid[r, :] = hidden
        hat, _unused = norm_stats(hidden)
        low[r, :] = (hat * aux[17:18, :]).astype(BF)

    logits = mm_nt(aux[0:16, :].astype(BF), low[...])
    masked = jnp.where(hit, logits, -1e30)
    weights = jnp.where(hit, jnp.exp(masked - jnp.max(masked, axis=0, keepdims=True)), 0.0)
    gate_t[...] = weights / jnp.maximum(jnp.sum(weights, axis=0, keepdims=True), 0.5)
    gsend[...] = jnp.zeros_like(gsend)

    @pl.loop(0, 4)
    def _(plane):
        fill_hits(ranks, plane, hits, cap)
        xsend[pl.ds(pl.multiple_of(plane * 4 * cap, 4 * cap), 4 * cap), :] = mm(hits[...], low[...]).astype(BF)
        for k in range(4):
            row = mm_nt(three_rows(gate_t[pl.ds(plane * 4 + k, 1), :]), hits[k * cap : (k + 1) * cap, :])
            gsend[plane * 4 + k, :, 0:cap] = jnp.broadcast_to(jnp.sum(row, axis=0, keepdims=True), (8, cap))

    in_quarters.forward()
    in_quarters.finish()
    for d in range(1, 16):
        p = (me.number + d) % 16
        cot_copy(p).wait_send()
        remote(
            csend.at[pl.ds(0, cap)], cotr.at[pl.ds(0, cap)], csem.at[0, p], csem.at[1, p], me.peer(p)
        ).wait_recv()
    own_copy.wait()


def attention_forward(qkv, att, lse, images):
    first = lax.broadcasted_iota(jnp.int32, (SEQ_PAD, 128), 1) < HEAD
    lane = lax.broadcasted_iota(jnp.int32, (SEQ_PAD, 128), 1)
    real = lax.broadcasted_iota(jnp.int32, (SEQ_PAD, SEQ_PAD), 1) < SEQ
    lse[...] = jnp.zeros_like(lse)

    @pl.loop(0, HEADS // 2)
    def _(pair):
        for i in range(images):
            r = slice(i * SEQ_PAD, (i + 1) * SEQ_PAD)
            cols = [pl.ds(pl.multiple_of(part * D + pair * 128, 128), 128) for part in range(3)]
            q, k, v = (qkv[r, cols[part]] for part in range(3))
            outs, lses = [], []
            for h in range(2):
                mine = first if h == 0 else jnp.logical_not(first)
                qh = (jnp.where(mine, q.astype(F32), 0.0) * 0.125).astype(BF)
                scores = jnp.where(real, mm_nt(qh, k), -1e30)
                top = jnp.max(scores, axis=1, keepdims=True)
                weights = jnp.exp(scores - top)
                total = jnp.sum(weights, axis=1, keepdims=True)
                lses.append(top + jnp.log(total))
                outs.append(mm((weights * (1.0 / total)).astype(BF), v))
            att[r, pl.ds(pl.multiple_of(pair * 128, 128), 128)] = jnp.where(first, outs[0], outs[1]).astype(BF)
            old = lse[r, :]
            lse[r, :] = jnp.where(lane == 2 * pair, lses[0], jnp.where(lane == 2 * pair + 1, lses[1], old))


def kernel_e(
    cap, xsend, gsend, cotr, wfull, w2,
    outs, ginh, ginb, ggb, gw,
    w1v, w2v, xr, gcot, gater, act, gpre, acc, stage, ggs, gcol,
    xsem, gsem, rsem, ggsem, lsem, wlsem, stsem, wsem, wrecv, wloc, fsem,
):
    me = Place()
    z, c, s = me.z, me.core, me.shard
    greet(me.peers() + [(z * 2 + 1 - c, t) for t in range(4)])
    block = 4 * cap

    def part(ref, p):
        return ref.at[pl.ds(pl.multiple_of(p * cap, cap), cap)]

    def x_copy(p):
        return remote(part(xsend, p), part(xr, me.number), xsem.at[0, p], xsem.at[1, me.number], me.peer(p))

    def g_copy(p):
        return remote(gsend.at[p], gater.at[me.number], gsem.at[0, p], gsem.at[1, me.number], me.peer(p))

    def r_copy(p):
        return remote(part(ginh, p), part(ginb, me.number), rsem.at[0, p], rsem.at[1, me.number], me.peer(p))

    def gg_copy(p):
        return remote(ggs.at[p], ggb.at[me.number], ggsem.at[0, p], ggsem.at[1, me.number], me.peer(p))

    local_copies = [
        pltpu.make_async_copy(part(xsend, me.number), part(xr, me.number), lsem.at[0]),
        pltpu.make_async_copy(gsend.at[me.number], gater.at[me.number], lsem.at[1]),
        pltpu.make_async_copy(cotr, gcot, lsem.at[2]),
    ]
    own_r = pltpu.make_async_copy(part(ginh, me.number), part(ginb, me.number), lsem.at[3])
    own_g = pltpu.make_async_copy(ggs.at[me.number], ggb.at[me.number], lsem.at[4])
    w_copies = [pltpu.make_async_copy(wfull, w1v, wlsem.at[0])]
    out_quarters = Quarters(
        me, w2, lambda q: w2v.at[pl.ds(pl.multiple_of(q * D, D), D)], wsem, wrecv, wloc, fsem
    )
    out_quarters.start()
    for d in range(1, 16):
        g_copy((me.number + d) % 16).start()
    for cp in local_copies + w_copies:
        cp.start()
    for step in range(4):
        for k in range(4):
            p = me.plane(step) * 4 + k

            @pl.when(p != me.number)
            def _():
                x_copy(p).start()

    ggs[...] = jnp.zeros_like(ggs)
    for cp in local_copies + w_copies:
        cp.wait()

    eye = lax.broadcasted_iota(jnp.int32, (cap, cap), 0) == lax.broadcasted_iota(jnp.int32, (cap, cap), 1)

    def recv_block(plane):
        for k in range(4):
            p = plane * 4 + k

            @pl.when(p != me.number)
            def _():
                remote(part(xsend, p), part(xr, p), xsem.at[0, p], xsem.at[1, p], me.peer(p)).wait_recv()
                remote(gsend.at[p], gater.at[p], gsem.at[0, p], gsem.at[1, p], me.peer(p)).wait_recv()

    def stage_out(plane, which):
        return pltpu.make_async_copy(
            stage.at[which], (outs if which == 0 else ginh).at[pl.ds(pl.multiple_of(plane * block, block), block)],
            stsem.at[which],
        )

    def first_half(step):
        plane = me.plane(step)
        recv_block(plane)
        r = pl.ds(pl.multiple_of(plane * block, block), block)

        @pl.loop(0, 4)
        def _(f):
            for n in range(3):
                cols = pl.ds(pl.multiple_of(f * D + n * 256, 256), 256)
                pre = mm(xr[r, :], w1v[f, :, n * 256 : (n + 1) * 256])
                square = pre * pre
                t = jnp.tanh(pre * (GELU_A + GELU_A * GELU_B * square))
                half = 0.5 + 0.5 * t
                act[r, cols] = (pre * half).astype(BF)
                slope = half + (0.5 * pre) * (1.0 - t * t) * (GELU_A + 3.0 * GELU_A * GELU_B * square)
                gpre[r, cols] = slope.astype(BF)

    first_half(0)
    first_half(1)
    out_quarters.forward()
    out_quarters.finish()

    @pl.loop(0, 4)
    def _(step):
        @pl.when(step > 1)
        def _():
            first_half(step)

        plane = me.plane(step)
        r = pl.ds(pl.multiple_of(plane * block, block), block)
        acc[...] = mm(act[r, :], w2v[...])

        for k in range(4):
            row = gater[plane * 4 + k, 0:1, 0:cap]
            column = jnp.sum(jnp.where(eye, row, 0.0), axis=1, keepdims=True)
            gcol[k * cap : (k + 1) * cap, :] = jnp.broadcast_to(column, (cap, 128))

        @pl.when(step > 0)
        def _():
            stage_out(plane, 0).wait()

        for k in range(4):
            rk = pl.ds(pl.multiple_of(plane * block + k * cap, cap), cap)
            kk = slice(k * cap, (k + 1) * cap)
            out = acc[kk, :].astype(BF).astype(F32)
            gate = gcol[kk, 0:1]
            g = gcot[rk, :].astype(F32)
            dots = jnp.sum(g * out, axis=1, keepdims=True)
            row = jnp.sum(jnp.where(eye, dots, 0.0), axis=0, keepdims=True)
            ggs[plane * 4 + k, :, 0:cap] = jnp.broadcast_to(row, (8, cap))
            stage[0, kk, :] = (gate * out).astype(BF)
            gcot[rk, :] = (gate * g).astype(BF)
        stage_out(plane, 0).start()

        @pl.loop(0, 4)
        def _(f):
            for n in range(3):
                cols = pl.ds(pl.multiple_of(f * D + n * 256, 256), 256)
                ga = mm_nt(gcot[r, :], w2v[cols, :])
                gpre[r, cols] = (ga * gpre[r, cols].astype(F32)).astype(BF)

        acc[...] = mm_nt(gpre[r, 0:D], w1v[0])
        for f in range(1, 4):
            acc[...] += mm_nt(gpre[r, f * D : (f + 1) * D], w1v[f])
        stage[1] = acc[...].astype(BF)
        stage_out(plane, 1).start()
        stage_out(plane, 1).wait()
        for k in range(4):
            p = plane * 4 + k

            @pl.when(p != me.number)
            def _():
                r_copy(p).start()
                gg_copy(p).start()

            @pl.when(p == me.number)
            def _():
                own_r.start()
                own_g.start()

    stage_out(0, 0).wait()

    @pl.loop(0, 4)
    def _(f):
        cols = pl.ds(pl.multiple_of(f * D, D), D)
        w1v[f] = mm_tn(xr[...], gpre[:, cols]).astype(BF)
        w2v[cols, :] = mm_tn(act[:, cols], gcot[...]).astype(BF)

    out_w = [pltpu.make_async_copy(w1v, gw.at[0], wlsem.at[0])] + [
        pltpu.make_async_copy(w2v.at[pl.ds(f * D, D)], gw.at[1, f], wlsem.at[1 + f]) for f in range(4)
    ]
    for cp in out_w:
        cp.start()
    for d in range(1, 16):
        p = (me.number + d) % 16
        x_copy(p).wait_send()
        g_copy(p).wait_send()
        r_copy(p).wait_send()
        gg_copy(p).wait_send()
        remote(part(ginh, p), part(ginb, p), rsem.at[0, p], rsem.at[1, p], me.peer(p)).wait_recv()
        remote(ggs.at[p], ggb.at[p], ggsem.at[0, p], ggsem.at[1, p], me.peer(p)).wait_recv()
    own_r.wait()
    own_g.wait()
    for cp in out_w:
        cp.wait()


def attention_backward(qkv, gatt, lse, gqkv, images, group):
    first = lax.broadcasted_iota(jnp.int32, (SEQ_PAD, 128), 1) < HEAD
    lane = lax.broadcasted_iota(jnp.int32, (SEQ_PAD, 128), 1)
    real = lax.broadcasted_iota(jnp.int32, (SEQ_PAD, SEQ_PAD), 1) < SEQ

    @pl.loop(0, 2)
    def _(near):
        pair = 2 * group + near
        for i in range(images):
            r = slice(i * SEQ_PAD, (i + 1) * SEQ_PAD)
            cols = [pl.ds(pl.multiple_of(part * D + pair * 128, 128), 128) for part in range(3)]
            q, k, v = (qkv[r, cols[part]] for part in range(3))
            g = gatt[r, pl.ds(pl.multiple_of(pair * 128, 128), 128)]
            logs = lse[r, :]
            parts = []
            for h in range(2):
                mine = first if h == 0 else jnp.logical_not(first)
                qh = (jnp.where(mine, q.astype(F32), 0.0) * 0.125).astype(BF)
                gh = jnp.where(mine, g.astype(F32), 0.0).astype(BF)
                log = jnp.sum(jnp.where(lane == 2 * pair + h, logs, 0.0), axis=1, keepdims=True)
                probs = jnp.where(real, jnp.exp(mm_nt(qh, k) - log), 0.0)
                grad_probs = mm_nt(gh, v)
                low = probs.astype(BF)
                delta = jnp.sum(probs * grad_probs, axis=1, keepdims=True)
                grad_scores = (probs * (grad_probs - delta)).astype(BF)
                parts.append((mm(grad_scores, k) * 0.125, mm_tn(grad_scores, q) * 0.125, mm_tn(low, g)))
            for part in range(3):
                place = pl.ds(pl.multiple_of(group * D + part * 256 + near * 128, 128), 128)
                gqkv[r, place] = jnp.where(first, parts[0][part], parts[1][part]).astype(BF)


def kernel_b(
    cap, tok, cot, dense, aux, qkv, att, hid, lse, gate_t, ranks, ggb, ginb, outs, gw,
    block_out, gtok, ghat, extra, outb, eg,
    rowsv, hits, gmoe, low, glow, gatt, gqkv, gd, ra, rb, sc, rc, exs, exl, gx, own_w, ggt,
    osem, lsem, wxsem, wsem, wload, wlocal, asem, bsem, zsem, fsem, esem, xsem,
):
    me = Place()
    z, c, s = me.z, me.core, me.shard
    rows = tok.shape[0]
    images = rows // SEQ_PAD
    block = 4 * cap
    quarter, wide, deep = D // 4, D // 2, D // 16
    greet(me.peers() + [(z * 2 + 1 - c, t) for t in range(4)])

    def part(ref, p):
        return ref.at[pl.ds(pl.multiple_of(p * cap, cap), cap)]

    def o_copy(p):
        return remote(part(outs, p), part(outb, me.number), osem.at[0, p], osem.at[1, me.number], me.peer(p))

    load_in = pltpu.make_async_copy(ginb, rowsv, lsem.at[0])
    load_in.start()
    swap = [remote(gw.at[1 - c, t], gx.at[t], wxsem.at[0, t], wxsem.at[1, t], me.sibling) for t in range(4)]
    for cp in swap:
        cp.start()
    own_o = pltpu.make_async_copy(part(outs, me.number), part(outb, me.number), lsem.at[1])
    own_o.start()

    def send_outs(step):
        for k in range(4):
            p = me.plane(step) * 4 + k

            @pl.when(p != me.number)
            def _():
                o_copy(p).start()

    for step in (3, 2, 1, 0):
        send_outs(step)

    load_in.wait()
    gmoe[...] = jnp.zeros_like(gmoe)

    @pl.loop(0, 4)
    def _(plane):
        fill_hits(ranks, plane, hits, cap)
        for k in range(4):
            rows8 = three_rows(ggb[plane * 4 + k, 0:1, 0:cap])
            row = mm(rows8, hits[k * cap : (k + 1) * cap, :])
            ggt[pl.ds(plane * 4 + k, 1), :] = jnp.sum(row, axis=0, keepdims=True)
        r = pl.ds(pl.multiple_of(plane * block, block), block)
        gmoe[...] += mm_tn(hits[...], rowsv[r, :])

    gates = gate_t[...]
    grad_gates = ggt[...]
    grad_logits = gates * (grad_gates - jnp.sum(gates * grad_gates, axis=0, keepdims=True))
    gl_high = grad_logits.astype(BF)
    gl_low = (grad_logits - gl_high.astype(F32)).astype(BF)

    @pl.loop(0, images)
    def _(i):
        r = pl.ds(pl.multiple_of(i * SEQ_PAD, SEQ_PAD), SEQ_PAD)
        hat, _unused = norm_stats(hid[r, :])
        low[r, :] = (hat * aux[17:18, :]).astype(BF)

    router = aux[0:16, :].astype(BF)
    gmoe[...] += mm_tn(gl_high, router) + mm_tn(gl_low, router)
    exs[0, 0:16, :] = mm(gl_high, low[...]) + mm(gl_low, low[...])
    exs[0, 16:32, :] = jnp.zeros((16, D), F32)

    @pl.loop(0, images)
    def _(i):
        r = pl.ds(pl.multiple_of(i * SEQ_PAD, SEQ_PAD), SEQ_PAD)
        hat, inv = norm_stats(hid[r, :])
        w = gmoe[r, :]
        scaled = w * aux[17:18, :]
        back = inv * (
            scaled - jnp.mean(scaled, axis=-1, keepdims=True) - hat * jnp.mean(scaled * hat, axis=-1, keepdims=True)
        )
        grad = cot[r, :].astype(F32) + back
        gtok[r, :] = grad
        glow[r, :] = grad.astype(BF)
        exs[0, 17:18, :] += jnp.sum(w * hat, axis=0, keepdims=True)
        hat, _unused = norm_stats(tok[r, :].astype(F32))
        low[r, :] = (hat * aux[16:17, :]).astype(BF)

    def put(group, value):
        for t in range(4):
            for h in range(2):
                gd[group, t, h] = value[t * quarter : (t + 1) * quarter, h * wide : (h + 1) * wide].astype(BF)

    def stage_a(g):
        return [
            remote(gd.at[g, t, 1 - c], ra.at[g, t], asem.at[0, g, t], asem.at[1, g, t], me.sibling) for t in range(4)
        ]

    def stage_b(g):
        return [
            remote(
                gd.at[g, (s + d) % 4, c], rb.at[g, d], bsem.at[0, g, d], bsem.at[1, g, d], (z * 2 + c, (s + d) % 4)
            )
            for d in range(1, 4)
        ]

    def stage_c(g):
        return [
            remote(
                sc.at[g, pl.ds(pl.multiple_of((z + d) % 4 * deep, deep), deep)], rc.at[g, d],
                zsem.at[0, g, d], zsem.at[1, g, d], ((z + d) % 4 * 2 + c, s),
            )
            for d in range(1, 4)
        ]

    my_rows = pl.ds(pl.multiple_of(z * deep, deep), deep)

    def stage_d(g):
        return [
            remote(
                ghat.at[g, c, my_rows], ghat.at[g, c, my_rows],
                fsem.at[0, g, d], fsem.at[1, g, d], ((z + d) % 4 * 2 + c, s),
            )
            for d in range(1, 4)
        ]

    def stage_e(g):
        return [remote(ghat.at[g, c], ghat.at[g, c], esem.at[0, g], esem.at[1, g], me.sibling)]

    def start(copies):
        for cp in copies:
            cp.start()

    def finish(copies):
        for cp in copies:
            cp.wait()

    def to_b(g):
        finish(stage_a(g))
        for t in range(4):
            gd[g, t, c] = (gd[g, t, c].astype(F32) + ra[g, t].astype(F32)).astype(BF)
        start(stage_b(g))

    def to_c(g):
        finish(stage_b(g))
        sc[g] = (
            (gd[g, s, c].astype(F32) + rb[g, 1].astype(F32)) + (rb[g, 2].astype(F32) + rb[g, 3].astype(F32))
        ).astype(BF)
        start(stage_c(g))

    def to_d(g):
        finish(stage_c(g))
        ghat[g, c, my_rows, :] = (
            (sc[g, my_rows, :].astype(F32) + rc[g, 1].astype(F32)) + (rc[g, 2].astype(F32) + rc[g, 3].astype(F32))
        ).astype(BF)
        start(stage_d(g))

    def to_e(g):
        finish(stage_d(g))
        start(stage_e(g))

    put(3, mm_tn(att[...], glow[...]))
    start(stage_a(3))
    gatt[...] = mm_nt(glow[...], dense[:, 2304:3072]).astype(BF)

    def owner_copy(t):
        return remote(
            gx.at[t], eg.at[s % 2, c], wsem.at[0, t], wsem.at[1, s % 2 * 2 + c], (z * 2 + s // 2, t)
        )

    mine_local = s // 2 == c
    owner_local = pltpu.make_async_copy(gx.at[s], eg.at[s % 2, c], wlocal)
    def to_owner(t):
        load = pltpu.make_async_copy(gw.at[c, t], own_w, wload)
        load.start()
        load.wait()
        remote(gw.at[1 - c, t], gx.at[t], wxsem.at[0, t], wxsem.at[1, t], me.sibling).wait()
        gx[t] = (gx[t].astype(F32) + own_w[...].astype(F32)).astype(BF)

        @pl.when(jnp.logical_not(mine_local & (s == t)))
        def _():
            owner_copy(t).start()

        @pl.when(mine_local & (s == t))
        def _():
            owner_local.start()

    for d in (1, 2, 3, 0):
        to_owner((s + d) % 4)
    to_b(3)
    for g in range(3):
        attention_backward(qkv, gatt, lse, gqkv, images, g)
        put(g, mm_tn(low[...], gqkv[:, g * D : (g + 1) * D]))
        start(stage_a(g))
        partial = [
            mm_nt(gqkv[:, g * D + 256 * n : g * D + 256 * (n + 1)], dense[:, n * D + g * 256 : n * D + (g + 1) * 256])
            for n in range(3)
        ]
        if g == 0:
            gmoe[...] = (partial[0] + partial[1]) + partial[2]
        else:
            gmoe[...] += (partial[0] + partial[1]) + partial[2]
            to_b(g - 1)

    @pl.loop(0, images)
    def _(i):
        r = pl.ds(pl.multiple_of(i * SEQ_PAD, SEQ_PAD), SEQ_PAD)
        hat, inv = norm_stats(tok[r, :].astype(F32))
        w = gmoe[r, :]
        scaled = w * aux[16:17, :]
        gtok[r, :] += inv * (
            scaled - jnp.mean(scaled, axis=-1, keepdims=True) - hat * jnp.mean(scaled * hat, axis=-1, keepdims=True)
        )
        exs[0, 16:17, :] += jnp.sum(w * hat, axis=0, keepdims=True)

    to_b(2)
    x_first = remote(exs.at[0], exl.at[0], xsem.at[0, 0], xsem.at[1, 0], me.sibling)
    x_first.start()
    to_c(3)
    x_first.wait()
    exs[1] = exs[0] + exl[0]
    exl[1 + s] = exs[1]
    x_second = [
        remote(exs.at[1], exl.at[1 + s], xsem.at[0, d], xsem.at[1, d], (z * 2 + c, (s + d) % 4)) for d in range(1, 4)
    ]
    start(x_second)
    to_c(0)
    to_c(1)
    to_c(2)
    finish(x_second)
    exs[2] = (exl[1] + exl[2]) + (exl[3] + exl[4])
    exl[5 + z] = exs[2]
    x_third = [
        remote(exs.at[2], exl.at[5 + z], xsem.at[0, 3 + d], xsem.at[1, 3 + d], ((z + d) % 4 * 2 + c, s))
        for d in range(1, 4)
    ]
    start(x_third)
    for g in (3, 0, 1, 2):
        to_d(g)
    finish(x_third)
    extra[...] = (exl[5] + exl[6]) + (exl[7] + exl[8])
    for g in (3, 0, 1, 2):
        to_e(g)

    own_o.wait()
    for d in range(1, 16):
        p = (me.number + d) % 16
        o_copy(p).wait_send()
        remote(part(outs, p), part(outb, p), osem.at[0, p], osem.at[1, p], me.peer(p)).wait_recv()
    load_out = pltpu.make_async_copy(outb, rowsv, lsem.at[0])
    load_out.start()
    load_out.wait()
    gmoe[...] = hid[...]

    @pl.loop(0, 4)
    def _(plane):
        fill_hits(ranks, plane, hits, cap)
        r = pl.ds(pl.multiple_of(plane * block, block), block)
        gmoe[...] += mm_tn(hits[...], rowsv[r, :])

    block_out[...] = gmoe[...].astype(BF)

    for t in range(4):
        @pl.when(jnp.logical_not(mine_local & (s == t)))
        def _():
            owner_copy(t).wait_send()

        @pl.when(mine_local & (s == t))
        def _():
            owner_local.wait()

    for i in range(2):
        for a in range(2):
            own = (a == c) & (s == 2 * c + i)

            @pl.when(jnp.logical_not(own))
            def _():
                remote(gx.at[0], eg.at[i, a], wsem.at[0, 0], wsem.at[1, i * 2 + a], me.sibling).wait_recv()

    for g in range(4):
        finish(stage_e(g))


def lane_sums(values, count):
    lane = lax.broadcasted_iota(jnp.int32, (1, count), 1)
    out = jnp.zeros((1, count), F32)
    for n, value in enumerate(values):
        out = jnp.where(lane == n, value, out)
    return out


def total(values):
    return jnp.sum(jnp.sum(values, axis=1, keepdims=True), axis=0, keepdims=True)


def set_columns(ref, columns):
    lane = lax.broadcasted_iota(jnp.int32, ref.shape, 1)
    out = jnp.zeros(ref.shape, F32)
    for n, column in enumerate(columns):
        out = jnp.where(lane == n, column, out)
    ref[...] = out


def pick(row, n):
    lane = lax.broadcasted_iota(jnp.int32, row.shape, 1)
    return jnp.sum(jnp.where(lane == n, row, 0.0), axis=1, keepdims=True)


def mean_square(square_sum, weight_sum, size):
    rms = jnp.sqrt(square_sum * (1.0 / size))
    return rms, -RATE * jnp.sqrt(weight_sum * (1.0 / size)) / jnp.maximum(CLIP, rms)


def kernel_s(
    eg, ghat, extra, w1, w2, dsh, gains, moments, rows3, row_router, v_gain,
    mine_new, v_new, rows3_new, row_router_new, moments_new, sums, sums_r,
    egv, tall, turned, stats, landed, stats_r, landed_r, dgrad,
    isem, xsem, rsem,
):
    me = Place()
    z, c, s = me.z, me.core, me.shard
    quarter = dsh.shape[0]
    load = pltpu.make_async_copy(eg, egv, isem)
    load.start()
    greet(me.mates())

    read_dense(ghat, dgrad)
    mine = jnp.zeros((32, quarter), F32)
    for t in range(4):
        mine = mine + jnp.where(s == t, extra[:, t * quarter : (t + 1) * quarter], 0.0)
    mine_new[...] = mine
    router = mine[0:16, :]
    gain = mine[16:18, :]
    v = DECAY * v_gain[...] + (1.0 - DECAY) * (gain * gain + EPS_SQUARE)
    v_new[...] = v
    raw_gain = gain * lax.rsqrt(v)
    gain_weight = gains[...].astype(F32)
    gain_square = jnp.sum(raw_gain * raw_gain, axis=1, keepdims=True)
    gain_size = jnp.sum(gain_weight * gain_weight, axis=1, keepdims=True)
    router_square = router * router
    router_row = DECAY * row_router[...] + (1.0 - DECAY) * (
        jnp.sum(router_square, axis=0, keepdims=True) * (1.0 / 16) + EPS_SQUARE
    )
    row_router_new[...] = router_row
    set_columns(
        stats_r,
        [
            jnp.sum(router_square, axis=1, keepdims=True) + quarter * EPS_SQUARE,
            jnp.sum(router_square * (1.0 / router_row), axis=1, keepdims=True),
        ],
    )
    router_weight = dsh[:, 4 * D : 4 * D + 16].astype(F32)
    qkv_square = dgrad[:, : 3 * D] * dgrad[:, : 3 * D]
    proj_square = dgrad[:, 3 * D :] * dgrad[:, 3 * D :]
    row_qkv = DECAY * rows3[:, 0:1] + (1.0 - DECAY) * (
        jnp.sum(qkv_square, axis=1, keepdims=True) * (1.0 / (3 * D)) + EPS_SQUARE
    )
    row_proj = DECAY * rows3[:, 1:2] + (1.0 - DECAY) * (
        jnp.sum(proj_square, axis=1, keepdims=True) * (1.0 / D) + EPS_SQUARE
    )
    rows3_new[...] = jnp.where(lax.broadcasted_iota(jnp.int32, rows3_new.shape, 1) == 0, row_qkv, row_proj)
    inv_qkv, inv_proj = 1.0 / row_qkv, 1.0 / row_proj
    for g in range(4):
        square, inv = (qkv_square[:, g * D : (g + 1) * D], inv_qkv) if g < 3 else (proj_square, inv_proj)
        stats[8 + g : 9 + g, :] = jnp.sum(square, axis=0, keepdims=True) + quarter * EPS_SQUARE
        stats[12 + g : 13 + g, :] = jnp.sum(square * inv, axis=0, keepdims=True)
    dense_weight = dsh[:, : 4 * D].astype(F32)
    sizes = [
        total(row_qkv), total(row_proj), total(router_row),
        total(dense_weight[:, : 3 * D] * dense_weight[:, : 3 * D]),
        total(dense_weight[:, 3 * D :] * dense_weight[:, 3 * D :]),
        total(router_weight * router_weight),
        gain_square[0:1], gain_square[1:2], gain_size[0:1], gain_size[1:2],
    ]

    tall[...] = jnp.zeros_like(tall)
    turned[...] = jnp.zeros_like(turned)
    turned[0:8, :] = moments[...]
    moment_columns = jnp.transpose(turned[...])
    load.wait()
    columns = []
    for i in range(2):
        grad = egv[i, 0].astype(F32)
        square = grad * grad
        col = DECAY * moments[2 + i : 3 + i, :] + (1.0 - DECAY) * (
            jnp.sum(square, axis=0, keepdims=True) * (1.0 / D) + EPS_SQUARE
        )
        moments_new[2 + i : 3 + i, :] = col
        columns.append(jnp.sum(square, axis=1, keepdims=True) + D * EPS_SQUARE)
        columns.append(jnp.sum(square * (1.0 / col), axis=1, keepdims=True))
        weight = w1[i].astype(F32)
        sizes.append(total(weight * weight))
    for i in range(2):
        grad = egv[i, 1].astype(F32)
        square = grad * grad
        row = DECAY * moment_columns[:, 4 + i : 5 + i] + (1.0 - DECAY) * (
            jnp.sum(square, axis=1, keepdims=True) * (1.0 / D) + EPS_SQUARE
        )
        columns.append(row)
        stats[4 + i : 5 + i, :] = jnp.sum(square, axis=0, keepdims=True) + D * EPS_SQUARE
        stats[6 + i : 7 + i, :] = jnp.sum(square * (1.0 / row), axis=0, keepdims=True)
        weight = w2[i].astype(F32)
        sizes.append(total(weight * weight))
        sizes.append(total(row))
    set_columns(tall, columns)
    flat = jnp.transpose(tall[...])
    for n, m in ((0, 0), (2, 1), (1, 2), (3, 3)):
        stats[m : m + 1, :] = flat[n : n + 1, :]
    moments_new[0:2, :] = flat[4:6, :]
    moments_new[4:8, :] = jnp.zeros((4, D), F32)
    stats[16:24, :] = jnp.zeros((8, D), F32)
    stats[16:17, :] = lane_sums(sizes, D)

    landed[s] = stats[...]
    landed_r[s] = stats_r[...]
    copies = []
    for d in range(1, 4):
        mate = (z * 2 + c, (s + d) % 4)
        copies.append(remote(stats, landed.at[s], xsem.at[0, d], xsem.at[1, d], mate))
        copies.append(remote(stats_r, landed_r.at[s], rsem.at[0, d], rsem.at[1, d], mate))
    for cp in copies:
        cp.start()
    for cp in copies:
        cp.wait()
    sums[...] = (landed[0] + landed[1]) + (landed[2] + landed[3])
    sums_r[...] = (landed_r[0] + landed_r[1]) + (landed_r[2] + landed_r[3])


def read_dense(ghat, dgrad):
    for g in range(4):
        for n in range(6):
            column = 3 * D + 128 * n if g == 3 else n // 2 * D + g * 256 + n % 2 * 128
            dgrad[:, column : column + 128] = ghat[g, n // 3, :, n % 3 * 128 : n % 3 * 128 + 128].astype(F32)


def kernel_u(
    eg, ghat, mine, w1, w2, dsh, gains, moments, moments_mid, rows3, row_router, cols, col_router, v, sums, sums_r,
    g_first, g_second, n_first, n_second, dense_rms, expert_rms, n_gain, g_qkv, n_qkv, g_proj, n_proj, n_router,
    cols_new, col_router_new, row_in_new, col_out_new,
    egv, grads, news, turned, tall_d, dgrad,
    isem, gsem, nsem,
):
    quarter = dsh.shape[0]
    load = pltpu.make_async_copy(eg, egv, isem)
    load.start()
    read_dense(ghat, dgrad)
    g_qkv[...] = dgrad[:, : 3 * D]
    g_proj[...] = dgrad[:, 3 * D :]
    router, gain = mine[0:16, :], mine[16:18, :]
    raw_gain = gain * lax.rsqrt(v[...])
    gain_weight = gains[...].astype(F32)
    router_row = row_router[...]
    router_weight = dsh[:, 4 * D : 4 * D + 16].astype(F32)
    row_qkv, row_proj = rows3[:, 0:1], rows3[:, 1:2]
    scalars = sums[16:17, :]
    one = lambda n: pick(scalars, n)
    load.wait()

    hidden = 4.0 * D
    row_in = DECAY * moments[0:2, :] + (1.0 - DECAY) * (sums[0:2, :] * (1.0 / hidden))
    row_in_new[...] = row_in
    col_out = DECAY * moments[6:8, :] + (1.0 - DECAY) * (sums[4:6, :] * (1.0 / hidden))
    col_out_new[...] = col_out
    turned[...] = jnp.zeros_like(turned)
    turned[0:2, :] = row_in
    turned[2:4, :] = moments_mid[0:2, :]
    back = jnp.transpose(turned[...])
    rms_all = []
    for i in range(2):
        r = row_in[i : i + 1, :]
        mean = jnp.sum(r, axis=1, keepdims=True) * (1.0 / D)
        raw = mean * jnp.sum(sums[2 + i : 3 + i, :] / r, axis=1, keepdims=True)
        rms, factor = mean_square(raw, one(10 + i), D * hidden)
        rms_all.append(rms)
        left = factor * lax.rsqrt(back[:, i : i + 1] / mean)
        grads[i] = egv[i, 0].astype(F32)
        pltpu.make_async_copy(grads.at[i], g_first.at[i], gsem.at[i]).start()
        news[i] = w1[i].astype(F32) + grads[i] * left * lax.rsqrt(moments_mid[2 + i : 3 + i, :])
        pltpu.make_async_copy(news.at[i], n_first.at[i], nsem.at[i]).start()
    for i in range(2):
        col = col_out[i : i + 1, :]
        mean = one(13 + 2 * i) * (1.0 / hidden)
        raw = mean * jnp.sum(sums[6 + i : 7 + i, :] / col, axis=1, keepdims=True)
        rms, factor = mean_square(raw, one(12 + 2 * i), D * hidden)
        rms_all.append(rms)
        left = factor * lax.rsqrt(back[:, 2 + i : 3 + i] / mean)
        grads[2 + i] = egv[i, 1].astype(F32)
        pltpu.make_async_copy(grads.at[2 + i], g_second.at[i], gsem.at[2 + i]).start()
        news[2 + i] = w2[i].astype(F32) + grads[2 + i] * left * lax.rsqrt(col)
        pltpu.make_async_copy(news.at[2 + i], n_second.at[i], nsem.at[2 + i]).start()
    expert_rms[...] = lane_sums(rms_all, 128)

    rms_g1, factor_g1 = mean_square(one(6), one(8), D)
    rms_g2, factor_g2 = mean_square(one(7), one(9), D)
    upper = lax.broadcasted_iota(jnp.int32, gain.shape, 0) == 0
    n_gain[...] = gain_weight + jnp.where(upper, factor_g1, factor_g2) * raw_gain
    col_dense = []
    for g in range(4):
        col = DECAY * cols[g : g + 1, :] + (1.0 - DECAY) * (sums[8 + g : 9 + g, :] * (1.0 / D))
        cols_new[g : g + 1, :] = col
        col_dense.append(col)
    mean_qkv, mean_proj, mean_router = one(0) * (1.0 / D), one(1) * (1.0 / D), one(2) * (1.0 / D)
    ratio = [jnp.sum(sums[12 + g : 13 + g, :] / col_dense[g], axis=1, keepdims=True) for g in range(4)]
    rms_qkv, factor_qkv = mean_square(mean_qkv * (ratio[0] + ratio[1] + ratio[2]), one(3), 3 * D * D)
    rms_proj, factor_proj = mean_square(mean_proj * ratio[3], one(4), D * D)
    left_qkv = factor_qkv * lax.rsqrt(row_qkv / mean_qkv)
    left_proj = factor_proj * lax.rsqrt(row_proj / mean_proj)
    for g in range(4):
        part = slice(g * D, (g + 1) * D)
        new = dsh[:, part].astype(F32) + dgrad[:, part] * (left_qkv if g < 3 else left_proj) * lax.rsqrt(col_dense[g])
        if g < 3:
            n_qkv[:, part] = new
        else:
            n_proj[...] = new
    col = DECAY * col_router[...] + (1.0 - DECAY) * (sums_r[:, 0:1] * (1.0 / D))
    col_router_new[...] = col
    raw_router = mean_router * jnp.sum(sums_r[:, 1:2] / col, axis=0, keepdims=True)
    rms_router, factor_router = mean_square(raw_router, one(5), 16 * D)
    tall_d[...] = jnp.zeros_like(tall_d)
    tall_d[0:16, 0:quarter] = router * (factor_router * lax.rsqrt(router_row / mean_router)) * lax.rsqrt(col)
    n_router[...] = router_weight + jnp.transpose(tall_d[...])[0:quarter, 0:16]
    dense_rms[...] = lane_sums([rms_g1, rms_g2, rms_qkv, rms_proj, rms_router], 128)
    for i in range(2):
        pltpu.make_async_copy(news.at[i], n_first.at[i], nsem.at[i]).wait()
        pltpu.make_async_copy(news.at[2 + i], n_second.at[i], nsem.at[2 + i]).wait()
        pltpu.make_async_copy(grads.at[i], g_first.at[i], gsem.at[i]).wait()
        pltpu.make_async_copy(grads.at[2 + i], g_second.at[i], gsem.at[2 + i]).wait()


def params(number):
    return pltpu.CompilerParams(collective_id=number, has_side_effects=True, vmem_limit_bytes=VMEM_LIMIT)


def dma(*shape):
    return pltpu.SemaphoreType.DMA(shape)


def fast(
    tokens, routes, cotangent, gain_attn, w_qkv, w_proj, gain_moe, w_router, w_in, w_out,
    v_attn, v_moe, row_qkv, col_qkv, row_proj, col_proj, row_router, col_router, row_in, col_in, row_out, col_out,
):
    count = tokens.shape[0]
    images = count // SEQ
    rows = images * SEQ_PAD
    experts = w_router.shape[1]
    cap = ((3 * count + experts - 1) // experts + 15) // 16 * 16
    slots = experts * cap
    vmem = pl.BlockSpec(memory_space=pltpu.VMEM)
    hbm = pl.BlockSpec(memory_space=pl.ANY)
    shape = jax.ShapeDtypeStruct

    def padded(array, value=0):
        array = array.reshape(images, SEQ, array.shape[1])
        array = jnp.pad(array, ((0, 0), (0, SEQ_PAD - SEQ), (0, 0)), constant_values=value)
        return array.reshape(rows, array.shape[2])

    tok = padded(tokens)
    cot = padded(cotangent)
    rt = padded(routes, -1).T
    quarter = w_qkv.shape[0]
    small = jnp.concatenate([w_router, gain_attn[:, None], gain_moe[:, None]], axis=1)
    small = jnp.pad(small, ((0, 0), (0, 128 - small.shape[1])))
    dsh = jnp.concatenate([w_qkv, w_proj, small], axis=1)
    wide = dsh.shape[1]

    qkv, att, hid, lse, gate_t, ranks, aux, dense, xsend, gsend, cotr, wfull = pl.pallas_call(
        functools.partial(kernel_a, cap),
        out_shape=(
            shape((rows, 3 * D), BF), shape((rows, D), BF), shape((rows, D), F32), shape((rows, 128), F32),
            shape((16, rows), F32), shape((16, rows), jnp.int32), shape((32, D), F32), shape((D, wide), BF),
            shape((slots, D), BF), shape((16, 8, 256), F32), shape((slots, D), BF), shape((4, D, D), BF),
        ),
        in_specs=[vmem] * 4 + [hbm],
        out_specs=(vmem,) * 10 + (hbm,) * 2,
        scratch_shapes=[
            pltpu.VMEM((slots, D), BF), pltpu.VMEM((rows, D), BF), pltpu.VMEM((4 * cap, rows), BF),
            pltpu.VMEM((rows, rows), BF), dma(2, 4), dma(2, 4), dma(2, 16), dma(2), dma(), dma(2), dma(2, 2), dma(),
        ],
        compiler_params=params(1),
        name="forward",
    )(tok, cot, rt, dsh, w_in)

    outs, ginh, ginb, ggb, gw = pl.pallas_call(
        functools.partial(kernel_e, cap),
        out_shape=(
            shape((slots, D), BF), shape((slots, D), BF), shape((slots, D), BF), shape((16, 8, 256), F32),
            shape((2, 4, D, D), BF),
        ),
        in_specs=[hbm, vmem, hbm, hbm, hbm],
        out_specs=(hbm, hbm, hbm, vmem, hbm),
        scratch_shapes=[
            pltpu.VMEM((4, D, D), BF), pltpu.VMEM((FF, D), BF), pltpu.VMEM((slots, D), BF), pltpu.VMEM((slots, D), BF),
            pltpu.VMEM((16, 8, 256), F32), pltpu.VMEM((slots, FF), BF), pltpu.VMEM((slots, FF), BF),
            pltpu.VMEM((4 * cap, D), F32), pltpu.VMEM((2, 4 * cap, D), BF),
            pltpu.VMEM((16, 8, 256), F32), pltpu.VMEM((4 * cap, 128), F32),
            dma(2, 16), dma(2, 16), dma(2, 16), dma(2, 16), dma(5), dma(5), dma(2), dma(2), dma(2), dma(), dma(2, 2),
        ],
        compiler_params=params(2),
        name="experts",
    )(xsend, gsend, cotr, wfull, w_out)

    block_out, gtok, ghat, extra, outb, eg = pl.pallas_call(
        functools.partial(kernel_b, cap),
        out_shape=(
            shape((rows, D), BF), shape((rows, D), F32), shape((4, 2, quarter, D // 2), BF), shape((32, D), F32),
            shape((slots, D), BF), shape((2, 2, D, D), BF),
        ),
        in_specs=[vmem] * 11 + [hbm] * 3,
        out_specs=(vmem,) * 4 + (hbm,) * 2,
        scratch_shapes=[
            pltpu.VMEM((slots, D), BF), pltpu.VMEM((4 * cap, rows), BF), pltpu.VMEM((rows, D), F32),
            pltpu.VMEM((rows, D), BF), pltpu.VMEM((rows, D), BF), pltpu.VMEM((rows, D), BF),
            pltpu.VMEM((rows, 3 * D), BF), pltpu.VMEM((4, 4, 2, quarter, D // 2), BF),
            pltpu.VMEM((4, 4, quarter, D // 2), BF), pltpu.VMEM((4, 4, quarter, D // 2), BF),
            pltpu.VMEM((4, quarter, D // 2), BF), pltpu.VMEM((4, 4, quarter // 4, D // 2), BF),
            pltpu.VMEM((3, 32, D), F32), pltpu.VMEM((9, 32, D), F32), pltpu.VMEM((4, D, D), BF),
            pltpu.VMEM((D, D), BF), pltpu.VMEM((16, rows), F32),
            dma(2, 16), dma(2), dma(2, 4), dma(2, 4), dma(), dma(), dma(2, 4, 4), dma(2, 4, 4), dma(2, 4, 4),
            dma(2, 4, 4), dma(2, 4), dma(2, 7),
        ],
        compiler_params=params(3),
        name="backward",
    )(tok, cot, dense, aux, qkv, att, hid, lse, gate_t, ranks, ggb, ginb, outs, gw)

    def unpadded(array):
        return array.reshape(images, SEQ_PAD, D)[:, :SEQ].reshape(count, D)

    gains = jnp.stack([gain_attn, gain_moe])
    moments = jnp.concatenate([row_in, col_in, row_out, col_out])
    mine, v_new, rows_new, row_router_new, moments_mid, sums, sums_r = pl.pallas_call(
        kernel_s,
        out_shape=(
            shape((32, quarter), F32), shape((2, quarter), F32), shape((quarter, 2), F32), shape((1, quarter), F32),
            shape((8, D), F32), shape((24, D), F32), shape((16, 128), F32),
        ),
        in_specs=[hbm] + [vmem] * 10,
        out_specs=(vmem,) * 7,
        scratch_shapes=[
            pltpu.VMEM((2, 2, D, D), BF), pltpu.VMEM((D, 128), F32), pltpu.VMEM((128, D), F32),
            pltpu.VMEM((24, D), F32), pltpu.VMEM((4, 24, D), F32), pltpu.VMEM((16, 128), F32),
            pltpu.VMEM((4, 16, 128), F32), pltpu.VMEM((quarter, 4 * D), F32), dma(), dma(2, 4), dma(2, 4),
        ],
        compiler_params=params(4),
        name="update_sums",
    )(
        eg, ghat, extra, w_in, w_out, dsh, gains, moments, jnp.stack([row_qkv, row_proj], axis=1), row_router[None],
        jnp.stack([v_attn, v_moe]),
    )
    (
        g_first, g_second, n_first, n_second, dense_rms, expert_rms, n_gain, g_qkv, n_qkv, g_proj, n_proj, n_router,
        cols_new, col_router_new, row_in_new, col_out_new,
    ) = pl.pallas_call(
        kernel_u,
        out_shape=(
            shape((2, D, D), F32), shape((2, D, D), F32), shape((2, D, D), F32), shape((2, D, D), F32),
            shape((1, 128), F32), shape((1, 128), F32), shape((2, quarter), F32),
            shape((quarter, 3 * D), F32), shape((quarter, 3 * D), F32),
            shape((quarter, D), F32), shape((quarter, D), F32), shape((quarter, 16), F32),
            shape((4, D), F32), shape((16, 1), F32), shape((2, D), F32), shape((2, D), F32),
        ),
        in_specs=[hbm] + [vmem] * 15,
        out_specs=(hbm,) * 4 + (vmem,) * 12,
        scratch_shapes=[
            pltpu.VMEM((2, 2, D, D), BF), pltpu.VMEM((4, D, D), F32), pltpu.VMEM((4, D, D), F32),
            pltpu.VMEM((128, D), F32), pltpu.VMEM((128, 256), F32), pltpu.VMEM((quarter, 4 * D), F32),
            dma(), dma(4), dma(4),
        ],
        compiler_params=pltpu.CompilerParams(vmem_limit_bytes=VMEM_LIMIT),
        name="update",
    )(
        eg, ghat, mine, w_in, w_out, dsh, gains, moments, moments_mid, rows_new, row_router_new,
        jnp.concatenate([col_qkv, col_proj]).reshape(4, D), col_router[:, None], v_new, sums, sums_r,
    )
    return (
        unpadded(block_out), unpadded(gtok), dense_rms[0, :5], expert_rms[0, :4].reshape(2, 2).T,
        mine[16], n_gain[0], v_new[0], mine[17], n_gain[1], v_new[1],
        g_qkv, n_qkv, rows_new[:, 0], cols_new[:3].reshape(3 * D),
        g_proj, n_proj, rows_new[:, 1], cols_new[3],
        mine[:16].T, n_router, row_router_new[0], col_router_new[:, 0],
        g_first, n_first, row_in_new, moments_mid[2:4],
        g_second, n_second, moments_mid[0:2], col_out_new,
    )


def local(
    tokens, routes, cotangent, gain_attn, w_qkv, w_proj, gain_moe, w_router, w_in, w_out,
    v_attn, v_moe, row_qkv, col_qkv, row_proj, col_proj, row_router, col_router, row_in, col_in, row_out, col_out,
):
    if (
        lax.axis_size("shard") == 4
        and lax.axis_size("expert") == 8
        and w_in.shape == w_out.shape == (2, D, D)
        and tokens.shape[0] % SEQ == 0
    ):
        return fast(
            tokens, routes, cotangent, gain_attn, w_qkv, w_proj, gain_moe, w_router, w_in, w_out,
            v_attn, v_moe, row_qkv, col_qkv, row_proj, col_proj, row_router, col_router, row_in, col_in, row_out, col_out,
        )
    block_out, grad_tokens, dense_parts, expert_parts = general(
        tokens, routes, cotangent, gain_attn, w_qkv, w_proj, gain_moe, w_router, w_in, w_out
    )
    part_g1, part_qkv, part_proj, part_g2, part_router = dense_parts
    grad_first, grad_second = expert_parts
    expert_count = part_router.shape[1]
    weight_g1 = gain_attn.astype(jnp.float32)
    weight_g2 = gain_moe.astype(jnp.float32)
    dense = (
        (part_qkv, w_qkv.astype(jnp.float32), row_qkv, col_qkv),
        (part_proj, w_proj.astype(jnp.float32), row_proj, col_proj),
        (part_router, w_router.astype(jnp.float32), row_router, col_router),
    )
    weight_first = w_in.astype(jnp.float32)
    weight_second = w_out.astype(jnp.float32)
    v_attn_new = DECAY * v_attn + (1.0 - DECAY) * (part_g1 * part_g1 + EPS_SQUARE)
    v_moe_new = DECAY * v_moe + (1.0 - DECAY) * (part_g2 * part_g2 + EPS_SQUARE)
    raw_g1 = part_g1 * lax.rsqrt(v_attn_new)
    raw_g2 = part_g2 * lax.rsqrt(v_moe_new)
    dense_rows, dense_sums = [], []
    for grad, weight, row, col in dense:
        square = grad * grad
        row_new = DECAY * row + (1.0 - DECAY) * jnp.mean(square + EPS_SQUARE, axis=1)
        dense_rows.append(row_new)
        dense_sums.append(
            (
                jnp.sum(square + EPS_SQUARE, axis=0),
                jnp.sum(square / row_new[:, None], axis=0),
                jnp.stack([jnp.sum(row_new), jnp.sum(weight * weight)]),
            )
        )
    square_first = grad_first * grad_first
    square_second = grad_second * grad_second
    col_in_new = DECAY * col_in + (1.0 - DECAY) * jnp.mean(square_first + EPS_SQUARE, axis=1)
    row_out_new = DECAY * row_out + (1.0 - DECAY) * jnp.mean(square_second + EPS_SQUARE, axis=2)
    gain_sums = jnp.stack(
        [
            jnp.sum(raw_g1 * raw_g1),
            jnp.sum(raw_g2 * raw_g2),
            jnp.sum(weight_g1 * weight_g1),
            jnp.sum(weight_g2 * weight_g2),
        ]
    )
    expert_sums = (
        jnp.sum(square_first + EPS_SQUARE, axis=2),
        jnp.sum(square_first / col_in_new[:, None, :], axis=2),
        jnp.sum(square_second + EPS_SQUARE, axis=1),
        jnp.sum(square_second / row_out_new[:, :, None], axis=1),
        jnp.stack(
            [
                jnp.sum(weight_first * weight_first, axis=(1, 2)),
                jnp.sum(row_out_new, axis=1),
                jnp.sum(weight_second * weight_second, axis=(1, 2)),
            ]
        ),
    )
    expert_sums = lax.psum(expert_sums, "shard")
    dense_sums, gain_sums = lax.psum((dense_sums, gain_sums), "shard")

    def step(square_sum, weight_sum, size):
        rms = jnp.sqrt(square_sum / size)
        return rms, -RATE * jnp.sqrt(weight_sum / size) / jnp.maximum(CLIP, rms)

    rms_g1, factor_g1 = step(gain_sums[0], gain_sums[2], D)
    rms_g2, factor_g2 = step(gain_sums[1], gain_sums[3], D)
    new_g1 = weight_g1 + factor_g1 * raw_g1
    new_g2 = weight_g2 + factor_g2 * raw_g2
    dense_new, dense_cols, dense_rms = [], [], [rms_g1, rms_g2]
    for (grad, weight, _, col), row_new, (col_sum, ratio_sum, both) in zip(dense, dense_rows, dense_sums):
        col_new = DECAY * col + (1.0 - DECAY) * (col_sum / D)
        row_mean = both[0] / D
        rms, factor = step(row_mean * jnp.sum(ratio_sum / col_new), both[1], grad.shape[1] * D)
        raw = grad * lax.rsqrt(row_new[:, None] * col_new[None, :] / row_mean)
        dense_new.append(weight + factor * raw)
        dense_cols.append(col_new)
        dense_rms.append(rms)
    new_qkv, new_proj, new_router = dense_new
    row_qkv_new, row_proj_new, row_router_new = dense_rows
    col_qkv_new, col_proj_new, col_router_new = dense_cols
    row_in_sum, ratio_in, col_out_sum, ratio_out, expert_scalars = expert_sums
    row_in_new = DECAY * row_in + (1.0 - DECAY) * (row_in_sum / FF)
    col_out_new = DECAY * col_out + (1.0 - DECAY) * (col_out_sum / FF)
    mean_in = jnp.mean(row_in_new, axis=1)
    mean_out = expert_scalars[1] / FF
    rms_first, factor_first = step(mean_in * jnp.sum(ratio_in / row_in_new, axis=1), expert_scalars[0], D * FF)
    rms_second, factor_second = step(mean_out * jnp.sum(ratio_out / col_out_new, axis=1), expert_scalars[2], D * FF)
    new_first = weight_first + factor_first[:, None, None] * grad_first * lax.rsqrt(
        row_in_new[:, :, None] * col_in_new[:, None, :] / mean_in[:, None, None]
    )
    new_second = weight_second + factor_second[:, None, None] * grad_second * lax.rsqrt(
        row_out_new[:, :, None] * col_out_new[:, None, :] / mean_out[:, None, None]
    )
    return (
        block_out,
        grad_tokens,
        jnp.stack(dense_rms),
        jnp.stack([rms_first, rms_second], axis=1),
        part_g1,
        new_g1,
        v_attn_new,
        part_g2,
        new_g2,
        v_moe_new,
        part_qkv,
        new_qkv,
        row_qkv_new,
        col_qkv_new,
        part_proj,
        new_proj,
        row_proj_new,
        col_proj_new,
        part_router,
        new_router,
        row_router_new,
        col_router_new,
        grad_first,
        new_first,
        row_in_new,
        col_in_new,
        grad_second,
        new_second,
        row_out_new,
        col_out_new,
    )


def solution(mesh):
    return jax.shard_map(
        local,
        mesh=mesh,
        in_specs=(
            P(("expert", "shard"), None),
            P(("expert", "shard"), None),
            P(("expert", "shard"), None),
            P("shard"),
            P("shard", None),
            P("shard", None),
            P("shard"),
            P("shard", None),
            P("expert", None, "shard"),
            P("expert", "shard", None),
            P("shard"),
            P("shard"),
            P("shard"),
            P(),
            P("shard"),
            P(),
            P("shard"),
            P(),
            P("expert", None),
            P("expert", "shard"),
            P("expert", "shard"),
            P("expert", None),
        ),
        out_specs=(
            P(("expert", "shard"), None),
            P(("expert", "shard"), None),
            P(),
            P("expert", None),
            P("shard"),
            P("shard"),
            P("shard"),
            P("shard"),
            P("shard"),
            P("shard"),
            P("shard", None),
            P("shard", None),
            P("shard"),
            P(),
            P("shard", None),
            P("shard", None),
            P("shard"),
            P(),
            P("shard", None),
            P("shard", None),
            P("shard"),
            P(),
            P("expert", None, "shard"),
            P("expert", None, "shard"),
            P("expert", None),
            P("expert", "shard"),
            P("expert", "shard", None),
            P("expert", "shard", None),
            P("expert", "shard"),
            P("expert", None),
        ),
        check_vma=False,
    )
```

```python
import functools

import jax
import jax.numpy as jnp
from jax import lax
from jax.experimental import pallas as pl
from jax.experimental.pallas import tpu as pltpu
from jax.sharding import PartitionSpec as P

D = 768
HEADS = 12
HEAD = 64
FF = 3072
SEQ = 197


PRECISE = lax.Precision.HIGHEST
EPS_NORM = 1e-06
EPS_SQUARE = 1e-30
RATE = 0.3
DECAY = 0.5
CLIP = 0.05


GELU_A = 0.7978845608028654
GELU_B = 0.044715


def normalize(values):
    center = values - jnp.mean(values, axis=-1, keepdims=True)
    inv_root = lax.rsqrt(jnp.mean(center * center, axis=-1, keepdims=True) + EPS_NORM)
    return (center * inv_root, inv_root)


def norm_back(grad, normed, inv_root, gain):
    scaled = grad * gain
    grad_in = inv_root * (
        scaled
        - jnp.mean(scaled, axis=-1, keepdims=True)
        - normed * jnp.mean(scaled * normed, axis=-1, keepdims=True)
    )
    return (grad_in, jnp.sum(grad * normed, axis=0))


def gelu_tanh(values):
    return jax.nn.gelu(values, approximate=True)


def general(
    tokens,
    routes,
    cotangent,
    gain_attn,
    w_qkv,
    w_proj,
    gain_moe,
    w_router,
    w_in,
    w_out,
):
    gain_first, qkv_full, proj_full, gain_second, router_full = (
        lax.all_gather(gain_attn, "shard", axis=0, tiled=True),
        lax.all_gather(w_qkv, "shard", axis=0, tiled=True),
        lax.all_gather(w_proj, "shard", axis=0, tiled=True),
        lax.all_gather(gain_moe, "shard", axis=0, tiled=True),
        lax.all_gather(w_router, "shard", axis=0, tiled=True),
    )
    first_full, second_full = (
        lax.all_gather(w_in, "shard", axis=2, tiled=True),
        lax.all_gather(w_out, "shard", axis=1, tiled=True),
    )
    row_count = tokens.shape[0]
    image_count = row_count // SEQ
    expert_count = router_full.shape[1]
    per_device = w_in.shape[0]
    axis_count = lax.axis_size("expert")
    capacity = ((3 * row_count + expert_count - 1) // expert_count + 7) // 8 * 8
    score_scale = HEAD ** (-0.5)
    tok_float = tokens.astype(jnp.float32)
    gain_one = gain_first.astype(jnp.float32)
    gain_two = gain_second.astype(jnp.float32)
    attn_hat, attn_inv = normalize(tok_float)
    attn_low = (attn_hat * gain_one).astype(jnp.bfloat16)
    qkv_low = jnp.dot(attn_low, qkv_full, preferred_element_type=jnp.float32).astype(jnp.bfloat16)
    qkv_split = qkv_low.reshape(image_count, SEQ, 3, HEADS, HEAD)
    query_part = qkv_split[:, :, 0]
    key_part = qkv_split[:, :, 1]
    value_part = qkv_split[:, :, 2]
    scores = (
        jnp.einsum("ishd,ithd->ihst", query_part, key_part, preferred_element_type=jnp.float32)
        * score_scale
    )
    log_total = jax.nn.logsumexp(scores, axis=-1, keepdims=True)
    soft_low = jnp.exp(scores - log_total).astype(jnp.bfloat16)
    attended = (
        jnp.einsum("ihst,ithd->ishd", soft_low, value_part, preferred_element_type=jnp.float32)
        .reshape(row_count, D)
        .astype(jnp.bfloat16)
    )
    hidden = tok_float + jnp.dot(attended, proj_full, preferred_element_type=jnp.float32)
    moe_hat, moe_inv = normalize(hidden)
    moe_low = (moe_hat * gain_two).astype(jnp.bfloat16)
    logits = jnp.dot(moe_low, router_full, preferred_element_type=jnp.float32)
    labels = jnp.arange(expert_count, dtype=jnp.int32)
    route_hits = (routes[:, :, None] == labels[None, None, :]).astype(jnp.float32)
    chosen = jnp.sum(route_hits * logits[:, None, :], axis=2)
    gates = jax.nn.softmax(chosen, axis=-1)
    flat_routes = routes.reshape(-1)
    earlier = (jnp.arange(row_count)[:, None] > jnp.arange(row_count)[None, :]).astype(jnp.bfloat16)
    before = jnp.dot(
        earlier, jnp.sum(route_hits, axis=1).astype(jnp.bfloat16), preferred_element_type=jnp.float32
    )
    slot_rank = jnp.sum(route_hits * before[:, None, :], axis=2).astype(jnp.int32).reshape(-1)
    slot_dest = flat_routes * capacity + slot_rank
    pair_index = jnp.arange(2 * row_count, dtype=jnp.int32)
    slot_pair = (
        jnp.full((expert_count * capacity,), 2 * row_count, jnp.int32).at[slot_dest].set(pair_index)
    )
    slot_token = slot_pair // 2
    zero_row = jnp.zeros((1, D), jnp.bfloat16)
    send_rows = jnp.concatenate([moe_low, zero_row], axis=0)[slot_token].reshape(
        axis_count, per_device, capacity, D
    )
    received = lax.all_to_all(send_rows, "expert", split_axis=0, concat_axis=0, tiled=True)
    pre_gelu = jnp.einsum(
        "sekd,edf->sekf", received, first_full, preferred_element_type=jnp.float32
    )
    activated = gelu_tanh(pre_gelu).astype(jnp.bfloat16)
    expert_out = jnp.einsum(
        "sekf,efd->sekd", activated, second_full, preferred_element_type=jnp.float32
    ).astype(jnp.bfloat16)
    back_rows = lax.all_to_all(expert_out, "expert", split_axis=0, concat_axis=0, tiled=True)
    back_rows, received, pre_gelu, activated = (back_rows, received, pre_gelu, activated)
    picked = (
        back_rows.reshape(expert_count * capacity, D)[slot_dest]
        .reshape(row_count, 2, D)
        .astype(jnp.float32)
    )
    block_out = (hidden + jnp.sum(gates[:, :, None] * picked, axis=1)).astype(jnp.bfloat16)
    grad_out = cotangent.astype(jnp.float32)
    grad_picked = (gates[:, :, None] * grad_out[:, None, :]).astype(jnp.bfloat16)
    grad_gates = jnp.sum(grad_out[:, None, :] * picked, axis=2)
    grad_chosen = gates * (grad_gates - jnp.sum(gates * grad_gates, axis=1, keepdims=True))
    grad_logits = jnp.sum(route_hits * grad_chosen[:, :, None], axis=1)
    grad_send = jnp.concatenate([grad_picked.reshape(2 * row_count, D), zero_row], axis=0)[
        slot_pair
    ].reshape(axis_count, per_device, capacity, D)
    grad_recv = lax.all_to_all(grad_send, "expert", split_axis=0, concat_axis=0, tiled=True)
    grad_act = jnp.einsum(
        "sekd,efd->sekf", grad_recv, second_full, preferred_element_type=jnp.float32
    )
    unused, gelu_pull = jax.vjp(gelu_tanh, pre_gelu)
    grad_pre = gelu_pull(grad_act)[0].astype(jnp.bfloat16)
    grad_rows = jnp.einsum(
        "sekf,edf->sekd", grad_pre, first_full, preferred_element_type=jnp.float32
    ).astype(jnp.bfloat16)
    grad_back = lax.all_to_all(grad_rows, "expert", split_axis=0, concat_axis=0, tiled=True)
    grad_first = jnp.einsum(
        "sekd,sekf->edf", received, grad_pre, preferred_element_type=jnp.float32
    )
    grad_second = jnp.einsum(
        "sekf,sekd->efd", activated, grad_recv, preferred_element_type=jnp.float32
    )
    grad_first, grad_second = (
        lax.psum_scatter(grad_first, "shard", scatter_dimension=2, tiled=True),
        lax.psum_scatter(grad_second, "shard", scatter_dimension=1, tiled=True),
    )
    returned = (
        grad_back.reshape(expert_count * capacity, D)[slot_dest]
        .reshape(row_count, 2, D)
        .astype(jnp.float32)
    )
    router_float = router_full.astype(jnp.float32)
    grad_moe = jnp.sum(returned, axis=1) + jnp.einsum(
        "te,de->td", grad_logits, router_float, precision=PRECISE
    )
    grad_router = jnp.einsum(
        "td,te->de", moe_low.astype(jnp.float32), grad_logits, precision=PRECISE
    )
    grad_from_moe, grad_g2 = norm_back(grad_moe, moe_hat, moe_inv, gain_two)
    grad_hidden = grad_out + grad_from_moe
    grad_low = grad_hidden.astype(jnp.bfloat16)
    grad_proj = jnp.einsum("tc,td->cd", attended, grad_low, preferred_element_type=jnp.float32)
    grad_att = (
        jnp.einsum("td,cd->tc", grad_low, proj_full, preferred_element_type=jnp.float32)
        .astype(jnp.bfloat16)
        .reshape(image_count, SEQ, HEADS, HEAD)
    )
    scores_again = (
        jnp.einsum("ishd,ithd->ihst", query_part, key_part, preferred_element_type=jnp.float32)
        * score_scale
    )
    soft_again = jnp.exp(scores_again - log_total)
    soft_again_low = soft_again.astype(jnp.bfloat16)
    grad_soft = jnp.einsum(
        "ishd,ithd->ihst", grad_att, value_part, preferred_element_type=jnp.float32
    )
    grad_value = jnp.einsum(
        "ihst,ishd->ithd", soft_again_low, grad_att, preferred_element_type=jnp.float32
    )
    row_delta = jnp.sum(soft_again * grad_soft, axis=-1, keepdims=True)
    grad_scores = (soft_again * (grad_soft - row_delta)).astype(jnp.bfloat16)
    grad_query = (
        jnp.einsum("ihst,ithd->ishd", grad_scores, key_part, preferred_element_type=jnp.float32)
        * score_scale
    )
    grad_key = (
        jnp.einsum("ihst,ishd->ithd", grad_scores, query_part, preferred_element_type=jnp.float32)
        * score_scale
    )
    grad_qkv_low = (
        jnp.stack([grad_query, grad_key, grad_value], axis=2)
        .reshape(row_count, 3 * D)
        .astype(jnp.bfloat16)
    )
    grad_qkv = jnp.einsum("tc,td->cd", attn_low, grad_qkv_low, preferred_element_type=jnp.float32)
    grad_attn_in = jnp.einsum(
        "td,cd->tc", grad_qkv_low, qkv_full, preferred_element_type=jnp.float32
    )
    grad_from_attn, grad_g1 = norm_back(grad_attn_in, attn_hat, attn_inv, gain_one)
    grad_tokens = grad_hidden + grad_from_attn
    dense_grads = (grad_g1, grad_qkv, grad_proj, grad_g2, grad_router)
    dense_total = lax.psum(
        (dense_grads[0], dense_grads[1], dense_grads[2], dense_grads[3], dense_grads[4]), "expert"
    )
    dense_parts = (
        lax.psum_scatter(dense_total[0], "shard", scatter_dimension=0, tiled=True),
        lax.psum_scatter(dense_total[1], "shard", scatter_dimension=0, tiled=True),
        lax.psum_scatter(dense_total[2], "shard", scatter_dimension=0, tiled=True),
        lax.psum_scatter(dense_total[3], "shard", scatter_dimension=0, tiled=True),
        lax.psum_scatter(dense_total[4], "shard", scatter_dimension=0, tiled=True),
    )
    return block_out, grad_tokens, dense_parts, (grad_first, grad_second)


SEQ_PAD = 224
MESH = pl.DeviceIdType.MESH
VMEM_LIMIT = 62 * 1024 * 1024
BF = jnp.bfloat16
F32 = jnp.float32


def mm(a, b):
    return lax.dot_general(a, b, (((1,), (0,)), ((), ())), preferred_element_type=F32)


def mm_nt(a, b):
    return lax.dot_general(a, b, (((1,), (1,)), ((), ())), preferred_element_type=F32)


def mm_tn(a, b):
    return lax.dot_general(a, b, (((0,), (0,)), ((), ())), preferred_element_type=F32)


def remote(src, dst, send, recv, device):
    return pltpu.make_async_remote_copy(
        src_ref=src, dst_ref=dst, send_sem=send, recv_sem=recv, device_id=device, device_id_type=MESH
    )


def greet(devices):
    barrier = pltpu.get_barrier_semaphore()
    for device in devices:
        pl.semaphore_signal(barrier, inc=1, device_id=device, device_id_type=MESH)
    pl.semaphore_wait(barrier, len(devices))


class Place:
    def __init__(self):
        expert = lax.axis_index("expert")
        self.shard = lax.axis_index("shard")
        self.z, self.core = expert // 2, expert % 2
        self.number = self.z * 4 + self.shard
        self.sibling = (self.z * 2 + 1 - self.core, self.shard)

    def plane(self, step):
        return (self.z // 2 + step // 2) % 2 * 2 + (self.z + step) % 2

    def peer(self, number):
        return (number // 4 * 2 + self.core, number % 4)

    def peers(self):
        return [self.peer((self.number + d) % 16) for d in range(1, 16)]

    def mates(self):
        return [(self.z * 2 + self.core, (self.shard + d) % 4) for d in range(1, 4)]


class Quarters:
    def __init__(self, me, source, place, send, recv, local, pass_on):
        self.me, self.source, self.place = me, source, place
        self.sems = send, recv, local, pass_on

    def outgoing(self, act):
        me, (send, recv, local, _) = self.me, self.sems
        core = me.shard % 2
        for i in range(2):
            chip = 2 * me.core + i
            own = (core == me.core) & (chip == me.shard)

            @pl.when(jnp.logical_not(own))
            def _():
                act(
                    remote(
                        self.source.at[i], self.place(me.shard), send.at[i], recv.at[me.shard // 2],
                        (me.z * 2 + core, chip),
                    )
                )

            @pl.when(own)
            def _():
                act(pltpu.make_async_copy(self.source.at[i], self.place(me.shard), local))

    def start(self):
        self.outgoing(lambda cp: cp.start())

    def handed_on(self, q):
        pass_on = self.sems[3]
        return remote(self.place(q), self.place(q), pass_on.at[0, q // 2], pass_on.at[1, q // 2], self.me.sibling)

    def forward(self):
        me, (send, recv, local, _) = self.me, self.sems
        for n in range(2):
            q = 2 * n + me.core
            here = (me.shard // 2 == me.core) & (me.shard == q)

            @pl.when(jnp.logical_not(here))
            def _():
                remote(self.source.at[0], self.place(q), send.at[0], recv.at[n], me.sibling).wait_recv()

            @pl.when(here)
            def _():
                pltpu.make_async_copy(self.source.at[0], self.place(q), local).wait()

            self.handed_on(q).start()

    def finish(self):
        me, (send, recv, _, _) = self.me, self.sems
        core = me.shard % 2
        for i in range(2):
            chip = 2 * me.core + i

            @pl.when(jnp.logical_not((core == me.core) & (chip == me.shard)))
            def _():
                remote(self.source.at[i], self.place(me.shard), send.at[i], recv.at[0], me.sibling).wait_send()

        for n in range(2):
            self.handed_on(2 * n + me.core).wait_send()
            self.handed_on(2 * n + 1 - me.core).wait_recv()


def split3(rows):
    high = rows.astype(BF)
    rest = rows - high.astype(F32)
    low = rest.astype(BF)
    last = (rest - low.astype(F32)).astype(BF)
    return high, low, last


def three_rows(row):
    high, low, last = split3(row)
    index = lax.broadcasted_iota(jnp.int32, (8, row.shape[1]), 0)
    out = jnp.where(index == 0, high.astype(F32), 0.0)
    out = jnp.where(index == 1, low.astype(F32), out)
    return jnp.where(index == 2, last.astype(F32), out).astype(BF)


def norm_stats(values):
    center = values - jnp.mean(values, axis=-1, keepdims=True)
    inv = lax.rsqrt(jnp.mean(center * center, axis=-1, keepdims=True) + EPS_NORM)
    return center * inv, inv


def fill_hits(ranks, plane, hits, cap):
    slot = lax.broadcasted_iota(jnp.int32, (cap, hits.shape[1]), 0)
    for k in range(4):
        row = ranks[pl.ds(plane * 4 + k, 1), :]
        hits[k * cap : (k + 1) * cap, :] = jnp.where(slot == row, 1.0, 0.0).astype(BF)


def kernel_a(
    cap, tok, cot, rt, dsh, w1, w2,
    qkv_out, att_out, hid_out, lse, gate_t, ranks, aux, dense_out, xsend_out, gsend, cotr, wfull, wfull2, xfar,
    qkv, att, hid, dense, xsend, ssem, csend, low, hits, tri, dsem, dfsem, csem, wsem, wloc, wrecv, fsem, wsem2, wloc2, wrecv2, fsem2, osem, xsem,
):
    me = Place()
    z, c, s = me.z, me.core, me.shard
    rows = tok.shape[0]
    images = rows // SEQ_PAD
    other = [(z * 2 + 1 - c, t) for t in range(4)]
    greet(me.peers() + other)

    quarter = dsh.shape[0]
    half = quarter // 2
    dense_copies = []
    for d in range(1, 4):
        cp = remote(
            dsh.at[pl.ds(pl.multiple_of(c * half, half), half)],
            dense.at[pl.ds(pl.multiple_of(s * quarter + c * half, half), half)],
            dsem.at[0, d], dsem.at[1, d], (z * 2 + c, (s + d) % 4),
        )
        cp.start()
        dense_copies.append(cp)
    dense[pl.ds(pl.multiple_of(s * quarter, quarter), quarter), :] = dsh[...]

    expert_row = lax.broadcasted_iota(jnp.int32, (16, rows), 0)
    hit = (expert_row == rt[0:1, :]) | (expert_row == rt[1:2, :])
    earlier = lax.broadcasted_iota(jnp.int32, (rows, rows), 0) < lax.broadcasted_iota(jnp.int32, (rows, rows), 1)
    tri[...] = jnp.where(earlier, 1.0, 0.0).astype(BF)
    before = mm(jnp.where(hit, 1.0, 0.0).astype(BF), tri[...])
    ranks[...] = jnp.where(hit, before, -1.0).astype(jnp.int32)

    def cot_copy(p):
        return remote(
            csend.at[pl.ds(pl.multiple_of(p * cap, cap), cap)],
            cotr.at[pl.ds(pl.multiple_of(me.number * cap, cap), cap)],
            csem.at[0, p], csem.at[1, me.number], me.peer(p),
        )

    own = pl.multiple_of(me.number * cap, cap)
    own_copy = pltpu.make_async_copy(csend.at[pl.ds(own, cap)], cotr.at[pl.ds(own, cap)], osem)

    @pl.loop(0, 4)
    def _(step):
        plane = me.plane(3 - step)
        fill_hits(ranks, plane, hits, cap)
        csend[pl.ds(pl.multiple_of(plane * 4 * cap, 4 * cap), 4 * cap), :] = mm(hits[...], cot[...]).astype(BF)
        for k in range(4):
            p = plane * 4 + k

            @pl.when(p != me.number)
            def _():
                cot_copy(p).start()

            @pl.when(p == me.number)
            def _():
                own_copy.start()

    forwards = []
    for d in range(1, 4):
        dense_copies[d - 1].wait()
        source = (s - d + 4) % 4
        place = pl.ds(pl.multiple_of(source * quarter + c * half, half), half)
        cp = remote(dense.at[place], dense.at[place], dfsem.at[0, d], dfsem.at[1, d], me.sibling)
        cp.start()
        forwards.append(cp)

    in_quarters = Quarters(me, w1, lambda q: wfull.at[q], wsem, wrecv, wloc, fsem)
    out_quarters = Quarters(me, w2, lambda q: wfull2.at[q], wsem2, wrecv2, wloc2, fsem2)

    for cp in forwards:
        cp.wait()
    in_quarters.start()
    out_quarters.start()

    flat = jnp.transpose(dense[:, 3072:3200].astype(F32))
    aux[...] = flat[0:32, :]

    @pl.loop(0, images)
    def _(i):
        r = pl.ds(pl.multiple_of(i * SEQ_PAD, SEQ_PAD), SEQ_PAD)
        hat, _unused = norm_stats(tok[r, :].astype(F32))
        low[r, :] = (hat * aux[16:17, :]).astype(BF)

    @pl.loop(0, 3)
    def _(n):
        columns = pl.ds(pl.multiple_of(n * D, D), D)
        qkv[:, columns] = mm(low[...], dense[:, columns]).astype(BF)

    attention_forward(qkv, att, lse, images)

    wproj = dense.at[:, 2304:3072]
    @pl.loop(0, images)
    def _(i):
        r = pl.ds(pl.multiple_of(i * SEQ_PAD, SEQ_PAD), SEQ_PAD)
        hidden = tok[r, :].astype(F32) + mm(att[r, :], wproj[...])
        hid[r, :] = hidden
        hat, _unused = norm_stats(hidden)
        low[r, :] = (hat * aux[17:18, :]).astype(BF)

    logits = mm_nt(aux[0:16, :].astype(BF), low[...])
    masked = jnp.where(hit, logits, -1e30)
    weights = jnp.where(hit, jnp.exp(masked - jnp.max(masked, axis=0, keepdims=True)), 0.0)
    gate_t[...] = weights / jnp.maximum(jnp.sum(weights, axis=0, keepdims=True), 0.5)
    gsend[...] = jnp.zeros_like(gsend)

    far = me.plane(3)

    def far_copy(k):
        return remote(
            xsend.at[pl.ds(pl.multiple_of((far * 4 + k) * cap, cap), cap)],
            xfar.at[pl.ds(pl.multiple_of(s * cap, cap), cap)],
            xsem.at[0, k], xsem.at[1, s], me.peer(far * 4 + k),
        )

    @pl.loop(0, 4)
    def _(step):
        plane = me.plane(3 - step)
        fill_hits(ranks, plane, hits, cap)
        xsend[pl.ds(pl.multiple_of(plane * 4 * cap, 4 * cap), 4 * cap), :] = mm(hits[...], low[...]).astype(BF)

        @pl.when(step == 0)
        def _():
            for k in range(4):
                far_copy(k).start()

        for k in range(4):
            row = mm_nt(three_rows(gate_t[pl.ds(plane * 4 + k, 1), :]), hits[k * cap : (k + 1) * cap, :])
            gsend[plane * 4 + k, :, 0:cap] = jnp.broadcast_to(jnp.sum(row, axis=0, keepdims=True), (8, cap))

    saves = [
        pltpu.make_async_copy(held, place, ssem.at[n])
        for n, (held, place) in enumerate(
            ((qkv, qkv_out), (att, att_out), (hid, hid_out), (dense, dense_out), (xsend, xsend_out))
        )
    ]
    for cp in saves:
        cp.start()

    in_quarters.forward()
    out_quarters.forward()
    in_quarters.finish()
    out_quarters.finish()
    for d in range(1, 16):
        p = (me.number + d) % 16
        cot_copy(p).wait_send()
        remote(
            csend.at[pl.ds(0, cap)], cotr.at[pl.ds(0, cap)], csem.at[0, p], csem.at[1, p], me.peer(p)
        ).wait_recv()
    own_copy.wait()
    for k in range(4):
        far_copy(k).wait_send()
        remote(
            xsend.at[pl.ds(0, cap)], xfar.at[pl.ds(k * cap, cap)], xsem.at[0, k], xsem.at[1, k], me.peer(far * 4 + k)
        ).wait_recv()
    for cp in saves:
        cp.wait()


def attention_forward(qkv, att, lse, images):
    first = lax.broadcasted_iota(jnp.int32, (SEQ_PAD, 128), 1) < HEAD
    lane = lax.broadcasted_iota(jnp.int32, (SEQ_PAD, 128), 1)
    real = lax.broadcasted_iota(jnp.int32, (SEQ_PAD, SEQ_PAD), 1) < SEQ
    lse[...] = jnp.zeros_like(lse)

    @pl.loop(0, HEADS // 2)
    def _(pair):
        for i in range(images):
            r = slice(i * SEQ_PAD, (i + 1) * SEQ_PAD)
            cols = [pl.ds(pl.multiple_of(part * D + pair * 128, 128), 128) for part in range(3)]
            q, k, v = (qkv[r, cols[part]] for part in range(3))
            outs, lses = [], []
            for h in range(2):
                mine = first if h == 0 else jnp.logical_not(first)
                qh = (jnp.where(mine, q.astype(F32), 0.0) * 0.125).astype(BF)
                scores = jnp.where(real, mm_nt(qh, k), -1e30)
                top = jnp.max(scores, axis=1, keepdims=True)
                weights = jnp.exp(scores - top)
                total = jnp.sum(weights, axis=1, keepdims=True)
                lses.append(top + jnp.log(total))
                outs.append(mm((weights * (1.0 / total)).astype(BF), v))
            att[r, pl.ds(pl.multiple_of(pair * 128, 128), 128)] = jnp.where(first, outs[0], outs[1]).astype(BF)
            old = lse[r, :]
            lse[r, :] = jnp.where(lane == 2 * pair, lses[0], jnp.where(lane == 2 * pair + 1, lses[1], old))


def kernel_e(
    cap, xsend, gsend, cotr, wfull, wfull2, xfar,
    outs, ginh, ginb, ggb, gw, outn,
    w1v, w2v, xr, gcot, gater, act, gpre, acc, stage, ggs, gcol,
    xsem, gsem, rsem, ggsem, lsem, wlsem, stsem, nsem,
):
    me = Place()
    z, c, s = me.z, me.core, me.shard
    greet(me.peers())
    block = 4 * cap

    def part(ref, p):
        return ref.at[pl.ds(pl.multiple_of(p * cap, cap), cap)]

    def x_copy(p):
        return remote(part(xsend, p), part(xr, me.number), xsem.at[0, p], xsem.at[1, me.number], me.peer(p))

    def g_copy(p):
        return remote(gsend.at[p], gater.at[me.number], gsem.at[0, p], gsem.at[1, me.number], me.peer(p))

    def r_copy(p):
        return remote(part(ginh, p), part(ginb, me.number), rsem.at[0, p], rsem.at[1, me.number], me.peer(p))

    def n_copy(p):
        return remote(part(outs, p), part(outn, me.number), nsem.at[0, p], nsem.at[1, me.number], me.peer(p))

    def gg_copy(p):
        return remote(ggs.at[p], ggb.at[me.number], ggsem.at[0, p], ggsem.at[1, me.number], me.peer(p))

    local_copies = [
        pltpu.make_async_copy(part(xsend, me.number), part(xr, me.number), lsem.at[0]),
        pltpu.make_async_copy(gsend.at[me.number], gater.at[me.number], lsem.at[1]),
        pltpu.make_async_copy(cotr, gcot, lsem.at[2]),
    ]
    own_r = pltpu.make_async_copy(part(ginh, me.number), part(ginb, me.number), lsem.at[3])
    own_g = pltpu.make_async_copy(ggs.at[me.number], ggb.at[me.number], lsem.at[4])
    own_n = pltpu.make_async_copy(part(outs, me.number), part(outn, me.number), lsem.at[5])
    far = me.plane(3)
    far_rows = pl.ds(pl.multiple_of(far * block, block), block)
    w_copies = [
        pltpu.make_async_copy(wfull, w1v, wlsem.at[0]), pltpu.make_async_copy(xfar, xr.at[far_rows], wlsem.at[5])
    ] + [pltpu.make_async_copy(wfull2.at[f], w2v.at[pl.ds(f * D, D)], wlsem.at[1 + f]) for f in range(4)]
    for d in range(1, 16):
        g_copy((me.number + d) % 16).start()
    for cp in local_copies + w_copies:
        cp.start()
    for step in (2, 1, 0):
        for k in range(4):
            p = me.plane(step) * 4 + k

            @pl.when(p != me.number)
            def _():
                x_copy(p).start()

    ggs[...] = jnp.zeros_like(ggs)
    for cp in local_copies + w_copies:
        cp.wait()

    eye = lax.broadcasted_iota(jnp.int32, (cap, cap), 0) == lax.broadcasted_iota(jnp.int32, (cap, cap), 1)

    def recv_block(plane):
        for k in range(4):
            p = plane * 4 + k

            @pl.when(p != me.number)
            def _():
                @pl.when(plane != far)
                def _():
                    remote(part(xsend, p), part(xr, p), xsem.at[0, p], xsem.at[1, p], me.peer(p)).wait_recv()

                remote(gsend.at[p], gater.at[p], gsem.at[0, p], gsem.at[1, p], me.peer(p)).wait_recv()

    def stage_out(plane, which):
        return pltpu.make_async_copy(
            stage.at[which], (outs if which == 0 else ginh).at[pl.ds(pl.multiple_of(plane * block, block), block)],
            stsem.at[which],
        )

    def first_half(step):
        plane = me.plane(step)
        recv_block(plane)
        r = pl.ds(pl.multiple_of(plane * block, block), block)

        @pl.loop(0, 4)
        def _(f):
            for n in range(3):
                cols = pl.ds(pl.multiple_of(f * D + n * 256, 256), 256)
                pre = mm(xr[r, :], w1v[f, :, n * 256 : (n + 1) * 256])
                square = pre * pre
                t = jnp.tanh(pre * (GELU_A + GELU_A * GELU_B * square))
                half = 0.5 + 0.5 * t
                act[r, cols] = (pre * half).astype(BF)
                slope = half + (0.5 * pre) * (1.0 - t * t) * (GELU_A + 3.0 * GELU_A * GELU_B * square)
                gpre[r, cols] = slope.astype(BF)

    @pl.loop(0, 4)
    def _(turn):
        step = (turn + 3) % 4
        first_half(step)
        plane = me.plane(step)
        r = pl.ds(pl.multiple_of(plane * block, block), block)
        acc[...] = mm(act[r, :], w2v[...])

        for k in range(4):
            row = gater[plane * 4 + k, 0:1, 0:cap]
            column = jnp.sum(jnp.where(eye, row, 0.0), axis=1, keepdims=True)
            gcol[k * cap : (k + 1) * cap, :] = jnp.broadcast_to(column, (cap, 128))

        for k in range(4):
            rk = pl.ds(pl.multiple_of(plane * block + k * cap, cap), cap)
            kk = slice(k * cap, (k + 1) * cap)
            out = acc[kk, :].astype(BF).astype(F32)
            gate = gcol[kk, 0:1]
            g = gcot[rk, :].astype(F32)
            dots = jnp.sum(g * out, axis=1, keepdims=True)
            row = jnp.sum(jnp.where(eye, dots, 0.0), axis=0, keepdims=True)
            ggs[plane * 4 + k, :, 0:cap] = jnp.broadcast_to(row, (8, cap))
            stage[0, kk, :] = (gate * out).astype(BF)
            gcot[rk, :] = (gate * g).astype(BF)
        stage_out(plane, 0).start()

        @pl.loop(0, 4)
        def _(f):
            for n in range(3):
                cols = pl.ds(pl.multiple_of(f * D + n * 256, 256), 256)
                ga = mm_nt(gcot[r, :], w2v[cols, :])
                gpre[r, cols] = (ga * gpre[r, cols].astype(F32)).astype(BF)

        acc[...] = mm_nt(gpre[r, 0:D], w1v[0])
        for f in range(1, 4):
            acc[...] += mm_nt(gpre[r, f * D : (f + 1) * D], w1v[f])
        stage[1] = acc[...].astype(BF)
        stage_out(plane, 1).start()
        stage_out(plane, 1).wait()
        for k in range(4):
            p = plane * 4 + k

            @pl.when(p != me.number)
            def _():
                r_copy(p).start()
                gg_copy(p).start()

            @pl.when(p == me.number)
            def _():
                own_r.start()
                own_g.start()

        stage_out(plane, 0).wait()

        @pl.when(step < 2)
        def _():
            for k in range(4):
                p = plane * 4 + k

                @pl.when(p != me.number)
                def _():
                    n_copy(p).start()

                @pl.when(p == me.number)
                def _():
                    own_n.start()


    @pl.loop(0, 4)
    def _(f):
        cols = pl.ds(pl.multiple_of(f * D, D), D)
        w1v[f] = mm_tn(xr[...], gpre[:, cols]).astype(BF)
        w2v[cols, :] = mm_tn(act[:, cols], gcot[...]).astype(BF)

    out_w = [pltpu.make_async_copy(w1v, gw.at[0], wlsem.at[0])] + [
        pltpu.make_async_copy(w2v.at[pl.ds(f * D, D)], gw.at[1, f], wlsem.at[1 + f]) for f in range(4)
    ]
    for cp in out_w:
        cp.start()
    for d in range(1, 16):
        p = (me.number + d) % 16

        @pl.when(p // 4 != far)
        def _():
            x_copy(p).wait_send()

        g_copy(p).wait_send()
        r_copy(p).wait_send()
        gg_copy(p).wait_send()
        remote(part(ginh, p), part(ginb, p), rsem.at[0, p], rsem.at[1, p], me.peer(p)).wait_recv()
        remote(ggs.at[p], ggb.at[p], ggsem.at[0, p], ggsem.at[1, p], me.peer(p)).wait_recv()
    own_r.wait()
    own_g.wait()
    own_n.wait()
    for step in range(2):
        for k in range(4):
            p = me.plane(step) * 4 + k

            @pl.when(p != me.number)
            def _():
                n_copy(p).wait_send()
                remote(part(outs, p), part(outn, p), nsem.at[0, p], nsem.at[1, p], me.peer(p)).wait_recv()

    for cp in out_w:
        cp.wait()


def attention_backward(qkv, gatt, lse, gqkv, images, group):
    first = lax.broadcasted_iota(jnp.int32, (SEQ_PAD, 128), 1) < HEAD
    lane = lax.broadcasted_iota(jnp.int32, (SEQ_PAD, 128), 1)
    real = lax.broadcasted_iota(jnp.int32, (SEQ_PAD, SEQ_PAD), 1) < SEQ

    @pl.loop(0, 2)
    def _(near):
        pair = 2 * group + near
        for i in range(images):
            r = slice(i * SEQ_PAD, (i + 1) * SEQ_PAD)
            cols = [pl.ds(pl.multiple_of(part * D + pair * 128, 128), 128) for part in range(3)]
            q, k, v = (qkv[r, cols[part]] for part in range(3))
            g = gatt[r, pl.ds(pl.multiple_of(pair * 128, 128), 128)]
            logs = lse[r, :]
            parts = []
            for h in range(2):
                mine = first if h == 0 else jnp.logical_not(first)
                qh = (jnp.where(mine, q.astype(F32), 0.0) * 0.125).astype(BF)
                gh = jnp.where(mine, g.astype(F32), 0.0).astype(BF)
                log = jnp.sum(jnp.where(lane == 2 * pair + h, logs, 0.0), axis=1, keepdims=True)
                probs = jnp.where(real, jnp.exp(mm_nt(qh, k) - log), 0.0)
                grad_probs = mm_nt(gh, v)
                low = probs.astype(BF)
                delta = jnp.sum(probs * grad_probs, axis=1, keepdims=True)
                grad_scores = (probs * (grad_probs - delta)).astype(BF)
                parts.append((mm(grad_scores, k) * 0.125, mm_tn(grad_scores, q) * 0.125, mm_tn(low, g)))
            for part in range(3):
                place = pl.ds(pl.multiple_of(group * D + part * 256 + near * 128, 128), 128)
                gqkv[r, place] = jnp.where(first, parts[0][part], parts[1][part]).astype(BF)


def kernel_b(
    cap, tok, cot, aux, lse, gate_t, ranks, ggb, dense_in, qkv_in, att_in, hid_in, ginb, outs, gw, outn,
    block_out, gtok, ghat, extra, outb, eg,
    dense, qkv, att, hid, hsem, rowsv, hits, gmoe, low, glow, gatt, gqkv, gd, ra, rb, sc, rc, exs, exl, gx, own_w, ggt,
    osem, lsem, wxsem, wsem, wload, wlocal, asem, bsem, zsem, fsem, esem, xsem,
):
    me = Place()
    z, c, s = me.z, me.core, me.shard
    rows = tok.shape[0]
    images = rows // SEQ_PAD
    block = 4 * cap
    quarter, wide, deep = D // 4, D // 2, D // 16
    greet(me.peers() + [(z * 2 + 1 - c, t) for t in range(4)])

    def part(ref, p):
        return ref.at[pl.ds(pl.multiple_of(p * cap, cap), cap)]

    def o_copy(p):
        return remote(part(outs, p), part(outb, me.number), osem.at[0, p], osem.at[1, me.number], me.peer(p))

    load_in = pltpu.make_async_copy(ginb, rowsv, lsem.at[0])
    load_in.start()
    held = [
        pltpu.make_async_copy(place, ref, hsem.at[n])
        for n, (place, ref) in enumerate(((hid_in, hid), (att_in, att), (dense_in, dense), (qkv_in, qkv)))
    ]
    swap = [remote(gw.at[1 - c, t], gx.at[t], wxsem.at[0, t], wxsem.at[1, t], me.sibling) for t in range(4)]
    for cp in swap:
        cp.start()

    def send_outs(step):
        for k in range(4):
            o_copy(me.plane(step) * 4 + k).start()

    send_outs(3)
    send_outs(2)
    for cp in held:
        cp.start()

    load_in.wait()
    gmoe[...] = jnp.zeros_like(gmoe)

    @pl.loop(0, 4)
    def _(plane):
        fill_hits(ranks, plane, hits, cap)
        for k in range(4):
            rows8 = three_rows(ggb[plane * 4 + k, 0:1, 0:cap])
            row = mm(rows8, hits[k * cap : (k + 1) * cap, :])
            ggt[pl.ds(plane * 4 + k, 1), :] = jnp.sum(row, axis=0, keepdims=True)
        r = pl.ds(pl.multiple_of(plane * block, block), block)
        gmoe[...] += mm_tn(hits[...], rowsv[r, :])

    for cp in held:
        cp.wait()
    gates = gate_t[...]
    grad_gates = ggt[...]
    grad_logits = gates * (grad_gates - jnp.sum(gates * grad_gates, axis=0, keepdims=True))
    gl_high = grad_logits.astype(BF)
    gl_low = (grad_logits - gl_high.astype(F32)).astype(BF)

    @pl.loop(0, images)
    def _(i):
        r = pl.ds(pl.multiple_of(i * SEQ_PAD, SEQ_PAD), SEQ_PAD)
        hat, _unused = norm_stats(hid[r, :])
        low[r, :] = (hat * aux[17:18, :]).astype(BF)

    router = aux[0:16, :].astype(BF)
    gmoe[...] += mm_tn(gl_high, router) + mm_tn(gl_low, router)
    exs[0, 0:16, :] = mm(gl_high, low[...]) + mm(gl_low, low[...])
    exs[0, 16:32, :] = jnp.zeros((16, D), F32)

    @pl.loop(0, images)
    def _(i):
        r = pl.ds(pl.multiple_of(i * SEQ_PAD, SEQ_PAD), SEQ_PAD)
        hat, inv = norm_stats(hid[r, :])
        w = gmoe[r, :]
        scaled = w * aux[17:18, :]
        back = inv * (
            scaled - jnp.mean(scaled, axis=-1, keepdims=True) - hat * jnp.mean(scaled * hat, axis=-1, keepdims=True)
        )
        grad = cot[r, :].astype(F32) + back
        gtok[r, :] = grad
        glow[r, :] = grad.astype(BF)
        exs[0, 17:18, :] += jnp.sum(w * hat, axis=0, keepdims=True)
        hat, _unused = norm_stats(tok[r, :].astype(F32))
        low[r, :] = (hat * aux[16:17, :]).astype(BF)

    def put(group, value):
        for t in range(4):
            for h in range(2):
                gd[group, t, h] = value[t * quarter : (t + 1) * quarter, h * wide : (h + 1) * wide].astype(BF)

    def stage_a(g):
        return [
            remote(gd.at[g, t, 1 - c], ra.at[g, t], asem.at[0, g, t], asem.at[1, g, t], me.sibling) for t in range(4)
        ]

    def stage_b(g):
        return [
            remote(
                gd.at[g, (s + d) % 4, c], rb.at[g, d], bsem.at[0, g, d], bsem.at[1, g, d], (z * 2 + c, (s + d) % 4)
            )
            for d in range(1, 4)
        ]

    def stage_c(g):
        return [
            remote(
                sc.at[g, pl.ds(pl.multiple_of((z + d) % 4 * deep, deep), deep)], rc.at[g, d],
                zsem.at[0, g, d], zsem.at[1, g, d], ((z + d) % 4 * 2 + c, s),
            )
            for d in range(1, 4)
        ]

    my_rows = pl.ds(pl.multiple_of(z * deep, deep), deep)

    def stage_d(g):
        return [
            remote(
                ghat.at[g, c, my_rows], ghat.at[g, c, my_rows],
                fsem.at[0, g, d], fsem.at[1, g, d], ((z + d) % 4 * 2 + c, s),
            )
            for d in range(1, 4)
        ]

    def stage_e(g):
        return [remote(ghat.at[g, c], ghat.at[g, c], esem.at[0, g], esem.at[1, g], me.sibling)]

    def start(copies):
        for cp in copies:
            cp.start()

    def finish(copies):
        for cp in copies:
            cp.wait()

    def to_b(g):
        finish(stage_a(g))
        for t in range(4):
            gd[g, t, c] = (gd[g, t, c].astype(F32) + ra[g, t].astype(F32)).astype(BF)
        start(stage_b(g))

    def to_c(g):
        finish(stage_b(g))
        sc[g] = (
            (gd[g, s, c].astype(F32) + rb[g, 1].astype(F32)) + (rb[g, 2].astype(F32) + rb[g, 3].astype(F32))
        ).astype(BF)
        start(stage_c(g))

    def to_d(g):
        finish(stage_c(g))
        ghat[g, c, my_rows, :] = (
            (sc[g, my_rows, :].astype(F32) + rc[g, 1].astype(F32)) + (rc[g, 2].astype(F32) + rc[g, 3].astype(F32))
        ).astype(BF)
        start(stage_d(g))

    def to_e(g):
        finish(stage_d(g))
        start(stage_e(g))

    put(3, mm_tn(att[...], glow[...]))
    start(stage_a(3))
    gatt[...] = mm_nt(glow[...], dense[:, 2304:3072]).astype(BF)

    def owner_copy(t):
        return remote(
            gx.at[t], eg.at[s % 2, c], wsem.at[0, t], wsem.at[1, s % 2 * 2 + c], (z * 2 + s // 2, t)
        )

    mine_local = s // 2 == c
    owner_local = pltpu.make_async_copy(gx.at[s], eg.at[s % 2, c], wlocal)
    def to_owner(t):
        load = pltpu.make_async_copy(gw.at[c, t], own_w, wload)
        load.start()
        load.wait()
        remote(gw.at[1 - c, t], gx.at[t], wxsem.at[0, t], wxsem.at[1, t], me.sibling).wait()
        gx[t] = (gx[t].astype(F32) + own_w[...].astype(F32)).astype(BF)

        @pl.when(jnp.logical_not(mine_local & (s == t)))
        def _():
            owner_copy(t).start()

        @pl.when(mine_local & (s == t))
        def _():
            owner_local.start()

    for d in (1, 2, 3, 0):
        to_owner((s + d) % 4)
    to_b(3)
    for g in range(3):
        attention_backward(qkv, gatt, lse, gqkv, images, g)
        put(g, mm_tn(low[...], gqkv[:, g * D : (g + 1) * D]))
        start(stage_a(g))
        partial = [
            mm_nt(gqkv[:, g * D + 256 * n : g * D + 256 * (n + 1)], dense[:, n * D + g * 256 : n * D + (g + 1) * 256])
            for n in range(3)
        ]
        if g == 0:
            gmoe[...] = (partial[0] + partial[1]) + partial[2]
        else:
            gmoe[...] += (partial[0] + partial[1]) + partial[2]
            to_b(g - 1)

    @pl.loop(0, images)
    def _(i):
        r = pl.ds(pl.multiple_of(i * SEQ_PAD, SEQ_PAD), SEQ_PAD)
        hat, inv = norm_stats(tok[r, :].astype(F32))
        w = gmoe[r, :]
        scaled = w * aux[16:17, :]
        gtok[r, :] += inv * (
            scaled - jnp.mean(scaled, axis=-1, keepdims=True) - hat * jnp.mean(scaled * hat, axis=-1, keepdims=True)
        )
        exs[0, 16:17, :] += jnp.sum(w * hat, axis=0, keepdims=True)

    def add_outputs(source, step):
        plane = me.plane(step)
        r = pl.ds(pl.multiple_of(plane * block, block), block)
        load = pltpu.make_async_copy(source.at[r], rowsv.at[r], lsem.at[0])
        load.start()
        fill_hits(ranks, plane, hits, cap)
        load.wait()
        gmoe[...] += mm_tn(hits[...], rowsv[r, :])

    to_b(2)
    x_first = remote(exs.at[0], exl.at[0], xsem.at[0, 0], xsem.at[1, 0], me.sibling)
    x_first.start()
    gmoe[...] = hid[...]
    add_outputs(outn, 0)
    add_outputs(outn, 1)
    to_c(3)
    x_first.wait()
    exs[1] = exs[0] + exl[0]
    exl[1 + s] = exs[1]
    x_second = [
        remote(exs.at[1], exl.at[1 + s], xsem.at[0, d], xsem.at[1, d], (z * 2 + c, (s + d) % 4)) for d in range(1, 4)
    ]
    start(x_second)
    to_c(0)
    to_c(1)
    to_c(2)
    finish(x_second)
    exs[2] = (exl[1] + exl[2]) + (exl[3] + exl[4])
    exl[5 + z] = exs[2]
    x_third = [
        remote(exs.at[2], exl.at[5 + z], xsem.at[0, 3 + d], xsem.at[1, 3 + d], ((z + d) % 4 * 2 + c, s))
        for d in range(1, 4)
    ]
    start(x_third)
    for g in (3, 0, 1, 2):
        to_d(g)
    finish(x_third)
    extra[...] = (exl[5] + exl[6]) + (exl[7] + exl[8])
    for g in (3, 0, 1, 2):
        to_e(g)

    for step in (2, 3):
        for k in range(4):
            p = me.plane(step) * 4 + k
            o_copy(p).wait_send()
            remote(part(outs, p), part(outb, p), osem.at[0, p], osem.at[1, p], me.peer(p)).wait_recv()
        add_outputs(outb, step)

    block_out[...] = gmoe[...].astype(BF)

    for t in range(4):
        @pl.when(jnp.logical_not(mine_local & (s == t)))
        def _():
            owner_copy(t).wait_send()

        @pl.when(mine_local & (s == t))
        def _():
            owner_local.wait()

    for i in range(2):
        for a in range(2):
            own = (a == c) & (s == 2 * c + i)

            @pl.when(jnp.logical_not(own))
            def _():
                remote(gx.at[0], eg.at[i, a], wsem.at[0, 0], wsem.at[1, i * 2 + a], me.sibling).wait_recv()

    for g in range(4):
        finish(stage_e(g))


def lane_sums(values, count):
    lane = lax.broadcasted_iota(jnp.int32, (1, count), 1)
    out = jnp.zeros((1, count), F32)
    for n, value in enumerate(values):
        out = jnp.where(lane == n, value, out)
    return out


def total(values):
    return jnp.sum(jnp.sum(values, axis=1, keepdims=True), axis=0, keepdims=True)


def set_columns(ref, columns):
    lane = lax.broadcasted_iota(jnp.int32, ref.shape, 1)
    out = jnp.zeros(ref.shape, F32)
    for n, column in enumerate(columns):
        out = jnp.where(lane == n, column, out)
    ref[...] = out


def pick(row, n):
    lane = lax.broadcasted_iota(jnp.int32, row.shape, 1)
    return jnp.sum(jnp.where(lane == n, row, 0.0), axis=1, keepdims=True)


def mean_square(square_sum, weight_sum, size):
    rms = jnp.sqrt(square_sum * (1.0 / size))
    return rms, -RATE * jnp.sqrt(weight_sum * (1.0 / size)) / jnp.maximum(CLIP, rms)


def kernel_s(
    eg, ghat, extra, w1, w2, dsh, gains, moments, rows3, row_router, v_gain,
    mine_new, v_new, rows3_new, row_router_new, moments_new, sums, sums_r,
    egv, tall, turned, stats, landed, stats_r, landed_r, dgrad,
    isem, xsem, rsem,
):
    me = Place()
    z, c, s = me.z, me.core, me.shard
    quarter = dsh.shape[0]
    load = pltpu.make_async_copy(eg, egv, isem)
    load.start()
    greet(me.mates())

    read_dense(ghat, dgrad)
    mine = jnp.zeros((32, quarter), F32)
    for t in range(4):
        mine = mine + jnp.where(s == t, extra[:, t * quarter : (t + 1) * quarter], 0.0)
    mine_new[...] = mine
    router = mine[0:16, :]
    gain = mine[16:18, :]
    v = DECAY * v_gain[...] + (1.0 - DECAY) * (gain * gain + EPS_SQUARE)
    v_new[...] = v
    raw_gain = gain * lax.rsqrt(v)
    gain_weight = gains[...].astype(F32)
    gain_square = jnp.sum(raw_gain * raw_gain, axis=1, keepdims=True)
    gain_size = jnp.sum(gain_weight * gain_weight, axis=1, keepdims=True)
    router_square = router * router
    router_row = DECAY * row_router[...] + (1.0 - DECAY) * (
        jnp.sum(router_square, axis=0, keepdims=True) * (1.0 / 16) + EPS_SQUARE
    )
    row_router_new[...] = router_row
    set_columns(
        stats_r,
        [
            jnp.sum(router_square, axis=1, keepdims=True) + quarter * EPS_SQUARE,
            jnp.sum(router_square * (1.0 / router_row), axis=1, keepdims=True),
        ],
    )
    router_weight = dsh[:, 4 * D : 4 * D + 16].astype(F32)
    qkv_square = dgrad[:, : 3 * D] * dgrad[:, : 3 * D]
    proj_square = dgrad[:, 3 * D :] * dgrad[:, 3 * D :]
    row_qkv = DECAY * rows3[:, 0:1] + (1.0 - DECAY) * (
        jnp.sum(qkv_square, axis=1, keepdims=True) * (1.0 / (3 * D)) + EPS_SQUARE
    )
    row_proj = DECAY * rows3[:, 1:2] + (1.0 - DECAY) * (
        jnp.sum(proj_square, axis=1, keepdims=True) * (1.0 / D) + EPS_SQUARE
    )
    rows3_new[...] = jnp.where(lax.broadcasted_iota(jnp.int32, rows3_new.shape, 1) == 0, row_qkv, row_proj)
    inv_qkv, inv_proj = 1.0 / row_qkv, 1.0 / row_proj
    for g in range(4):
        square, inv = (qkv_square[:, g * D : (g + 1) * D], inv_qkv) if g < 3 else (proj_square, inv_proj)
        stats[8 + g : 9 + g, :] = jnp.sum(square, axis=0, keepdims=True) + quarter * EPS_SQUARE
        stats[12 + g : 13 + g, :] = jnp.sum(square * inv, axis=0, keepdims=True)
    dense_weight = dsh[:, : 4 * D].astype(F32)
    sizes = [
        total(row_qkv), total(row_proj), total(router_row),
        total(dense_weight[:, : 3 * D] * dense_weight[:, : 3 * D]),
        total(dense_weight[:, 3 * D :] * dense_weight[:, 3 * D :]),
        total(router_weight * router_weight),
        gain_square[0:1], gain_square[1:2], gain_size[0:1], gain_size[1:2],
    ]

    tall[...] = jnp.zeros_like(tall)
    turned[...] = jnp.zeros_like(turned)
    turned[0:8, :] = moments[...]
    moment_columns = jnp.transpose(turned[...])
    load.wait()
    columns = []
    for i in range(2):
        grad = egv[i, 0].astype(F32)
        square = grad * grad
        col = DECAY * moments[2 + i : 3 + i, :] + (1.0 - DECAY) * (
            jnp.sum(square, axis=0, keepdims=True) * (1.0 / D) + EPS_SQUARE
        )
        moments_new[2 + i : 3 + i, :] = col
        columns.append(jnp.sum(square, axis=1, keepdims=True) + D * EPS_SQUARE)
        columns.append(jnp.sum(square * (1.0 / col), axis=1, keepdims=True))
        weight = w1[i].astype(F32)
        sizes.append(total(weight * weight))
    for i in range(2):
        grad = egv[i, 1].astype(F32)
        square = grad * grad
        row = DECAY * moment_columns[:, 4 + i : 5 + i] + (1.0 - DECAY) * (
            jnp.sum(square, axis=1, keepdims=True) * (1.0 / D) + EPS_SQUARE
        )
        columns.append(row)
        stats[4 + i : 5 + i, :] = jnp.sum(square, axis=0, keepdims=True) + D * EPS_SQUARE
        stats[6 + i : 7 + i, :] = jnp.sum(square * (1.0 / row), axis=0, keepdims=True)
        weight = w2[i].astype(F32)
        sizes.append(total(weight * weight))
        sizes.append(total(row))
    set_columns(tall, columns)
    flat = jnp.transpose(tall[...])
    for n, m in ((0, 0), (2, 1), (1, 2), (3, 3)):
        stats[m : m + 1, :] = flat[n : n + 1, :]
    moments_new[0:2, :] = flat[4:6, :]
    moments_new[4:8, :] = jnp.zeros((4, D), F32)
    stats[16:24, :] = jnp.zeros((8, D), F32)
    stats[16:17, :] = lane_sums(sizes, D)

    landed[s] = stats[...]
    landed_r[s] = stats_r[...]
    copies = []
    for d in range(1, 4):
        mate = (z * 2 + c, (s + d) % 4)
        copies.append(remote(stats, landed.at[s], xsem.at[0, d], xsem.at[1, d], mate))
        copies.append(remote(stats_r, landed_r.at[s], rsem.at[0, d], rsem.at[1, d], mate))
    for cp in copies:
        cp.start()
    for cp in copies:
        cp.wait()
    sums[...] = (landed[0] + landed[1]) + (landed[2] + landed[3])
    sums_r[...] = (landed_r[0] + landed_r[1]) + (landed_r[2] + landed_r[3])


def read_dense(ghat, dgrad):
    for g in range(4):
        for n in range(6):
            column = 3 * D + 128 * n if g == 3 else n // 2 * D + g * 256 + n % 2 * 128
            dgrad[:, column : column + 128] = ghat[g, n // 3, :, n % 3 * 128 : n % 3 * 128 + 128].astype(F32)


def kernel_u(
    eg, ghat, mine, w1, w2, dsh, gains, moments, moments_mid, rows3, row_router, cols, col_router, v, sums, sums_r,
    g_first, g_second, n_first, n_second, dense_rms, expert_rms, n_gain, g_qkv, n_qkv, g_proj, n_proj, n_router,
    cols_new, col_router_new, row_in_new, col_out_new,
    egv, grads, news, turned, tall_d, dgrad,
    isem, gsem, nsem,
):
    quarter = dsh.shape[0]
    load = pltpu.make_async_copy(eg, egv, isem)
    load.start()
    read_dense(ghat, dgrad)
    g_qkv[...] = dgrad[:, : 3 * D]
    g_proj[...] = dgrad[:, 3 * D :]
    router, gain = mine[0:16, :], mine[16:18, :]
    raw_gain = gain * lax.rsqrt(v[...])
    gain_weight = gains[...].astype(F32)
    router_row = row_router[...]
    router_weight = dsh[:, 4 * D : 4 * D + 16].astype(F32)
    row_qkv, row_proj = rows3[:, 0:1], rows3[:, 1:2]
    scalars = sums[16:17, :]
    one = lambda n: pick(scalars, n)
    load.wait()

    hidden = 4.0 * D
    row_in = DECAY * moments[0:2, :] + (1.0 - DECAY) * (sums[0:2, :] * (1.0 / hidden))
    row_in_new[...] = row_in
    col_out = DECAY * moments[6:8, :] + (1.0 - DECAY) * (sums[4:6, :] * (1.0 / hidden))
    col_out_new[...] = col_out
    turned[...] = jnp.zeros_like(turned)
    turned[0:2, :] = row_in
    turned[2:4, :] = moments_mid[0:2, :]
    back = jnp.transpose(turned[...])
    rms_all = []
    for i in range(2):
        r = row_in[i : i + 1, :]
        mean = jnp.sum(r, axis=1, keepdims=True) * (1.0 / D)
        raw = mean * jnp.sum(sums[2 + i : 3 + i, :] / r, axis=1, keepdims=True)
        rms, factor = mean_square(raw, one(10 + i), D * hidden)
        rms_all.append(rms)
        left = factor * lax.rsqrt(back[:, i : i + 1] / mean)
        grads[i] = egv[i, 0].astype(F32)
        pltpu.make_async_copy(grads.at[i], g_first.at[i], gsem.at[i]).start()
        news[i] = w1[i].astype(F32) + grads[i] * left * lax.rsqrt(moments_mid[2 + i : 3 + i, :])
        pltpu.make_async_copy(news.at[i], n_first.at[i], nsem.at[i]).start()
    for i in range(2):
        col = col_out[i : i + 1, :]
        mean = one(13 + 2 * i) * (1.0 / hidden)
        raw = mean * jnp.sum(sums[6 + i : 7 + i, :] / col, axis=1, keepdims=True)
        rms, factor = mean_square(raw, one(12 + 2 * i), D * hidden)
        rms_all.append(rms)
        left = factor * lax.rsqrt(back[:, 2 + i : 3 + i] / mean)
        grads[2 + i] = egv[i, 1].astype(F32)
        pltpu.make_async_copy(grads.at[2 + i], g_second.at[i], gsem.at[2 + i]).start()
        news[2 + i] = w2[i].astype(F32) + grads[2 + i] * left * lax.rsqrt(col)
        pltpu.make_async_copy(news.at[2 + i], n_second.at[i], nsem.at[2 + i]).start()
    expert_rms[...] = lane_sums(rms_all, 128)

    rms_g1, factor_g1 = mean_square(one(6), one(8), D)
    rms_g2, factor_g2 = mean_square(one(7), one(9), D)
    upper = lax.broadcasted_iota(jnp.int32, gain.shape, 0) == 0
    n_gain[...] = gain_weight + jnp.where(upper, factor_g1, factor_g2) * raw_gain
    col_dense = []
    for g in range(4):
        col = DECAY * cols[g : g + 1, :] + (1.0 - DECAY) * (sums[8 + g : 9 + g, :] * (1.0 / D))
        cols_new[g : g + 1, :] = col
        col_dense.append(col)
    mean_qkv, mean_proj, mean_router = one(0) * (1.0 / D), one(1) * (1.0 / D), one(2) * (1.0 / D)
    ratio = [jnp.sum(sums[12 + g : 13 + g, :] / col_dense[g], axis=1, keepdims=True) for g in range(4)]
    rms_qkv, factor_qkv = mean_square(mean_qkv * (ratio[0] + ratio[1] + ratio[2]), one(3), 3 * D * D)
    rms_proj, factor_proj = mean_square(mean_proj * ratio[3], one(4), D * D)
    left_qkv = factor_qkv * lax.rsqrt(row_qkv / mean_qkv)
    left_proj = factor_proj * lax.rsqrt(row_proj / mean_proj)
    for g in range(4):
        part = slice(g * D, (g + 1) * D)
        new = dsh[:, part].astype(F32) + dgrad[:, part] * (left_qkv if g < 3 else left_proj) * lax.rsqrt(col_dense[g])
        if g < 3:
            n_qkv[:, part] = new
        else:
            n_proj[...] = new
    col = DECAY * col_router[...] + (1.0 - DECAY) * (sums_r[:, 0:1] * (1.0 / D))
    col_router_new[...] = col
    raw_router = mean_router * jnp.sum(sums_r[:, 1:2] / col, axis=0, keepdims=True)
    rms_router, factor_router = mean_square(raw_router, one(5), 16 * D)
    tall_d[...] = jnp.zeros_like(tall_d)
    tall_d[0:16, 0:quarter] = router * (factor_router * lax.rsqrt(router_row / mean_router)) * lax.rsqrt(col)
    n_router[...] = router_weight + jnp.transpose(tall_d[...])[0:quarter, 0:16]
    dense_rms[...] = lane_sums([rms_g1, rms_g2, rms_qkv, rms_proj, rms_router], 128)
    for i in range(2):
        pltpu.make_async_copy(news.at[i], n_first.at[i], nsem.at[i]).wait()
        pltpu.make_async_copy(news.at[2 + i], n_second.at[i], nsem.at[2 + i]).wait()
        pltpu.make_async_copy(grads.at[i], g_first.at[i], gsem.at[i]).wait()
        pltpu.make_async_copy(grads.at[2 + i], g_second.at[i], gsem.at[2 + i]).wait()


def params(number):
    return pltpu.CompilerParams(collective_id=number, has_side_effects=True, vmem_limit_bytes=VMEM_LIMIT)


def dma(*shape):
    return pltpu.SemaphoreType.DMA(shape)


def fast(
    tokens, routes, cotangent, gain_attn, w_qkv, w_proj, gain_moe, w_router, w_in, w_out,
    v_attn, v_moe, row_qkv, col_qkv, row_proj, col_proj, row_router, col_router, row_in, col_in, row_out, col_out,
):
    count = tokens.shape[0]
    images = count // SEQ
    rows = images * SEQ_PAD
    experts = w_router.shape[1]
    cap = ((3 * count + experts - 1) // experts + 15) // 16 * 16
    slots = experts * cap
    vmem = pl.BlockSpec(memory_space=pltpu.VMEM)
    hbm = pl.BlockSpec(memory_space=pl.ANY)
    shape = jax.ShapeDtypeStruct

    def padded(array, value=0):
        array = array.reshape(images, SEQ, array.shape[1])
        array = jnp.pad(array, ((0, 0), (0, SEQ_PAD - SEQ), (0, 0)), constant_values=value)
        return array.reshape(rows, array.shape[2])

    tok = padded(tokens)
    cot = padded(cotangent)
    rt = padded(routes, -1).T
    quarter = w_qkv.shape[0]
    small = jnp.concatenate([w_router, gain_attn[:, None], gain_moe[:, None]], axis=1)
    small = jnp.pad(small, ((0, 0), (0, 128 - small.shape[1])))
    dsh = jnp.concatenate([w_qkv, w_proj, small], axis=1)
    wide = dsh.shape[1]

    qkv, att, hid, lse, gate_t, ranks, aux, dense, xsend, gsend, cotr, wfull, wfull2, xfar = pl.pallas_call(
        functools.partial(kernel_a, cap),
        out_shape=(
            shape((rows, 3 * D), BF), shape((rows, D), BF), shape((rows, D), F32), shape((rows, 128), F32),
            shape((16, rows), F32), shape((16, rows), jnp.int32), shape((32, D), F32), shape((D, wide), BF),
            shape((slots, D), BF), shape((16, 8, 256), F32), shape((slots, D), BF), shape((4, D, D), BF),
            shape((4, D, D), BF), shape((4 * cap, D), BF),
        ),
        in_specs=[vmem] * 4 + [hbm] * 2,
        out_specs=(hbm,) * 3 + (vmem,) * 4 + (hbm,) * 2 + (vmem,) + (hbm,) * 4,
        scratch_shapes=[
            pltpu.VMEM((rows, 3 * D), BF), pltpu.VMEM((rows, D), BF), pltpu.VMEM((rows, D), F32),
            pltpu.VMEM((D, wide), BF), pltpu.VMEM((slots, D), BF), dma(5),
            pltpu.VMEM((slots, D), BF), pltpu.VMEM((rows, D), BF), pltpu.VMEM((4 * cap, rows), BF),
            pltpu.VMEM((rows, rows), BF), dma(2, 4), dma(2, 4), dma(2, 16), dma(2), dma(), dma(2), dma(2, 2),
            dma(2), dma(), dma(2), dma(2, 2), dma(), dma(2, 4),
        ],
        compiler_params=params(1),
        name="forward",
    )(tok, cot, rt, dsh, w_in, w_out)

    outs, ginh, ginb, ggb, gw, outn = pl.pallas_call(
        functools.partial(kernel_e, cap),
        out_shape=(
            shape((slots, D), BF), shape((slots, D), BF), shape((slots, D), BF), shape((16, 8, 256), F32),
            shape((2, 4, D, D), BF), shape((slots, D), BF),
        ),
        in_specs=[hbm, vmem, hbm, hbm, hbm, hbm],
        out_specs=(hbm, hbm, hbm, vmem, hbm, hbm),
        scratch_shapes=[
            pltpu.VMEM((4, D, D), BF), pltpu.VMEM((FF, D), BF), pltpu.VMEM((slots, D), BF), pltpu.VMEM((slots, D), BF),
            pltpu.VMEM((16, 8, 256), F32), pltpu.VMEM((slots, FF), BF), pltpu.VMEM((slots, FF), BF),
            pltpu.VMEM((4 * cap, D), F32), pltpu.VMEM((2, 4 * cap, D), BF),
            pltpu.VMEM((16, 8, 256), F32), pltpu.VMEM((4 * cap, 128), F32),
            dma(2, 16), dma(2, 16), dma(2, 16), dma(2, 16), dma(6), dma(6), dma(2), dma(2, 16),
        ],
        compiler_params=params(2),
        name="experts",
    )(xsend, gsend, cotr, wfull, wfull2, xfar)

    block_out, gtok, ghat, extra, outb, eg = pl.pallas_call(
        functools.partial(kernel_b, cap),
        out_shape=(
            shape((rows, D), BF), shape((rows, D), F32), shape((4, 2, quarter, D // 2), BF), shape((32, D), F32),
            shape((slots, D), BF), shape((2, 2, D, D), BF),
        ),
        in_specs=[vmem] * 7 + [hbm] * 8,
        out_specs=(vmem,) * 4 + (hbm,) * 2,
        scratch_shapes=[
            pltpu.VMEM((D, wide), BF), pltpu.VMEM((rows, 3 * D), BF), pltpu.VMEM((rows, D), BF),
            pltpu.VMEM((rows, D), F32), dma(4), pltpu.VMEM((slots, D), BF), pltpu.VMEM((4 * cap, rows), BF), pltpu.VMEM((rows, D), F32),
            pltpu.VMEM((rows, D), BF), pltpu.VMEM((rows, D), BF), pltpu.VMEM((rows, D), BF),
            pltpu.VMEM((rows, 3 * D), BF), pltpu.VMEM((4, 4, 2, quarter, D // 2), BF),
            pltpu.VMEM((4, 4, quarter, D // 2), BF), pltpu.VMEM((4, 4, quarter, D // 2), BF),
            pltpu.VMEM((4, quarter, D // 2), BF), pltpu.VMEM((4, 4, quarter // 4, D // 2), BF),
            pltpu.VMEM((3, 32, D), F32), pltpu.VMEM((9, 32, D), F32), pltpu.VMEM((4, D, D), BF),
            pltpu.VMEM((D, D), BF), pltpu.VMEM((16, rows), F32),
            dma(2, 16), dma(2), dma(2, 4), dma(2, 4), dma(), dma(), dma(2, 4, 4), dma(2, 4, 4), dma(2, 4, 4),
            dma(2, 4, 4), dma(2, 4), dma(2, 7),
        ],
        compiler_params=params(3),
        name="backward",
    )(tok, cot, aux, lse, gate_t, ranks, ggb, dense, qkv, att, hid, ginb, outs, gw, outn)

    def unpadded(array):
        return array.reshape(images, SEQ_PAD, D)[:, :SEQ].reshape(count, D)

    gains = jnp.stack([gain_attn, gain_moe])
    moments = jnp.concatenate([row_in, col_in, row_out, col_out])
    mine, v_new, rows_new, row_router_new, moments_mid, sums, sums_r = pl.pallas_call(
        kernel_s,
        out_shape=(
            shape((32, quarter), F32), shape((2, quarter), F32), shape((quarter, 2), F32), shape((1, quarter), F32),
            shape((8, D), F32), shape((24, D), F32), shape((16, 128), F32),
        ),
        in_specs=[hbm] + [vmem] * 10,
        out_specs=(vmem,) * 7,
        scratch_shapes=[
            pltpu.VMEM((2, 2, D, D), BF), pltpu.VMEM((D, 128), F32), pltpu.VMEM((128, D), F32),
            pltpu.VMEM((24, D), F32), pltpu.VMEM((4, 24, D), F32), pltpu.VMEM((16, 128), F32),
            pltpu.VMEM((4, 16, 128), F32), pltpu.VMEM((quarter, 4 * D), F32), dma(), dma(2, 4), dma(2, 4),
        ],
        compiler_params=params(4),
        name="update_sums",
    )(
        eg, ghat, extra, w_in, w_out, dsh, gains, moments, jnp.stack([row_qkv, row_proj], axis=1), row_router[None],
        jnp.stack([v_attn, v_moe]),
    )
    (
        g_first, g_second, n_first, n_second, dense_rms, expert_rms, n_gain, g_qkv, n_qkv, g_proj, n_proj, n_router,
        cols_new, col_router_new, row_in_new, col_out_new,
    ) = pl.pallas_call(
        kernel_u,
        out_shape=(
            shape((2, D, D), F32), shape((2, D, D), F32), shape((2, D, D), F32), shape((2, D, D), F32),
            shape((1, 128), F32), shape((1, 128), F32), shape((2, quarter), F32),
            shape((quarter, 3 * D), F32), shape((quarter, 3 * D), F32),
            shape((quarter, D), F32), shape((quarter, D), F32), shape((quarter, 16), F32),
            shape((4, D), F32), shape((16, 1), F32), shape((2, D), F32), shape((2, D), F32),
        ),
        in_specs=[hbm] + [vmem] * 15,
        out_specs=(hbm,) * 4 + (vmem,) * 12,
        scratch_shapes=[
            pltpu.VMEM((2, 2, D, D), BF), pltpu.VMEM((4, D, D), F32), pltpu.VMEM((4, D, D), F32),
            pltpu.VMEM((128, D), F32), pltpu.VMEM((128, 256), F32), pltpu.VMEM((quarter, 4 * D), F32),
            dma(), dma(4), dma(4),
        ],
        compiler_params=pltpu.CompilerParams(vmem_limit_bytes=VMEM_LIMIT),
        name="update",
    )(
        eg, ghat, mine, w_in, w_out, dsh, gains, moments, moments_mid, rows_new, row_router_new,
        jnp.concatenate([col_qkv, col_proj]).reshape(4, D), col_router[:, None], v_new, sums, sums_r,
    )
    return (
        unpadded(block_out), unpadded(gtok), dense_rms[0, :5], expert_rms[0, :4].reshape(2, 2).T,
        mine[16], n_gain[0], v_new[0], mine[17], n_gain[1], v_new[1],
        g_qkv, n_qkv, rows_new[:, 0], cols_new[:3].reshape(3 * D),
        g_proj, n_proj, rows_new[:, 1], cols_new[3],
        mine[:16].T, n_router, row_router_new[0], col_router_new[:, 0],
        g_first, n_first, row_in_new, moments_mid[2:4],
        g_second, n_second, moments_mid[0:2], col_out_new,
    )


def local(
    tokens, routes, cotangent, gain_attn, w_qkv, w_proj, gain_moe, w_router, w_in, w_out,
    v_attn, v_moe, row_qkv, col_qkv, row_proj, col_proj, row_router, col_router, row_in, col_in, row_out, col_out,
):
    if (
        lax.axis_size("shard") == 4
        and lax.axis_size("expert") == 8
        and w_in.shape == w_out.shape == (2, D, D)
        and tokens.shape[0] % SEQ == 0
    ):
        return fast(
            tokens, routes, cotangent, gain_attn, w_qkv, w_proj, gain_moe, w_router, w_in, w_out,
            v_attn, v_moe, row_qkv, col_qkv, row_proj, col_proj, row_router, col_router, row_in, col_in, row_out, col_out,
        )
    block_out, grad_tokens, dense_parts, expert_parts = general(
        tokens, routes, cotangent, gain_attn, w_qkv, w_proj, gain_moe, w_router, w_in, w_out
    )
    part_g1, part_qkv, part_proj, part_g2, part_router = dense_parts
    grad_first, grad_second = expert_parts
    expert_count = part_router.shape[1]
    weight_g1 = gain_attn.astype(jnp.float32)
    weight_g2 = gain_moe.astype(jnp.float32)
    dense = (
        (part_qkv, w_qkv.astype(jnp.float32), row_qkv, col_qkv),
        (part_proj, w_proj.astype(jnp.float32), row_proj, col_proj),
        (part_router, w_router.astype(jnp.float32), row_router, col_router),
    )
    weight_first = w_in.astype(jnp.float32)
    weight_second = w_out.astype(jnp.float32)
    v_attn_new = DECAY * v_attn + (1.0 - DECAY) * (part_g1 * part_g1 + EPS_SQUARE)
    v_moe_new = DECAY * v_moe + (1.0 - DECAY) * (part_g2 * part_g2 + EPS_SQUARE)
    raw_g1 = part_g1 * lax.rsqrt(v_attn_new)
    raw_g2 = part_g2 * lax.rsqrt(v_moe_new)
    dense_rows, dense_sums = [], []
    for grad, weight, row, col in dense:
        square = grad * grad
        row_new = DECAY * row + (1.0 - DECAY) * jnp.mean(square + EPS_SQUARE, axis=1)
        dense_rows.append(row_new)
        dense_sums.append(
            (
                jnp.sum(square + EPS_SQUARE, axis=0),
                jnp.sum(square / row_new[:, None], axis=0),
                jnp.stack([jnp.sum(row_new), jnp.sum(weight * weight)]),
            )
        )
    square_first = grad_first * grad_first
    square_second = grad_second * grad_second
    col_in_new = DECAY * col_in + (1.0 - DECAY) * jnp.mean(square_first + EPS_SQUARE, axis=1)
    row_out_new = DECAY * row_out + (1.0 - DECAY) * jnp.mean(square_second + EPS_SQUARE, axis=2)
    gain_sums = jnp.stack(
        [
            jnp.sum(raw_g1 * raw_g1),
            jnp.sum(raw_g2 * raw_g2),
            jnp.sum(weight_g1 * weight_g1),
            jnp.sum(weight_g2 * weight_g2),
        ]
    )
    expert_sums = (
        jnp.sum(square_first + EPS_SQUARE, axis=2),
        jnp.sum(square_first / col_in_new[:, None, :], axis=2),
        jnp.sum(square_second + EPS_SQUARE, axis=1),
        jnp.sum(square_second / row_out_new[:, :, None], axis=1),
        jnp.stack(
            [
                jnp.sum(weight_first * weight_first, axis=(1, 2)),
                jnp.sum(row_out_new, axis=1),
                jnp.sum(weight_second * weight_second, axis=(1, 2)),
            ]
        ),
    )
    expert_sums = lax.psum(expert_sums, "shard")
    dense_sums, gain_sums = lax.psum((dense_sums, gain_sums), "shard")

    def step(square_sum, weight_sum, size):
        rms = jnp.sqrt(square_sum / size)
        return rms, -RATE * jnp.sqrt(weight_sum / size) / jnp.maximum(CLIP, rms)

    rms_g1, factor_g1 = step(gain_sums[0], gain_sums[2], D)
    rms_g2, factor_g2 = step(gain_sums[1], gain_sums[3], D)
    new_g1 = weight_g1 + factor_g1 * raw_g1
    new_g2 = weight_g2 + factor_g2 * raw_g2
    dense_new, dense_cols, dense_rms = [], [], [rms_g1, rms_g2]
    for (grad, weight, _, col), row_new, (col_sum, ratio_sum, both) in zip(dense, dense_rows, dense_sums):
        col_new = DECAY * col + (1.0 - DECAY) * (col_sum / D)
        row_mean = both[0] / D
        rms, factor = step(row_mean * jnp.sum(ratio_sum / col_new), both[1], grad.shape[1] * D)
        raw = grad * lax.rsqrt(row_new[:, None] * col_new[None, :] / row_mean)
        dense_new.append(weight + factor * raw)
        dense_cols.append(col_new)
        dense_rms.append(rms)
    new_qkv, new_proj, new_router = dense_new
    row_qkv_new, row_proj_new, row_router_new = dense_rows
    col_qkv_new, col_proj_new, col_router_new = dense_cols
    row_in_sum, ratio_in, col_out_sum, ratio_out, expert_scalars = expert_sums
    row_in_new = DECAY * row_in + (1.0 - DECAY) * (row_in_sum / FF)
    col_out_new = DECAY * col_out + (1.0 - DECAY) * (col_out_sum / FF)
    mean_in = jnp.mean(row_in_new, axis=1)
    mean_out = expert_scalars[1] / FF
    rms_first, factor_first = step(mean_in * jnp.sum(ratio_in / row_in_new, axis=1), expert_scalars[0], D * FF)
    rms_second, factor_second = step(mean_out * jnp.sum(ratio_out / col_out_new, axis=1), expert_scalars[2], D * FF)
    new_first = weight_first + factor_first[:, None, None] * grad_first * lax.rsqrt(
        row_in_new[:, :, None] * col_in_new[:, None, :] / mean_in[:, None, None]
    )
    new_second = weight_second + factor_second[:, None, None] * grad_second * lax.rsqrt(
        row_out_new[:, :, None] * col_out_new[:, None, :] / mean_out[:, None, None]
    )
    return (
        block_out,
        grad_tokens,
        jnp.stack(dense_rms),
        jnp.stack([rms_first, rms_second], axis=1),
        part_g1,
        new_g1,
        v_attn_new,
        part_g2,
        new_g2,
        v_moe_new,
        part_qkv,
        new_qkv,
        row_qkv_new,
        col_qkv_new,
        part_proj,
        new_proj,
        row_proj_new,
        col_proj_new,
        part_router,
        new_router,
        row_router_new,
        col_router_new,
        grad_first,
        new_first,
        row_in_new,
        col_in_new,
        grad_second,
        new_second,
        row_out_new,
        col_out_new,
    )


def solution(mesh):
    return jax.shard_map(
        local,
        mesh=mesh,
        in_specs=(
            P(("expert", "shard"), None),
            P(("expert", "shard"), None),
            P(("expert", "shard"), None),
            P("shard"),
            P("shard", None),
            P("shard", None),
            P("shard"),
            P("shard", None),
            P("expert", None, "shard"),
            P("expert", "shard", None),
            P("shard"),
            P("shard"),
            P("shard"),
            P(),
            P("shard"),
            P(),
            P("shard"),
            P(),
            P("expert", None),
            P("expert", "shard"),
            P("expert", "shard"),
            P("expert", None),
        ),
        out_specs=(
            P(("expert", "shard"), None),
            P(("expert", "shard"), None),
            P(),
            P("expert", None),
            P("shard"),
            P("shard"),
            P("shard"),
            P("shard"),
            P("shard"),
            P("shard"),
            P("shard", None),
            P("shard", None),
            P("shard"),
            P(),
            P("shard", None),
            P("shard", None),
            P("shard"),
            P(),
            P("shard", None),
            P("shard", None),
            P("shard"),
            P(),
            P("expert", None, "shard"),
            P("expert", None, "shard"),
            P("expert", None),
            P("expert", "shard"),
            P("expert", "shard", None),
            P("expert", "shard", None),
            P("expert", "shard"),
            P("expert", None),
        ),
        check_vma=False,
    )
```

```python
import functools

import jax
import jax.numpy as jnp
from jax import lax
from jax.experimental import pallas as pl
from jax.experimental.pallas import tpu as pltpu
from jax.sharding import PartitionSpec as P

D = 768
HEADS = 12
HEAD = 64
FF = 3072
SEQ = 197


PRECISE = lax.Precision.HIGHEST
EPS_NORM = 1e-06
EPS_SQUARE = 1e-30
RATE = 0.3
DECAY = 0.5
CLIP = 0.05


GELU_A = 0.7978845608028654
GELU_B = 0.044715


def normalize(values):
    center = values - jnp.mean(values, axis=-1, keepdims=True)
    inv_root = lax.rsqrt(jnp.mean(center * center, axis=-1, keepdims=True) + EPS_NORM)
    return (center * inv_root, inv_root)


def norm_back(grad, normed, inv_root, gain):
    scaled = grad * gain
    grad_in = inv_root * (
        scaled
        - jnp.mean(scaled, axis=-1, keepdims=True)
        - normed * jnp.mean(scaled * normed, axis=-1, keepdims=True)
    )
    return (grad_in, jnp.sum(grad * normed, axis=0))


def gelu_tanh(values):
    return jax.nn.gelu(values, approximate=True)


def general(
    tokens,
    routes,
    cotangent,
    gain_attn,
    w_qkv,
    w_proj,
    gain_moe,
    w_router,
    w_in,
    w_out,
):
    gain_first, qkv_full, proj_full, gain_second, router_full = (
        lax.all_gather(gain_attn, "shard", axis=0, tiled=True),
        lax.all_gather(w_qkv, "shard", axis=0, tiled=True),
        lax.all_gather(w_proj, "shard", axis=0, tiled=True),
        lax.all_gather(gain_moe, "shard", axis=0, tiled=True),
        lax.all_gather(w_router, "shard", axis=0, tiled=True),
    )
    first_full, second_full = (
        lax.all_gather(w_in, "shard", axis=2, tiled=True),
        lax.all_gather(w_out, "shard", axis=1, tiled=True),
    )
    row_count = tokens.shape[0]
    image_count = row_count // SEQ
    expert_count = router_full.shape[1]
    per_device = w_in.shape[0]
    axis_count = lax.axis_size("expert")
    capacity = ((3 * row_count + expert_count - 1) // expert_count + 7) // 8 * 8
    score_scale = HEAD ** (-0.5)
    tok_float = tokens.astype(jnp.float32)
    gain_one = gain_first.astype(jnp.float32)
    gain_two = gain_second.astype(jnp.float32)
    attn_hat, attn_inv = normalize(tok_float)
    attn_low = (attn_hat * gain_one).astype(jnp.bfloat16)
    qkv_low = jnp.dot(attn_low, qkv_full, preferred_element_type=jnp.float32).astype(jnp.bfloat16)
    qkv_split = qkv_low.reshape(image_count, SEQ, 3, HEADS, HEAD)
    query_part = qkv_split[:, :, 0]
    key_part = qkv_split[:, :, 1]
    value_part = qkv_split[:, :, 2]
    scores = (
        jnp.einsum("ishd,ithd->ihst", query_part, key_part, preferred_element_type=jnp.float32)
        * score_scale
    )
    log_total = jax.nn.logsumexp(scores, axis=-1, keepdims=True)
    soft_low = jnp.exp(scores - log_total).astype(jnp.bfloat16)
    attended = (
        jnp.einsum("ihst,ithd->ishd", soft_low, value_part, preferred_element_type=jnp.float32)
        .reshape(row_count, D)
        .astype(jnp.bfloat16)
    )
    hidden = tok_float + jnp.dot(attended, proj_full, preferred_element_type=jnp.float32)
    moe_hat, moe_inv = normalize(hidden)
    moe_low = (moe_hat * gain_two).astype(jnp.bfloat16)
    logits = jnp.dot(moe_low, router_full, preferred_element_type=jnp.float32)
    labels = jnp.arange(expert_count, dtype=jnp.int32)
    route_hits = (routes[:, :, None] == labels[None, None, :]).astype(jnp.float32)
    chosen = jnp.sum(route_hits * logits[:, None, :], axis=2)
    gates = jax.nn.softmax(chosen, axis=-1)
    flat_routes = routes.reshape(-1)
    earlier = (jnp.arange(row_count)[:, None] > jnp.arange(row_count)[None, :]).astype(jnp.bfloat16)
    before = jnp.dot(
        earlier, jnp.sum(route_hits, axis=1).astype(jnp.bfloat16), preferred_element_type=jnp.float32
    )
    slot_rank = jnp.sum(route_hits * before[:, None, :], axis=2).astype(jnp.int32).reshape(-1)
    slot_dest = flat_routes * capacity + slot_rank
    pair_index = jnp.arange(2 * row_count, dtype=jnp.int32)
    slot_pair = (
        jnp.full((expert_count * capacity,), 2 * row_count, jnp.int32).at[slot_dest].set(pair_index)
    )
    slot_token = slot_pair // 2
    zero_row = jnp.zeros((1, D), jnp.bfloat16)
    send_rows = jnp.concatenate([moe_low, zero_row], axis=0)[slot_token].reshape(
        axis_count, per_device, capacity, D
    )
    received = lax.all_to_all(send_rows, "expert", split_axis=0, concat_axis=0, tiled=True)
    pre_gelu = jnp.einsum(
        "sekd,edf->sekf", received, first_full, preferred_element_type=jnp.float32
    )
    activated = gelu_tanh(pre_gelu).astype(jnp.bfloat16)
    expert_out = jnp.einsum(
        "sekf,efd->sekd", activated, second_full, preferred_element_type=jnp.float32
    ).astype(jnp.bfloat16)
    back_rows = lax.all_to_all(expert_out, "expert", split_axis=0, concat_axis=0, tiled=True)
    back_rows, received, pre_gelu, activated = (back_rows, received, pre_gelu, activated)
    picked = (
        back_rows.reshape(expert_count * capacity, D)[slot_dest]
        .reshape(row_count, 2, D)
        .astype(jnp.float32)
    )
    block_out = (hidden + jnp.sum(gates[:, :, None] * picked, axis=1)).astype(jnp.bfloat16)
    grad_out = cotangent.astype(jnp.float32)
    grad_picked = (gates[:, :, None] * grad_out[:, None, :]).astype(jnp.bfloat16)
    grad_gates = jnp.sum(grad_out[:, None, :] * picked, axis=2)
    grad_chosen = gates * (grad_gates - jnp.sum(gates * grad_gates, axis=1, keepdims=True))
    grad_logits = jnp.sum(route_hits * grad_chosen[:, :, None], axis=1)
    grad_send = jnp.concatenate([grad_picked.reshape(2 * row_count, D), zero_row], axis=0)[
        slot_pair
    ].reshape(axis_count, per_device, capacity, D)
    grad_recv = lax.all_to_all(grad_send, "expert", split_axis=0, concat_axis=0, tiled=True)
    grad_act = jnp.einsum(
        "sekd,efd->sekf", grad_recv, second_full, preferred_element_type=jnp.float32
    )
    unused, gelu_pull = jax.vjp(gelu_tanh, pre_gelu)
    grad_pre = gelu_pull(grad_act)[0].astype(jnp.bfloat16)
    grad_rows = jnp.einsum(
        "sekf,edf->sekd", grad_pre, first_full, preferred_element_type=jnp.float32
    ).astype(jnp.bfloat16)
    grad_back = lax.all_to_all(grad_rows, "expert", split_axis=0, concat_axis=0, tiled=True)
    grad_first = jnp.einsum(
        "sekd,sekf->edf", received, grad_pre, preferred_element_type=jnp.float32
    )
    grad_second = jnp.einsum(
        "sekf,sekd->efd", activated, grad_recv, preferred_element_type=jnp.float32
    )
    grad_first, grad_second = (
        lax.psum_scatter(grad_first, "shard", scatter_dimension=2, tiled=True),
        lax.psum_scatter(grad_second, "shard", scatter_dimension=1, tiled=True),
    )
    returned = (
        grad_back.reshape(expert_count * capacity, D)[slot_dest]
        .reshape(row_count, 2, D)
        .astype(jnp.float32)
    )
    router_float = router_full.astype(jnp.float32)
    grad_moe = jnp.sum(returned, axis=1) + jnp.einsum(
        "te,de->td", grad_logits, router_float, precision=PRECISE
    )
    grad_router = jnp.einsum(
        "td,te->de", moe_low.astype(jnp.float32), grad_logits, precision=PRECISE
    )
    grad_from_moe, grad_g2 = norm_back(grad_moe, moe_hat, moe_inv, gain_two)
    grad_hidden = grad_out + grad_from_moe
    grad_low = grad_hidden.astype(jnp.bfloat16)
    grad_proj = jnp.einsum("tc,td->cd", attended, grad_low, preferred_element_type=jnp.float32)
    grad_att = (
        jnp.einsum("td,cd->tc", grad_low, proj_full, preferred_element_type=jnp.float32)
        .astype(jnp.bfloat16)
        .reshape(image_count, SEQ, HEADS, HEAD)
    )
    scores_again = (
        jnp.einsum("ishd,ithd->ihst", query_part, key_part, preferred_element_type=jnp.float32)
        * score_scale
    )
    soft_again = jnp.exp(scores_again - log_total)
    soft_again_low = soft_again.astype(jnp.bfloat16)
    grad_soft = jnp.einsum(
        "ishd,ithd->ihst", grad_att, value_part, preferred_element_type=jnp.float32
    )
    grad_value = jnp.einsum(
        "ihst,ishd->ithd", soft_again_low, grad_att, preferred_element_type=jnp.float32
    )
    row_delta = jnp.sum(soft_again * grad_soft, axis=-1, keepdims=True)
    grad_scores = (soft_again * (grad_soft - row_delta)).astype(jnp.bfloat16)
    grad_query = (
        jnp.einsum("ihst,ithd->ishd", grad_scores, key_part, preferred_element_type=jnp.float32)
        * score_scale
    )
    grad_key = (
        jnp.einsum("ihst,ishd->ithd", grad_scores, query_part, preferred_element_type=jnp.float32)
        * score_scale
    )
    grad_qkv_low = (
        jnp.stack([grad_query, grad_key, grad_value], axis=2)
        .reshape(row_count, 3 * D)
        .astype(jnp.bfloat16)
    )
    grad_qkv = jnp.einsum("tc,td->cd", attn_low, grad_qkv_low, preferred_element_type=jnp.float32)
    grad_attn_in = jnp.einsum(
        "td,cd->tc", grad_qkv_low, qkv_full, preferred_element_type=jnp.float32
    )
    grad_from_attn, grad_g1 = norm_back(grad_attn_in, attn_hat, attn_inv, gain_one)
    grad_tokens = grad_hidden + grad_from_attn
    dense_grads = (grad_g1, grad_qkv, grad_proj, grad_g2, grad_router)
    dense_total = lax.psum(
        (dense_grads[0], dense_grads[1], dense_grads[2], dense_grads[3], dense_grads[4]), "expert"
    )
    dense_parts = (
        lax.psum_scatter(dense_total[0], "shard", scatter_dimension=0, tiled=True),
        lax.psum_scatter(dense_total[1], "shard", scatter_dimension=0, tiled=True),
        lax.psum_scatter(dense_total[2], "shard", scatter_dimension=0, tiled=True),
        lax.psum_scatter(dense_total[3], "shard", scatter_dimension=0, tiled=True),
        lax.psum_scatter(dense_total[4], "shard", scatter_dimension=0, tiled=True),
    )
    return block_out, grad_tokens, dense_parts, (grad_first, grad_second)


SEQ_PAD = 224
MESH = pl.DeviceIdType.MESH
VMEM_LIMIT = 62 * 1024 * 1024
BF = jnp.bfloat16
F32 = jnp.float32


def mm(a, b):
    return lax.dot_general(a, b, (((1,), (0,)), ((), ())), preferred_element_type=F32)


def mm_nt(a, b):
    return lax.dot_general(a, b, (((1,), (1,)), ((), ())), preferred_element_type=F32)


def mm_tn(a, b):
    return lax.dot_general(a, b, (((0,), (0,)), ((), ())), preferred_element_type=F32)


def remote(src, dst, send, recv, device):
    return pltpu.make_async_remote_copy(
        src_ref=src, dst_ref=dst, send_sem=send, recv_sem=recv, device_id=device, device_id_type=MESH
    )


def greet(devices):
    barrier = pltpu.get_barrier_semaphore()
    for device in devices:
        pl.semaphore_signal(barrier, inc=1, device_id=device, device_id_type=MESH)
    pl.semaphore_wait(barrier, len(devices))


class Place:
    def __init__(self):
        expert = lax.axis_index("expert")
        self.shard = lax.axis_index("shard")
        self.z, self.core = expert // 2, expert % 2
        self.number = self.z * 4 + self.shard
        self.sibling = (self.z * 2 + 1 - self.core, self.shard)

    def plane(self, step):
        return (self.z // 2 + step // 2) % 2 * 2 + (self.z + step) % 2

    def peer(self, number):
        return (number // 4 * 2 + self.core, number % 4)

    def peers(self):
        return [self.peer((self.number + d) % 16) for d in range(1, 16)]

    def mates(self):
        return [(self.z * 2 + self.core, (self.shard + d) % 4) for d in range(1, 4)]


class Quarters:
    def __init__(self, me, source, place, send, recv, local, pass_on):
        self.me, self.source, self.place = me, source, place
        self.sems = send, recv, local, pass_on

    def outgoing(self, act):
        me, (send, recv, local, _) = self.me, self.sems
        core = me.shard % 2
        for i in range(2):
            chip = 2 * me.core + i
            own = (core == me.core) & (chip == me.shard)

            @pl.when(jnp.logical_not(own))
            def _():
                act(
                    remote(
                        self.source.at[i], self.place(me.shard), send.at[i], recv.at[me.shard // 2],
                        (me.z * 2 + core, chip),
                    )
                )

            @pl.when(own)
            def _():
                act(pltpu.make_async_copy(self.source.at[i], self.place(me.shard), local))

    def start(self):
        self.outgoing(lambda cp: cp.start())

    def handed_on(self, q):
        pass_on = self.sems[3]
        return remote(self.place(q), self.place(q), pass_on.at[0, q // 2], pass_on.at[1, q // 2], self.me.sibling)

    def forward(self):
        me, (send, recv, local, _) = self.me, self.sems
        for n in range(2):
            q = 2 * n + me.core
            here = (me.shard // 2 == me.core) & (me.shard == q)

            @pl.when(jnp.logical_not(here))
            def _():
                remote(self.source.at[0], self.place(q), send.at[0], recv.at[n], me.sibling).wait_recv()

            @pl.when(here)
            def _():
                pltpu.make_async_copy(self.source.at[0], self.place(q), local).wait()

            self.handed_on(q).start()

    def finish(self):
        me, (send, recv, _, _) = self.me, self.sems
        core = me.shard % 2
        for i in range(2):
            chip = 2 * me.core + i

            @pl.when(jnp.logical_not((core == me.core) & (chip == me.shard)))
            def _():
                remote(self.source.at[i], self.place(me.shard), send.at[i], recv.at[0], me.sibling).wait_send()

        for n in range(2):
            self.handed_on(2 * n + me.core).wait_send()
            self.handed_on(2 * n + 1 - me.core).wait_recv()


def split3(rows):
    high = rows.astype(BF)
    rest = rows - high.astype(F32)
    low = rest.astype(BF)
    last = (rest - low.astype(F32)).astype(BF)
    return high, low, last


def three_rows(row):
    high, low, last = split3(row)
    index = lax.broadcasted_iota(jnp.int32, (8, row.shape[1]), 0)
    out = jnp.where(index == 0, high.astype(F32), 0.0)
    out = jnp.where(index == 1, low.astype(F32), out)
    return jnp.where(index == 2, last.astype(F32), out).astype(BF)


def norm_stats(values):
    center = values - jnp.mean(values, axis=-1, keepdims=True)
    inv = lax.rsqrt(jnp.mean(center * center, axis=-1, keepdims=True) + EPS_NORM)
    return center * inv, inv


def fill_hits(ranks, plane, hits, cap):
    slot = lax.broadcasted_iota(jnp.int32, (cap, hits.shape[1]), 0)
    for k in range(4):
        row = ranks[pl.ds(plane * 4 + k, 1), :]
        hits[k * cap : (k + 1) * cap, :] = jnp.where(slot == row, 1.0, 0.0).astype(BF)


def kernel_a(
    cap, tok, cot, rt, dsh, w1, w2,
    qkv_out, att_out, hid_out, lse, gate_t, ranks, aux, dense_out, xsend_out, gsend, cotr, wfull, wfull2, xfar,
    qkv, att, hid, dense, xsend, ssem, csend, low, hits, tri, dsem, dfsem, csem, wsem, wloc, wrecv, fsem, wsem2, wloc2, wrecv2, fsem2, osem, xsem,
):
    me = Place()
    z, c, s = me.z, me.core, me.shard
    rows = tok.shape[0]
    images = rows // SEQ_PAD
    other = [(z * 2 + 1 - c, t) for t in range(4)]
    greet(me.peers() + other)

    quarter = dsh.shape[0]
    half = quarter // 2
    dense_copies = []
    for d in range(1, 4):
        cp = remote(
            dsh.at[pl.ds(pl.multiple_of(c * half, half), half)],
            dense.at[pl.ds(pl.multiple_of(s * quarter + c * half, half), half)],
            dsem.at[0, d], dsem.at[1, d], (z * 2 + c, (s + d) % 4),
        )
        cp.start()
        dense_copies.append(cp)
    dense[pl.ds(pl.multiple_of(s * quarter, quarter), quarter), :] = dsh[...]

    expert_row = lax.broadcasted_iota(jnp.int32, (16, rows), 0)
    hit = (expert_row == rt[0:1, :]) | (expert_row == rt[1:2, :])
    earlier = lax.broadcasted_iota(jnp.int32, (rows, rows), 0) < lax.broadcasted_iota(jnp.int32, (rows, rows), 1)
    tri[...] = jnp.where(earlier, 1.0, 0.0).astype(BF)
    before = mm(jnp.where(hit, 1.0, 0.0).astype(BF), tri[...])
    ranks[...] = jnp.where(hit, before, -1.0).astype(jnp.int32)

    def cot_copy(p):
        return remote(
            csend.at[pl.ds(pl.multiple_of(p * cap, cap), cap)],
            cotr.at[pl.ds(pl.multiple_of(me.number * cap, cap), cap)],
            csem.at[0, p], csem.at[1, me.number], me.peer(p),
        )

    own = pl.multiple_of(me.number * cap, cap)
    own_copy = pltpu.make_async_copy(csend.at[pl.ds(own, cap)], cotr.at[pl.ds(own, cap)], osem)

    @pl.loop(0, 4)
    def _(step):
        plane = me.plane(3 - step)
        fill_hits(ranks, plane, hits, cap)
        csend[pl.ds(pl.multiple_of(plane * 4 * cap, 4 * cap), 4 * cap), :] = mm(hits[...], cot[...]).astype(BF)
        for k in range(4):
            p = plane * 4 + k

            @pl.when(p != me.number)
            def _():
                cot_copy(p).start()

            @pl.when(p == me.number)
            def _():
                own_copy.start()

    forwards = []
    for d in range(1, 4):
        dense_copies[d - 1].wait()
        source = (s - d + 4) % 4
        place = pl.ds(pl.multiple_of(source * quarter + c * half, half), half)
        cp = remote(dense.at[place], dense.at[place], dfsem.at[0, d], dfsem.at[1, d], me.sibling)
        cp.start()
        forwards.append(cp)

    in_quarters = Quarters(me, w1, lambda q: wfull.at[q], wsem, wrecv, wloc, fsem)
    out_quarters = Quarters(me, w2, lambda q: wfull2.at[q], wsem2, wrecv2, wloc2, fsem2)

    for cp in forwards:
        cp.wait()
    in_quarters.start()
    out_quarters.start()

    flat = jnp.transpose(dense[:, 3072:3200].astype(F32))
    aux[...] = flat[0:32, :]

    @pl.loop(0, images)
    def _(i):
        r = pl.ds(pl.multiple_of(i * SEQ_PAD, SEQ_PAD), SEQ_PAD)
        hat, _unused = norm_stats(tok[r, :].astype(F32))
        low[r, :] = (hat * aux[16:17, :]).astype(BF)

    @pl.loop(0, 3)
    def _(n):
        columns = pl.ds(pl.multiple_of(n * D, D), D)
        qkv[:, columns] = mm(low[...], dense[:, columns]).astype(BF)

    attention_forward(qkv, att, lse, images)

    wproj = dense.at[:, 2304:3072]
    @pl.loop(0, images)
    def _(i):
        r = pl.ds(pl.multiple_of(i * SEQ_PAD, SEQ_PAD), SEQ_PAD)
        hidden = tok[r, :].astype(F32) + mm(att[r, :], wproj[...])
        hid[r, :] = hidden
        hat, _unused = norm_stats(hidden)
        low[r, :] = (hat * aux[17:18, :]).astype(BF)

    logits = mm_nt(aux[0:16, :].astype(BF), low[...])
    masked = jnp.where(hit, logits, -1e30)
    weights = jnp.where(hit, jnp.exp(masked - jnp.max(masked, axis=0, keepdims=True)), 0.0)
    gate_t[...] = weights / jnp.maximum(jnp.sum(weights, axis=0, keepdims=True), 0.5)
    gsend[...] = jnp.zeros_like(gsend)

    far = me.plane(3)

    def far_copy(k):
        return remote(
            xsend.at[pl.ds(pl.multiple_of((far * 4 + k) * cap, cap), cap)],
            xfar.at[pl.ds(pl.multiple_of(s * cap, cap), cap)],
            xsem.at[0, k], xsem.at[1, s], me.peer(far * 4 + k),
        )

    @pl.loop(0, 4)
    def _(step):
        plane = me.plane(3 - step)
        fill_hits(ranks, plane, hits, cap)
        xsend[pl.ds(pl.multiple_of(plane * 4 * cap, 4 * cap), 4 * cap), :] = mm(hits[...], low[...]).astype(BF)

        @pl.when(step == 0)
        def _():
            for k in range(4):
                far_copy(k).start()

        for k in range(4):
            row = mm_nt(three_rows(gate_t[pl.ds(plane * 4 + k, 1), :]), hits[k * cap : (k + 1) * cap, :])
            gsend[plane * 4 + k, :, 0:cap] = jnp.broadcast_to(jnp.sum(row, axis=0, keepdims=True), (8, cap))

    saves = [
        pltpu.make_async_copy(held, place, ssem.at[n])
        for n, (held, place) in enumerate(
            ((qkv, qkv_out), (att, att_out), (hid, hid_out), (dense, dense_out), (xsend, xsend_out))
        )
    ]
    for cp in saves:
        cp.start()

    in_quarters.forward()
    out_quarters.forward()
    in_quarters.finish()
    out_quarters.finish()
    for d in range(1, 16):
        p = (me.number + d) % 16
        cot_copy(p).wait_send()
        remote(
            csend.at[pl.ds(0, cap)], cotr.at[pl.ds(0, cap)], csem.at[0, p], csem.at[1, p], me.peer(p)
        ).wait_recv()
    own_copy.wait()
    for k in range(4):
        far_copy(k).wait_send()
        remote(
            xsend.at[pl.ds(0, cap)], xfar.at[pl.ds(k * cap, cap)], xsem.at[0, k], xsem.at[1, k], me.peer(far * 4 + k)
        ).wait_recv()
    for cp in saves:
        cp.wait()


def attention_forward(qkv, att, lse, images):
    first = lax.broadcasted_iota(jnp.int32, (SEQ_PAD, 128), 1) < HEAD
    lane = lax.broadcasted_iota(jnp.int32, (SEQ_PAD, 128), 1)
    real = lax.broadcasted_iota(jnp.int32, (SEQ_PAD, SEQ_PAD), 1) < SEQ
    lse[...] = jnp.zeros_like(lse)

    @pl.loop(0, HEADS // 2)
    def _(pair):
        for i in range(images):
            r = slice(i * SEQ_PAD, (i + 1) * SEQ_PAD)
            cols = [pl.ds(pl.multiple_of(part * D + pair * 128, 128), 128) for part in range(3)]
            q, k, v = (qkv[r, cols[part]] for part in range(3))
            outs, lses = [], []
            for h in range(2):
                mine = first if h == 0 else jnp.logical_not(first)
                qh = (jnp.where(mine, q.astype(F32), 0.0) * 0.125).astype(BF)
                scores = jnp.where(real, mm_nt(qh, k), -1e30)
                top = jnp.max(scores, axis=1, keepdims=True)
                weights = jnp.exp(scores - top)
                total = jnp.sum(weights, axis=1, keepdims=True)
                lses.append(top + jnp.log(total))
                outs.append(mm((weights * (1.0 / total)).astype(BF), v))
            att[r, pl.ds(pl.multiple_of(pair * 128, 128), 128)] = jnp.where(first, outs[0], outs[1]).astype(BF)
            old = lse[r, :]
            lse[r, :] = jnp.where(lane == 2 * pair, lses[0], jnp.where(lane == 2 * pair + 1, lses[1], old))


def kernel_e(
    cap, xsend, gsend, cotr, wfull, wfull2, xfar,
    outs, ginh, ginb, ggb, gw, outn,
    w1v, w2v, xr, gcot, gater, act, gpre, acc, stage, ggs, gcol,
    xsem, gsem, rsem, ggsem, lsem, wlsem, stsem, nsem,
):
    me = Place()
    z, c, s = me.z, me.core, me.shard
    greet(me.peers())
    block = 4 * cap

    def part(ref, p):
        return ref.at[pl.ds(pl.multiple_of(p * cap, cap), cap)]

    def x_copy(p):
        return remote(part(xsend, p), part(xr, me.number), xsem.at[0, p], xsem.at[1, me.number], me.peer(p))

    def g_copy(p):
        return remote(gsend.at[p], gater.at[me.number], gsem.at[0, p], gsem.at[1, me.number], me.peer(p))

    def r_copy(p):
        return remote(part(ginh, p), part(ginb, me.number), rsem.at[0, p], rsem.at[1, me.number], me.peer(p))

    def n_copy(p):
        return remote(part(outs, p), part(outn, me.number), nsem.at[0, p], nsem.at[1, me.number], me.peer(p))

    def gg_copy(p):
        return remote(ggs.at[p], ggb.at[me.number], ggsem.at[0, p], ggsem.at[1, me.number], me.peer(p))

    local_copies = [
        pltpu.make_async_copy(part(xsend, me.number), part(xr, me.number), lsem.at[0]),
        pltpu.make_async_copy(gsend.at[me.number], gater.at[me.number], lsem.at[1]),
        pltpu.make_async_copy(cotr, gcot, lsem.at[2]),
    ]
    own_r = pltpu.make_async_copy(part(ginh, me.number), part(ginb, me.number), lsem.at[3])
    own_g = pltpu.make_async_copy(ggs.at[me.number], ggb.at[me.number], lsem.at[4])
    own_n = pltpu.make_async_copy(part(outs, me.number), part(outn, me.number), lsem.at[5])
    far = me.plane(3)
    far_rows = pl.ds(pl.multiple_of(far * block, block), block)
    w_copies = [
        pltpu.make_async_copy(wfull, w1v, wlsem.at[0]), pltpu.make_async_copy(xfar, xr.at[far_rows], wlsem.at[5])
    ] + [pltpu.make_async_copy(wfull2.at[f], w2v.at[pl.ds(f * D, D)], wlsem.at[1 + f]) for f in range(4)]
    for d in range(1, 16):
        g_copy((me.number + d) % 16).start()
    for cp in local_copies + w_copies:
        cp.start()
    for step in (2, 1, 0):
        for k in range(4):
            p = me.plane(step) * 4 + k

            @pl.when(p != me.number)
            def _():
                x_copy(p).start()

    ggs[...] = jnp.zeros_like(ggs)
    for cp in local_copies + w_copies:
        cp.wait()

    eye = lax.broadcasted_iota(jnp.int32, (cap, cap), 0) == lax.broadcasted_iota(jnp.int32, (cap, cap), 1)

    def recv_block(plane):
        for k in range(4):
            p = plane * 4 + k

            @pl.when(p != me.number)
            def _():
                @pl.when(plane != far)
                def _():
                    remote(part(xsend, p), part(xr, p), xsem.at[0, p], xsem.at[1, p], me.peer(p)).wait_recv()

                remote(gsend.at[p], gater.at[p], gsem.at[0, p], gsem.at[1, p], me.peer(p)).wait_recv()

    def stage_out(plane, which):
        return pltpu.make_async_copy(
            stage.at[which], (outs if which == 0 else ginh).at[pl.ds(pl.multiple_of(plane * block, block), block)],
            stsem.at[which],
        )

    def first_half(step):
        plane = me.plane(step)
        recv_block(plane)
        r = pl.ds(pl.multiple_of(plane * block, block), block)

        @pl.loop(0, 4)
        def _(f):
            for n in range(3):
                cols = pl.ds(pl.multiple_of(f * D + n * 256, 256), 256)
                pre = mm(xr[r, :], w1v[f, :, n * 256 : (n + 1) * 256])
                square = pre * pre
                t = jnp.tanh(pre * (GELU_A + GELU_A * GELU_B * square))
                half = 0.5 + 0.5 * t
                act[r, cols] = (pre * half).astype(BF)
                slope = half + (0.5 * pre) * (1.0 - t * t) * (GELU_A + 3.0 * GELU_A * GELU_B * square)
                gpre[r, cols] = slope.astype(BF)

    def give_back(plane):
        for k in range(4):
            p = plane * 4 + k

            @pl.when(p != me.number)
            def _():
                r_copy(p).start()
                gg_copy(p).start()

            @pl.when(p == me.number)
            def _():
                own_r.start()
                own_g.start()

    @pl.loop(0, 4)
    def _(turn):
        step = (turn + 3) % 4
        first_half(step)
        plane = me.plane(step)
        r = pl.ds(pl.multiple_of(plane * block, block), block)
        acc[...] = mm(act[r, :], w2v[...])

        for k in range(4):
            row = gater[plane * 4 + k, 0:1, 0:cap]
            column = jnp.sum(jnp.where(eye, row, 0.0), axis=1, keepdims=True)
            gcol[k * cap : (k + 1) * cap, :] = jnp.broadcast_to(column, (cap, 128))

        for k in range(4):
            rk = pl.ds(pl.multiple_of(plane * block + k * cap, cap), cap)
            kk = slice(k * cap, (k + 1) * cap)
            out = acc[kk, :].astype(BF).astype(F32)
            gate = gcol[kk, 0:1]
            g = gcot[rk, :].astype(F32)
            dots = jnp.sum(g * out, axis=1, keepdims=True)
            row = jnp.sum(jnp.where(eye, dots, 0.0), axis=0, keepdims=True)
            ggs[plane * 4 + k, :, 0:cap] = jnp.broadcast_to(row, (8, cap))
            stage[0, kk, :] = (gate * out).astype(BF)
            gcot[rk, :] = (gate * g).astype(BF)
        stage_out(plane, 0).start()

        @pl.loop(0, 4)
        def _(f):
            for n in range(3):
                cols = pl.ds(pl.multiple_of(f * D + n * 256, 256), 256)
                ga = mm_nt(gcot[r, :], w2v[cols, :])
                gpre[r, cols] = (ga * gpre[r, cols].astype(F32)).astype(BF)

        acc[...] = mm_nt(gpre[r, 0:D], w1v[0])
        for f in range(1, 4):
            acc[...] += mm_nt(gpre[r, f * D : (f + 1) * D], w1v[f])
        stage[1] = acc[...].astype(BF)
        stage_out(plane, 1).start()
        stage_out(plane, 1).wait()
        give_back(plane)

        stage_out(plane, 0).wait()

        @pl.when(step < 2)
        def _():
            for k in range(4):
                p = plane * 4 + k

                @pl.when(p != me.number)
                def _():
                    n_copy(p).start()

                @pl.when(p == me.number)
                def _():
                    own_n.start()


    @pl.loop(0, 4)
    def _(f):
        cols = pl.ds(pl.multiple_of(f * D, D), D)
        w1v[f] = mm_tn(xr[...], gpre[:, cols]).astype(BF)
        w2v[cols, :] = mm_tn(act[:, cols], gcot[...]).astype(BF)

    out_w = [pltpu.make_async_copy(w1v, gw.at[0], wlsem.at[0])] + [
        pltpu.make_async_copy(w2v.at[pl.ds(f * D, D)], gw.at[1, f], wlsem.at[1 + f]) for f in range(4)
    ]
    for cp in out_w:
        cp.start()
    for d in range(1, 16):
        p = (me.number + d) % 16

        @pl.when(p // 4 != far)
        def _():
            x_copy(p).wait_send()

        g_copy(p).wait_send()
        r_copy(p).wait_send()
        gg_copy(p).wait_send()
        remote(part(ginh, p), part(ginb, p), rsem.at[0, p], rsem.at[1, p], me.peer(p)).wait_recv()
        remote(ggs.at[p], ggb.at[p], ggsem.at[0, p], ggsem.at[1, p], me.peer(p)).wait_recv()
    own_r.wait()
    own_g.wait()
    own_n.wait()
    for step in range(2):
        for k in range(4):
            p = me.plane(step) * 4 + k

            @pl.when(p != me.number)
            def _():
                n_copy(p).wait_send()
                remote(part(outs, p), part(outn, p), nsem.at[0, p], nsem.at[1, p], me.peer(p)).wait_recv()

    for cp in out_w:
        cp.wait()


def attention_backward(qkv, gatt, lse, gqkv, images, group):
    first = lax.broadcasted_iota(jnp.int32, (SEQ_PAD, 128), 1) < HEAD
    lane = lax.broadcasted_iota(jnp.int32, (SEQ_PAD, 128), 1)
    real = lax.broadcasted_iota(jnp.int32, (SEQ_PAD, SEQ_PAD), 1) < SEQ

    @pl.loop(0, 2)
    def _(near):
        pair = 2 * group + near
        for i in range(images):
            r = slice(i * SEQ_PAD, (i + 1) * SEQ_PAD)
            cols = [pl.ds(pl.multiple_of(part * D + pair * 128, 128), 128) for part in range(3)]
            q, k, v = (qkv[r, cols[part]] for part in range(3))
            g = gatt[r, pl.ds(pl.multiple_of(pair * 128, 128), 128)]
            logs = lse[r, :]
            parts = []
            for h in range(2):
                mine = first if h == 0 else jnp.logical_not(first)
                qh = (jnp.where(mine, q.astype(F32), 0.0) * 0.125).astype(BF)
                gh = jnp.where(mine, g.astype(F32), 0.0).astype(BF)
                log = jnp.sum(jnp.where(lane == 2 * pair + h, logs, 0.0), axis=1, keepdims=True)
                probs = jnp.where(real, jnp.exp(mm_nt(qh, k) - log), 0.0)
                grad_probs = mm_nt(gh, v)
                low = probs.astype(BF)
                delta = jnp.sum(probs * grad_probs, axis=1, keepdims=True)
                grad_scores = (probs * (grad_probs - delta)).astype(BF)
                parts.append((mm(grad_scores, k) * 0.125, mm_tn(grad_scores, q) * 0.125, mm_tn(low, g)))
            for part in range(3):
                place = pl.ds(pl.multiple_of(group * D + part * 256 + near * 128, 128), 128)
                gqkv[r, place] = jnp.where(first, parts[0][part], parts[1][part]).astype(BF)


def kernel_b(
    cap, tok, cot, aux, lse, gate_t, ranks, ggb, dense_in, qkv_in, att_in, hid_in, ginb, outs, gw, outn,
    block_out, gtok, ghat, extra, outb, eg,
    dense, qkv, att, hid, hsem, rowsv, hits, gmoe, low, glow, gatt, gqkv, gd, ra, rb, sc, rc, exs, exl, gx, own_w, ggt,
    osem, lsem, wxsem, wsem, wload, wlocal, asem, bsem, zsem, fsem, esem, xsem,
):
    me = Place()
    z, c, s = me.z, me.core, me.shard
    rows = tok.shape[0]
    images = rows // SEQ_PAD
    block = 4 * cap
    quarter, wide, deep = D // 4, D // 2, D // 16
    greet(me.peers() + [(z * 2 + 1 - c, t) for t in range(4)])

    def part(ref, p):
        return ref.at[pl.ds(pl.multiple_of(p * cap, cap), cap)]

    def o_copy(p):
        return remote(part(outs, p), part(outb, me.number), osem.at[0, p], osem.at[1, me.number], me.peer(p))

    load_in = pltpu.make_async_copy(ginb, rowsv, lsem.at[0])
    load_in.start()
    held = [
        pltpu.make_async_copy(place, ref, hsem.at[n])
        for n, (place, ref) in enumerate(((hid_in, hid), (att_in, att), (dense_in, dense), (qkv_in, qkv)))
    ]
    swap = [remote(gw.at[1 - c, t], gx.at[t], wxsem.at[0, t], wxsem.at[1, t], me.sibling) for t in range(4)]
    for cp in swap:
        cp.start()

    def send_outs(step):
        for k in range(4):
            o_copy(me.plane(step) * 4 + k).start()

    send_outs(3)
    send_outs(2)
    for cp in held:
        cp.start()

    load_in.wait()
    gmoe[...] = jnp.zeros_like(gmoe)

    @pl.loop(0, 4)
    def _(plane):
        fill_hits(ranks, plane, hits, cap)
        for k in range(4):
            rows8 = three_rows(ggb[plane * 4 + k, 0:1, 0:cap])
            row = mm(rows8, hits[k * cap : (k + 1) * cap, :])
            ggt[pl.ds(plane * 4 + k, 1), :] = jnp.sum(row, axis=0, keepdims=True)
        r = pl.ds(pl.multiple_of(plane * block, block), block)
        gmoe[...] += mm_tn(hits[...], rowsv[r, :])

    for cp in held:
        cp.wait()
    gates = gate_t[...]
    grad_gates = ggt[...]
    grad_logits = gates * (grad_gates - jnp.sum(gates * grad_gates, axis=0, keepdims=True))
    gl_high = grad_logits.astype(BF)
    gl_low = (grad_logits - gl_high.astype(F32)).astype(BF)

    @pl.loop(0, images)
    def _(i):
        r = pl.ds(pl.multiple_of(i * SEQ_PAD, SEQ_PAD), SEQ_PAD)
        hat, _unused = norm_stats(hid[r, :])
        low[r, :] = (hat * aux[17:18, :]).astype(BF)

    router = aux[0:16, :].astype(BF)
    gmoe[...] += mm_tn(gl_high, router) + mm_tn(gl_low, router)
    exs[0, 0:16, :] = mm(gl_high, low[...]) + mm(gl_low, low[...])
    exs[0, 16:32, :] = jnp.zeros((16, D), F32)

    @pl.loop(0, images)
    def _(i):
        r = pl.ds(pl.multiple_of(i * SEQ_PAD, SEQ_PAD), SEQ_PAD)
        hat, inv = norm_stats(hid[r, :])
        w = gmoe[r, :]
        scaled = w * aux[17:18, :]
        back = inv * (
            scaled - jnp.mean(scaled, axis=-1, keepdims=True) - hat * jnp.mean(scaled * hat, axis=-1, keepdims=True)
        )
        grad = cot[r, :].astype(F32) + back
        gtok[r, :] = grad
        glow[r, :] = grad.astype(BF)
        exs[0, 17:18, :] += jnp.sum(w * hat, axis=0, keepdims=True)
        hat, _unused = norm_stats(tok[r, :].astype(F32))
        low[r, :] = (hat * aux[16:17, :]).astype(BF)

    def put(group, value):
        for t in range(4):
            for h in range(2):
                gd[group, t, h] = value[t * quarter : (t + 1) * quarter, h * wide : (h + 1) * wide].astype(BF)

    def stage_a(g):
        return [
            remote(gd.at[g, t, 1 - c], ra.at[g, t], asem.at[0, g, t], asem.at[1, g, t], me.sibling) for t in range(4)
        ]

    def stage_b(g):
        return [
            remote(
                gd.at[g, (s + d) % 4, c], rb.at[g, d], bsem.at[0, g, d], bsem.at[1, g, d], (z * 2 + c, (s + d) % 4)
            )
            for d in range(1, 4)
        ]

    def stage_c(g):
        return [
            remote(
                sc.at[g, pl.ds(pl.multiple_of((z + d) % 4 * deep, deep), deep)], rc.at[g, d],
                zsem.at[0, g, d], zsem.at[1, g, d], ((z + d) % 4 * 2 + c, s),
            )
            for d in range(1, 4)
        ]

    my_rows = pl.ds(pl.multiple_of(z * deep, deep), deep)

    def stage_d(g):
        return [
            remote(
                ghat.at[g, c, my_rows], ghat.at[g, c, my_rows],
                fsem.at[0, g, d], fsem.at[1, g, d], ((z + d) % 4 * 2 + c, s),
            )
            for d in range(1, 4)
        ]

    def stage_e(g):
        return [remote(ghat.at[g, c], ghat.at[g, c], esem.at[0, g], esem.at[1, g], me.sibling)]

    def start(copies):
        for cp in copies:
            cp.start()

    def finish(copies):
        for cp in copies:
            cp.wait()

    def to_b(g):
        finish(stage_a(g))
        for t in range(4):
            gd[g, t, c] = (gd[g, t, c].astype(F32) + ra[g, t].astype(F32)).astype(BF)
        start(stage_b(g))

    def to_c(g):
        finish(stage_b(g))
        sc[g] = (
            (gd[g, s, c].astype(F32) + rb[g, 1].astype(F32)) + (rb[g, 2].astype(F32) + rb[g, 3].astype(F32))
        ).astype(BF)
        start(stage_c(g))

    def to_d(g):
        finish(stage_c(g))
        ghat[g, c, my_rows, :] = (
            (sc[g, my_rows, :].astype(F32) + rc[g, 1].astype(F32)) + (rc[g, 2].astype(F32) + rc[g, 3].astype(F32))
        ).astype(BF)
        start(stage_d(g))

    def to_e(g):
        finish(stage_d(g))
        start(stage_e(g))

    put(3, mm_tn(att[...], glow[...]))
    start(stage_a(3))
    gatt[...] = mm_nt(glow[...], dense[:, 2304:3072]).astype(BF)

    def owner_copy(t):
        return remote(
            gx.at[t], eg.at[s % 2, c], wsem.at[0, t], wsem.at[1, s % 2 * 2 + c], (z * 2 + s // 2, t)
        )

    mine_local = s // 2 == c
    owner_local = pltpu.make_async_copy(gx.at[s], eg.at[s % 2, c], wlocal)
    def to_owner(t):
        load = pltpu.make_async_copy(gw.at[c, t], own_w, wload)
        load.start()
        load.wait()
        remote(gw.at[1 - c, t], gx.at[t], wxsem.at[0, t], wxsem.at[1, t], me.sibling).wait()
        gx[t] = (gx[t].astype(F32) + own_w[...].astype(F32)).astype(BF)

        @pl.when(jnp.logical_not(mine_local & (s == t)))
        def _():
            owner_copy(t).start()

        @pl.when(mine_local & (s == t))
        def _():
            owner_local.start()

    to_owner((s + 1) % 4)
    to_b(3)
    for g in range(3):
        attention_backward(qkv, gatt, lse, gqkv, images, g)
        put(g, mm_tn(low[...], gqkv[:, g * D : (g + 1) * D]))
        start(stage_a(g))
        partial = [
            mm_nt(gqkv[:, g * D + 256 * n : g * D + 256 * (n + 1)], dense[:, n * D + g * 256 : n * D + (g + 1) * 256])
            for n in range(3)
        ]
        if g == 0:
            gmoe[...] = (partial[0] + partial[1]) + partial[2]
            to_owner((s + 2) % 4)
        else:
            gmoe[...] += (partial[0] + partial[1]) + partial[2]
            to_b(g - 1)
            if g == 1:
                to_owner((s + 3) % 4)
                to_owner(s)

    @pl.loop(0, images)
    def _(i):
        r = pl.ds(pl.multiple_of(i * SEQ_PAD, SEQ_PAD), SEQ_PAD)
        hat, inv = norm_stats(tok[r, :].astype(F32))
        w = gmoe[r, :]
        scaled = w * aux[16:17, :]
        gtok[r, :] += inv * (
            scaled - jnp.mean(scaled, axis=-1, keepdims=True) - hat * jnp.mean(scaled * hat, axis=-1, keepdims=True)
        )
        exs[0, 16:17, :] += jnp.sum(w * hat, axis=0, keepdims=True)

    def add_outputs(source, step):
        plane = me.plane(step)
        r = pl.ds(pl.multiple_of(plane * block, block), block)
        load = pltpu.make_async_copy(source.at[r], rowsv.at[r], lsem.at[0])
        load.start()
        fill_hits(ranks, plane, hits, cap)
        load.wait()
        gmoe[...] += mm_tn(hits[...], rowsv[r, :])

    to_b(2)
    x_first = remote(exs.at[0], exl.at[0], xsem.at[0, 0], xsem.at[1, 0], me.sibling)
    x_first.start()
    gmoe[...] = hid[...]
    add_outputs(outn, 0)
    add_outputs(outn, 1)
    to_c(3)
    x_first.wait()
    exs[1] = exs[0] + exl[0]
    exl[1 + s] = exs[1]
    x_second = [
        remote(exs.at[1], exl.at[1 + s], xsem.at[0, d], xsem.at[1, d], (z * 2 + c, (s + d) % 4)) for d in range(1, 4)
    ]
    start(x_second)
    to_c(0)
    to_c(1)
    to_c(2)
    finish(x_second)
    exs[2] = (exl[1] + exl[2]) + (exl[3] + exl[4])
    exl[5 + z] = exs[2]
    x_third = [
        remote(exs.at[2], exl.at[5 + z], xsem.at[0, 3 + d], xsem.at[1, 3 + d], ((z + d) % 4 * 2 + c, s))
        for d in range(1, 4)
    ]
    start(x_third)
    for g in (3, 0, 1, 2):
        to_d(g)
    finish(x_third)
    extra[...] = (exl[5] + exl[6]) + (exl[7] + exl[8])
    for g in (3, 0, 1, 2):
        to_e(g)

    for step in (2, 3):
        for k in range(4):
            p = me.plane(step) * 4 + k
            o_copy(p).wait_send()
            remote(part(outs, p), part(outb, p), osem.at[0, p], osem.at[1, p], me.peer(p)).wait_recv()
        add_outputs(outb, step)

    block_out[...] = gmoe[...].astype(BF)

    for t in range(4):
        @pl.when(jnp.logical_not(mine_local & (s == t)))
        def _():
            owner_copy(t).wait_send()

        @pl.when(mine_local & (s == t))
        def _():
            owner_local.wait()

    for i in range(2):
        for a in range(2):
            own = (a == c) & (s == 2 * c + i)

            @pl.when(jnp.logical_not(own))
            def _():
                remote(gx.at[0], eg.at[i, a], wsem.at[0, 0], wsem.at[1, i * 2 + a], me.sibling).wait_recv()

    for g in range(4):
        finish(stage_e(g))


def lane_sums(values, count):
    lane = lax.broadcasted_iota(jnp.int32, (1, count), 1)
    out = jnp.zeros((1, count), F32)
    for n, value in enumerate(values):
        out = jnp.where(lane == n, value, out)
    return out


def total(values):
    return jnp.sum(jnp.sum(values, axis=1, keepdims=True), axis=0, keepdims=True)


def set_columns(ref, columns):
    lane = lax.broadcasted_iota(jnp.int32, ref.shape, 1)
    out = jnp.zeros(ref.shape, F32)
    for n, column in enumerate(columns):
        out = jnp.where(lane == n, column, out)
    ref[...] = out


def pick(row, n):
    lane = lax.broadcasted_iota(jnp.int32, row.shape, 1)
    return jnp.sum(jnp.where(lane == n, row, 0.0), axis=1, keepdims=True)


def mean_square(square_sum, weight_sum, size):
    rms = jnp.sqrt(square_sum * (1.0 / size))
    return rms, -RATE * jnp.sqrt(weight_sum * (1.0 / size)) / jnp.maximum(CLIP, rms)


def kernel_s(
    eg, ghat, extra, w1, w2, dsh, gains, moments, rows3, row_router, v_gain,
    mine_new, v_new, rows3_new, row_router_new, moments_new, sums, sums_r,
    egv, tall, turned, stats, landed, stats_r, landed_r, dgrad,
    isem, xsem, rsem,
):
    me = Place()
    z, c, s = me.z, me.core, me.shard
    quarter = dsh.shape[0]
    load = pltpu.make_async_copy(eg, egv, isem)
    load.start()
    greet(me.mates())

    read_dense(ghat, dgrad)
    mine = jnp.zeros((32, quarter), F32)
    for t in range(4):
        mine = mine + jnp.where(s == t, extra[:, t * quarter : (t + 1) * quarter], 0.0)
    mine_new[...] = mine
    router = mine[0:16, :]
    gain = mine[16:18, :]
    v = DECAY * v_gain[...] + (1.0 - DECAY) * (gain * gain + EPS_SQUARE)
    v_new[...] = v
    raw_gain = gain * lax.rsqrt(v)
    gain_weight = gains[...].astype(F32)
    gain_square = jnp.sum(raw_gain * raw_gain, axis=1, keepdims=True)
    gain_size = jnp.sum(gain_weight * gain_weight, axis=1, keepdims=True)
    router_square = router * router
    router_row = DECAY * row_router[...] + (1.0 - DECAY) * (
        jnp.sum(router_square, axis=0, keepdims=True) * (1.0 / 16) + EPS_SQUARE
    )
    row_router_new[...] = router_row
    set_columns(
        stats_r,
        [
            jnp.sum(router_square, axis=1, keepdims=True) + quarter * EPS_SQUARE,
            jnp.sum(router_square * (1.0 / router_row), axis=1, keepdims=True),
        ],
    )
    router_weight = dsh[:, 4 * D : 4 * D + 16].astype(F32)
    qkv_square = dgrad[:, : 3 * D] * dgrad[:, : 3 * D]
    proj_square = dgrad[:, 3 * D :] * dgrad[:, 3 * D :]
    row_qkv = DECAY * rows3[:, 0:1] + (1.0 - DECAY) * (
        jnp.sum(qkv_square, axis=1, keepdims=True) * (1.0 / (3 * D)) + EPS_SQUARE
    )
    row_proj = DECAY * rows3[:, 1:2] + (1.0 - DECAY) * (
        jnp.sum(proj_square, axis=1, keepdims=True) * (1.0 / D) + EPS_SQUARE
    )
    rows3_new[...] = jnp.where(lax.broadcasted_iota(jnp.int32, rows3_new.shape, 1) == 0, row_qkv, row_proj)
    inv_qkv, inv_proj = 1.0 / row_qkv, 1.0 / row_proj
    for g in range(4):
        square, inv = (qkv_square[:, g * D : (g + 1) * D], inv_qkv) if g < 3 else (proj_square, inv_proj)
        stats[8 + g : 9 + g, :] = jnp.sum(square, axis=0, keepdims=True) + quarter * EPS_SQUARE
        stats[12 + g : 13 + g, :] = jnp.sum(square * inv, axis=0, keepdims=True)
    dense_weight = dsh[:, : 4 * D].astype(F32)
    sizes = [
        total(row_qkv), total(row_proj), total(router_row),
        total(dense_weight[:, : 3 * D] * dense_weight[:, : 3 * D]),
        total(dense_weight[:, 3 * D :] * dense_weight[:, 3 * D :]),
        total(router_weight * router_weight),
        gain_square[0:1], gain_square[1:2], gain_size[0:1], gain_size[1:2],
    ]

    tall[...] = jnp.zeros_like(tall)
    turned[...] = jnp.zeros_like(turned)
    turned[0:8, :] = moments[...]
    moment_columns = jnp.transpose(turned[...])
    load.wait()
    columns = []
    for i in range(2):
        grad = egv[i, 0].astype(F32)
        square = grad * grad
        col = DECAY * moments[2 + i : 3 + i, :] + (1.0 - DECAY) * (
            jnp.sum(square, axis=0, keepdims=True) * (1.0 / D) + EPS_SQUARE
        )
        moments_new[2 + i : 3 + i, :] = col
        columns.append(jnp.sum(square, axis=1, keepdims=True) + D * EPS_SQUARE)
        columns.append(jnp.sum(square * (1.0 / col), axis=1, keepdims=True))
        weight = w1[i].astype(F32)
        sizes.append(total(weight * weight))
    for i in range(2):
        grad = egv[i, 1].astype(F32)
        square = grad * grad
        row = DECAY * moment_columns[:, 4 + i : 5 + i] + (1.0 - DECAY) * (
            jnp.sum(square, axis=1, keepdims=True) * (1.0 / D) + EPS_SQUARE
        )
        columns.append(row)
        stats[4 + i : 5 + i, :] = jnp.sum(square, axis=0, keepdims=True) + D * EPS_SQUARE
        stats[6 + i : 7 + i, :] = jnp.sum(square * (1.0 / row), axis=0, keepdims=True)
        weight = w2[i].astype(F32)
        sizes.append(total(weight * weight))
        sizes.append(total(row))
    set_columns(tall, columns)
    flat = jnp.transpose(tall[...])
    for n, m in ((0, 0), (2, 1), (1, 2), (3, 3)):
        stats[m : m + 1, :] = flat[n : n + 1, :]
    moments_new[0:2, :] = flat[4:6, :]
    moments_new[4:8, :] = jnp.zeros((4, D), F32)
    stats[16:24, :] = jnp.zeros((8, D), F32)
    stats[16:17, :] = lane_sums(sizes, D)

    landed[s] = stats[...]
    landed_r[s] = stats_r[...]
    copies = []
    for d in range(1, 4):
        mate = (z * 2 + c, (s + d) % 4)
        copies.append(remote(stats, landed.at[s], xsem.at[0, d], xsem.at[1, d], mate))
        copies.append(remote(stats_r, landed_r.at[s], rsem.at[0, d], rsem.at[1, d], mate))
    for cp in copies:
        cp.start()
    for cp in copies:
        cp.wait()
    sums[...] = (landed[0] + landed[1]) + (landed[2] + landed[3])
    sums_r[...] = (landed_r[0] + landed_r[1]) + (landed_r[2] + landed_r[3])


def read_dense(ghat, dgrad):
    for g in range(4):
        for n in range(6):
            column = 3 * D + 128 * n if g == 3 else n // 2 * D + g * 256 + n % 2 * 128
            dgrad[:, column : column + 128] = ghat[g, n // 3, :, n % 3 * 128 : n % 3 * 128 + 128].astype(F32)


def kernel_u(
    eg, ghat, mine, w1, w2, dsh, gains, moments, moments_mid, rows3, row_router, cols, col_router, v, sums, sums_r,
    g_first, g_second, n_first, n_second, dense_rms, expert_rms, n_gain, g_qkv, n_qkv, g_proj, n_proj, n_router,
    cols_new, col_router_new, row_in_new, col_out_new,
    egv, grads, news, turned, tall_d, dgrad,
    isem, gsem, nsem,
):
    quarter = dsh.shape[0]
    load = pltpu.make_async_copy(eg, egv, isem)
    load.start()
    read_dense(ghat, dgrad)
    g_qkv[...] = dgrad[:, : 3 * D]
    g_proj[...] = dgrad[:, 3 * D :]
    router, gain = mine[0:16, :], mine[16:18, :]
    raw_gain = gain * lax.rsqrt(v[...])
    gain_weight = gains[...].astype(F32)
    router_row = row_router[...]
    router_weight = dsh[:, 4 * D : 4 * D + 16].astype(F32)
    row_qkv, row_proj = rows3[:, 0:1], rows3[:, 1:2]
    scalars = sums[16:17, :]
    one = lambda n: pick(scalars, n)
    load.wait()

    hidden = 4.0 * D
    row_in = DECAY * moments[0:2, :] + (1.0 - DECAY) * (sums[0:2, :] * (1.0 / hidden))
    row_in_new[...] = row_in
    col_out = DECAY * moments[6:8, :] + (1.0 - DECAY) * (sums[4:6, :] * (1.0 / hidden))
    col_out_new[...] = col_out
    turned[...] = jnp.zeros_like(turned)
    turned[0:2, :] = row_in
    turned[2:4, :] = moments_mid[0:2, :]
    back = jnp.transpose(turned[...])
    rms_all = []
    for i in range(2):
        r = row_in[i : i + 1, :]
        mean = jnp.sum(r, axis=1, keepdims=True) * (1.0 / D)
        raw = mean * jnp.sum(sums[2 + i : 3 + i, :] / r, axis=1, keepdims=True)
        rms, factor = mean_square(raw, one(10 + i), D * hidden)
        rms_all.append(rms)
        left = factor * lax.rsqrt(back[:, i : i + 1] / mean)
        grads[i] = egv[i, 0].astype(F32)
        pltpu.make_async_copy(grads.at[i], g_first.at[i], gsem.at[i]).start()
        news[i] = w1[i].astype(F32) + grads[i] * left * lax.rsqrt(moments_mid[2 + i : 3 + i, :])
        pltpu.make_async_copy(news.at[i], n_first.at[i], nsem.at[i]).start()
    for i in range(2):
        col = col_out[i : i + 1, :]
        mean = one(13 + 2 * i) * (1.0 / hidden)
        raw = mean * jnp.sum(sums[6 + i : 7 + i, :] / col, axis=1, keepdims=True)
        rms, factor = mean_square(raw, one(12 + 2 * i), D * hidden)
        rms_all.append(rms)
        left = factor * lax.rsqrt(back[:, 2 + i : 3 + i] / mean)
        grads[2 + i] = egv[i, 1].astype(F32)
        pltpu.make_async_copy(grads.at[2 + i], g_second.at[i], gsem.at[2 + i]).start()
        news[2 + i] = w2[i].astype(F32) + grads[2 + i] * left * lax.rsqrt(col)
        pltpu.make_async_copy(news.at[2 + i], n_second.at[i], nsem.at[2 + i]).start()
    expert_rms[...] = lane_sums(rms_all, 128)

    rms_g1, factor_g1 = mean_square(one(6), one(8), D)
    rms_g2, factor_g2 = mean_square(one(7), one(9), D)
    upper = lax.broadcasted_iota(jnp.int32, gain.shape, 0) == 0
    n_gain[...] = gain_weight + jnp.where(upper, factor_g1, factor_g2) * raw_gain
    col_dense = []
    for g in range(4):
        col = DECAY * cols[g : g + 1, :] + (1.0 - DECAY) * (sums[8 + g : 9 + g, :] * (1.0 / D))
        cols_new[g : g + 1, :] = col
        col_dense.append(col)
    mean_qkv, mean_proj, mean_router = one(0) * (1.0 / D), one(1) * (1.0 / D), one(2) * (1.0 / D)
    ratio = [jnp.sum(sums[12 + g : 13 + g, :] / col_dense[g], axis=1, keepdims=True) for g in range(4)]
    rms_qkv, factor_qkv = mean_square(mean_qkv * (ratio[0] + ratio[1] + ratio[2]), one(3), 3 * D * D)
    rms_proj, factor_proj = mean_square(mean_proj * ratio[3], one(4), D * D)
    left_qkv = factor_qkv * lax.rsqrt(row_qkv / mean_qkv)
    left_proj = factor_proj * lax.rsqrt(row_proj / mean_proj)
    for g in range(4):
        part = slice(g * D, (g + 1) * D)
        new = dsh[:, part].astype(F32) + dgrad[:, part] * (left_qkv if g < 3 else left_proj) * lax.rsqrt(col_dense[g])
        if g < 3:
            n_qkv[:, part] = new
        else:
            n_proj[...] = new
    col = DECAY * col_router[...] + (1.0 - DECAY) * (sums_r[:, 0:1] * (1.0 / D))
    col_router_new[...] = col
    raw_router = mean_router * jnp.sum(sums_r[:, 1:2] / col, axis=0, keepdims=True)
    rms_router, factor_router = mean_square(raw_router, one(5), 16 * D)
    tall_d[...] = jnp.zeros_like(tall_d)
    tall_d[0:16, 0:quarter] = router * (factor_router * lax.rsqrt(router_row / mean_router)) * lax.rsqrt(col)
    n_router[...] = router_weight + jnp.transpose(tall_d[...])[0:quarter, 0:16]
    dense_rms[...] = lane_sums([rms_g1, rms_g2, rms_qkv, rms_proj, rms_router], 128)
    for i in range(2):
        pltpu.make_async_copy(news.at[i], n_first.at[i], nsem.at[i]).wait()
        pltpu.make_async_copy(news.at[2 + i], n_second.at[i], nsem.at[2 + i]).wait()
        pltpu.make_async_copy(grads.at[i], g_first.at[i], gsem.at[i]).wait()
        pltpu.make_async_copy(grads.at[2 + i], g_second.at[i], gsem.at[2 + i]).wait()


def params(number):
    return pltpu.CompilerParams(collective_id=number, has_side_effects=True, vmem_limit_bytes=VMEM_LIMIT)


def dma(*shape):
    return pltpu.SemaphoreType.DMA(shape)


def fast(
    tokens, routes, cotangent, gain_attn, w_qkv, w_proj, gain_moe, w_router, w_in, w_out,
    v_attn, v_moe, row_qkv, col_qkv, row_proj, col_proj, row_router, col_router, row_in, col_in, row_out, col_out,
):
    count = tokens.shape[0]
    images = count // SEQ
    rows = images * SEQ_PAD
    experts = w_router.shape[1]
    cap = ((3 * count + experts - 1) // experts + 15) // 16 * 16
    slots = experts * cap
    vmem = pl.BlockSpec(memory_space=pltpu.VMEM)
    hbm = pl.BlockSpec(memory_space=pl.ANY)
    shape = jax.ShapeDtypeStruct

    def padded(array, value=0):
        array = array.reshape(images, SEQ, array.shape[1])
        array = jnp.pad(array, ((0, 0), (0, SEQ_PAD - SEQ), (0, 0)), constant_values=value)
        return array.reshape(rows, array.shape[2])

    tok = padded(tokens)
    cot = padded(cotangent)
    rt = padded(routes, -1).T
    quarter = w_qkv.shape[0]
    small = jnp.concatenate([w_router, gain_attn[:, None], gain_moe[:, None]], axis=1)
    small = jnp.pad(small, ((0, 0), (0, 128 - small.shape[1])))
    dsh = jnp.concatenate([w_qkv, w_proj, small], axis=1)
    wide = dsh.shape[1]

    qkv, att, hid, lse, gate_t, ranks, aux, dense, xsend, gsend, cotr, wfull, wfull2, xfar = pl.pallas_call(
        functools.partial(kernel_a, cap),
        out_shape=(
            shape((rows, 3 * D), BF), shape((rows, D), BF), shape((rows, D), F32), shape((rows, 128), F32),
            shape((16, rows), F32), shape((16, rows), jnp.int32), shape((32, D), F32), shape((D, wide), BF),
            shape((slots, D), BF), shape((16, 8, 256), F32), shape((slots, D), BF), shape((4, D, D), BF),
            shape((4, D, D), BF), shape((4 * cap, D), BF),
        ),
        in_specs=[vmem] * 4 + [hbm] * 2,
        out_specs=(hbm,) * 3 + (vmem,) * 4 + (hbm,) * 2 + (vmem,) + (hbm,) * 4,
        scratch_shapes=[
            pltpu.VMEM((rows, 3 * D), BF), pltpu.VMEM((rows, D), BF), pltpu.VMEM((rows, D), F32),
            pltpu.VMEM((D, wide), BF), pltpu.VMEM((slots, D), BF), dma(5),
            pltpu.VMEM((slots, D), BF), pltpu.VMEM((rows, D), BF), pltpu.VMEM((4 * cap, rows), BF),
            pltpu.VMEM((rows, rows), BF), dma(2, 4), dma(2, 4), dma(2, 16), dma(2), dma(), dma(2), dma(2, 2),
            dma(2), dma(), dma(2), dma(2, 2), dma(), dma(2, 4),
        ],
        compiler_params=params(1),
        name="forward",
    )(tok, cot, rt, dsh, w_in, w_out)

    outs, ginh, ginb, ggb, gw, outn = pl.pallas_call(
        functools.partial(kernel_e, cap),
        out_shape=(
            shape((slots, D), BF), shape((slots, D), BF), shape((slots, D), BF), shape((16, 8, 256), F32),
            shape((2, 4, D, D), BF), shape((slots, D), BF),
        ),
        in_specs=[hbm, vmem, hbm, hbm, hbm, hbm],
        out_specs=(hbm, hbm, hbm, vmem, hbm, hbm),
        scratch_shapes=[
            pltpu.VMEM((4, D, D), BF), pltpu.VMEM((FF, D), BF), pltpu.VMEM((slots, D), BF), pltpu.VMEM((slots, D), BF),
            pltpu.VMEM((16, 8, 256), F32), pltpu.VMEM((slots, FF), BF), pltpu.VMEM((slots, FF), BF),
            pltpu.VMEM((4 * cap, D), F32), pltpu.VMEM((2, 4 * cap, D), BF),
            pltpu.VMEM((16, 8, 256), F32), pltpu.VMEM((4 * cap, 128), F32),
            dma(2, 16), dma(2, 16), dma(2, 16), dma(2, 16), dma(6), dma(6), dma(2), dma(2, 16),
        ],
        compiler_params=params(2),
        name="experts",
    )(xsend, gsend, cotr, wfull, wfull2, xfar)

    block_out, gtok, ghat, extra, outb, eg = pl.pallas_call(
        functools.partial(kernel_b, cap),
        out_shape=(
            shape((rows, D), BF), shape((rows, D), F32), shape((4, 2, quarter, D // 2), BF), shape((32, D), F32),
            shape((slots, D), BF), shape((2, 2, D, D), BF),
        ),
        in_specs=[vmem] * 7 + [hbm] * 8,
        out_specs=(vmem,) * 4 + (hbm,) * 2,
        scratch_shapes=[
            pltpu.VMEM((D, wide), BF), pltpu.VMEM((rows, 3 * D), BF), pltpu.VMEM((rows, D), BF),
            pltpu.VMEM((rows, D), F32), dma(4), pltpu.VMEM((slots, D), BF), pltpu.VMEM((4 * cap, rows), BF), pltpu.VMEM((rows, D), F32),
            pltpu.VMEM((rows, D), BF), pltpu.VMEM((rows, D), BF), pltpu.VMEM((rows, D), BF),
            pltpu.VMEM((rows, 3 * D), BF), pltpu.VMEM((4, 4, 2, quarter, D // 2), BF),
            pltpu.VMEM((4, 4, quarter, D // 2), BF), pltpu.VMEM((4, 4, quarter, D // 2), BF),
            pltpu.VMEM((4, quarter, D // 2), BF), pltpu.VMEM((4, 4, quarter // 4, D // 2), BF),
            pltpu.VMEM((3, 32, D), F32), pltpu.VMEM((9, 32, D), F32), pltpu.VMEM((4, D, D), BF),
            pltpu.VMEM((D, D), BF), pltpu.VMEM((16, rows), F32),
            dma(2, 16), dma(2), dma(2, 4), dma(2, 4), dma(), dma(), dma(2, 4, 4), dma(2, 4, 4), dma(2, 4, 4),
            dma(2, 4, 4), dma(2, 4), dma(2, 7),
        ],
        compiler_params=params(3),
        name="backward",
    )(tok, cot, aux, lse, gate_t, ranks, ggb, dense, qkv, att, hid, ginb, outs, gw, outn)

    def unpadded(array):
        return array.reshape(images, SEQ_PAD, D)[:, :SEQ].reshape(count, D)

    gains = jnp.stack([gain_attn, gain_moe])
    moments = jnp.concatenate([row_in, col_in, row_out, col_out])
    mine, v_new, rows_new, row_router_new, moments_mid, sums, sums_r = pl.pallas_call(
        kernel_s,
        out_shape=(
            shape((32, quarter), F32), shape((2, quarter), F32), shape((quarter, 2), F32), shape((1, quarter), F32),
            shape((8, D), F32), shape((24, D), F32), shape((16, 128), F32),
        ),
        in_specs=[hbm] + [vmem] * 10,
        out_specs=(vmem,) * 7,
        scratch_shapes=[
            pltpu.VMEM((2, 2, D, D), BF), pltpu.VMEM((D, 128), F32), pltpu.VMEM((128, D), F32),
            pltpu.VMEM((24, D), F32), pltpu.VMEM((4, 24, D), F32), pltpu.VMEM((16, 128), F32),
            pltpu.VMEM((4, 16, 128), F32), pltpu.VMEM((quarter, 4 * D), F32), dma(), dma(2, 4), dma(2, 4),
        ],
        compiler_params=params(4),
        name="update_sums",
    )(
        eg, ghat, extra, w_in, w_out, dsh, gains, moments, jnp.stack([row_qkv, row_proj], axis=1), row_router[None],
        jnp.stack([v_attn, v_moe]),
    )
    (
        g_first, g_second, n_first, n_second, dense_rms, expert_rms, n_gain, g_qkv, n_qkv, g_proj, n_proj, n_router,
        cols_new, col_router_new, row_in_new, col_out_new,
    ) = pl.pallas_call(
        kernel_u,
        out_shape=(
            shape((2, D, D), F32), shape((2, D, D), F32), shape((2, D, D), F32), shape((2, D, D), F32),
            shape((1, 128), F32), shape((1, 128), F32), shape((2, quarter), F32),
            shape((quarter, 3 * D), F32), shape((quarter, 3 * D), F32),
            shape((quarter, D), F32), shape((quarter, D), F32), shape((quarter, 16), F32),
            shape((4, D), F32), shape((16, 1), F32), shape((2, D), F32), shape((2, D), F32),
        ),
        in_specs=[hbm] + [vmem] * 15,
        out_specs=(hbm,) * 4 + (vmem,) * 12,
        scratch_shapes=[
            pltpu.VMEM((2, 2, D, D), BF), pltpu.VMEM((4, D, D), F32), pltpu.VMEM((4, D, D), F32),
            pltpu.VMEM((128, D), F32), pltpu.VMEM((128, 256), F32), pltpu.VMEM((quarter, 4 * D), F32),
            dma(), dma(4), dma(4),
        ],
        compiler_params=pltpu.CompilerParams(vmem_limit_bytes=VMEM_LIMIT),
        name="update",
    )(
        eg, ghat, mine, w_in, w_out, dsh, gains, moments, moments_mid, rows_new, row_router_new,
        jnp.concatenate([col_qkv, col_proj]).reshape(4, D), col_router[:, None], v_new, sums, sums_r,
    )
    return (
        unpadded(block_out), unpadded(gtok), dense_rms[0, :5], expert_rms[0, :4].reshape(2, 2).T,
        mine[16], n_gain[0], v_new[0], mine[17], n_gain[1], v_new[1],
        g_qkv, n_qkv, rows_new[:, 0], cols_new[:3].reshape(3 * D),
        g_proj, n_proj, rows_new[:, 1], cols_new[3],
        mine[:16].T, n_router, row_router_new[0], col_router_new[:, 0],
        g_first, n_first, row_in_new, moments_mid[2:4],
        g_second, n_second, moments_mid[0:2], col_out_new,
    )


def local(
    tokens, routes, cotangent, gain_attn, w_qkv, w_proj, gain_moe, w_router, w_in, w_out,
    v_attn, v_moe, row_qkv, col_qkv, row_proj, col_proj, row_router, col_router, row_in, col_in, row_out, col_out,
):
    if (
        lax.axis_size("shard") == 4
        and lax.axis_size("expert") == 8
        and w_in.shape == w_out.shape == (2, D, D)
        and tokens.shape[0] % SEQ == 0
    ):
        return fast(
            tokens, routes, cotangent, gain_attn, w_qkv, w_proj, gain_moe, w_router, w_in, w_out,
            v_attn, v_moe, row_qkv, col_qkv, row_proj, col_proj, row_router, col_router, row_in, col_in, row_out, col_out,
        )
    block_out, grad_tokens, dense_parts, expert_parts = general(
        tokens, routes, cotangent, gain_attn, w_qkv, w_proj, gain_moe, w_router, w_in, w_out
    )
    part_g1, part_qkv, part_proj, part_g2, part_router = dense_parts
    grad_first, grad_second = expert_parts
    expert_count = part_router.shape[1]
    weight_g1 = gain_attn.astype(jnp.float32)
    weight_g2 = gain_moe.astype(jnp.float32)
    dense = (
        (part_qkv, w_qkv.astype(jnp.float32), row_qkv, col_qkv),
        (part_proj, w_proj.astype(jnp.float32), row_proj, col_proj),
        (part_router, w_router.astype(jnp.float32), row_router, col_router),
    )
    weight_first = w_in.astype(jnp.float32)
    weight_second = w_out.astype(jnp.float32)
    v_attn_new = DECAY * v_attn + (1.0 - DECAY) * (part_g1 * part_g1 + EPS_SQUARE)
    v_moe_new = DECAY * v_moe + (1.0 - DECAY) * (part_g2 * part_g2 + EPS_SQUARE)
    raw_g1 = part_g1 * lax.rsqrt(v_attn_new)
    raw_g2 = part_g2 * lax.rsqrt(v_moe_new)
    dense_rows, dense_sums = [], []
    for grad, weight, row, col in dense:
        square = grad * grad
        row_new = DECAY * row + (1.0 - DECAY) * jnp.mean(square + EPS_SQUARE, axis=1)
        dense_rows.append(row_new)
        dense_sums.append(
            (
                jnp.sum(square + EPS_SQUARE, axis=0),
                jnp.sum(square / row_new[:, None], axis=0),
                jnp.stack([jnp.sum(row_new), jnp.sum(weight * weight)]),
            )
        )
    square_first = grad_first * grad_first
    square_second = grad_second * grad_second
    col_in_new = DECAY * col_in + (1.0 - DECAY) * jnp.mean(square_first + EPS_SQUARE, axis=1)
    row_out_new = DECAY * row_out + (1.0 - DECAY) * jnp.mean(square_second + EPS_SQUARE, axis=2)
    gain_sums = jnp.stack(
        [
            jnp.sum(raw_g1 * raw_g1),
            jnp.sum(raw_g2 * raw_g2),
            jnp.sum(weight_g1 * weight_g1),
            jnp.sum(weight_g2 * weight_g2),
        ]
    )
    expert_sums = (
        jnp.sum(square_first + EPS_SQUARE, axis=2),
        jnp.sum(square_first / col_in_new[:, None, :], axis=2),
        jnp.sum(square_second + EPS_SQUARE, axis=1),
        jnp.sum(square_second / row_out_new[:, :, None], axis=1),
        jnp.stack(
            [
                jnp.sum(weight_first * weight_first, axis=(1, 2)),
                jnp.sum(row_out_new, axis=1),
                jnp.sum(weight_second * weight_second, axis=(1, 2)),
            ]
        ),
    )
    expert_sums = lax.psum(expert_sums, "shard")
    dense_sums, gain_sums = lax.psum((dense_sums, gain_sums), "shard")

    def step(square_sum, weight_sum, size):
        rms = jnp.sqrt(square_sum / size)
        return rms, -RATE * jnp.sqrt(weight_sum / size) / jnp.maximum(CLIP, rms)

    rms_g1, factor_g1 = step(gain_sums[0], gain_sums[2], D)
    rms_g2, factor_g2 = step(gain_sums[1], gain_sums[3], D)
    new_g1 = weight_g1 + factor_g1 * raw_g1
    new_g2 = weight_g2 + factor_g2 * raw_g2
    dense_new, dense_cols, dense_rms = [], [], [rms_g1, rms_g2]
    for (grad, weight, _, col), row_new, (col_sum, ratio_sum, both) in zip(dense, dense_rows, dense_sums):
        col_new = DECAY * col + (1.0 - DECAY) * (col_sum / D)
        row_mean = both[0] / D
        rms, factor = step(row_mean * jnp.sum(ratio_sum / col_new), both[1], grad.shape[1] * D)
        raw = grad * lax.rsqrt(row_new[:, None] * col_new[None, :] / row_mean)
        dense_new.append(weight + factor * raw)
        dense_cols.append(col_new)
        dense_rms.append(rms)
    new_qkv, new_proj, new_router = dense_new
    row_qkv_new, row_proj_new, row_router_new = dense_rows
    col_qkv_new, col_proj_new, col_router_new = dense_cols
    row_in_sum, ratio_in, col_out_sum, ratio_out, expert_scalars = expert_sums
    row_in_new = DECAY * row_in + (1.0 - DECAY) * (row_in_sum / FF)
    col_out_new = DECAY * col_out + (1.0 - DECAY) * (col_out_sum / FF)
    mean_in = jnp.mean(row_in_new, axis=1)
    mean_out = expert_scalars[1] / FF
    rms_first, factor_first = step(mean_in * jnp.sum(ratio_in / row_in_new, axis=1), expert_scalars[0], D * FF)
    rms_second, factor_second = step(mean_out * jnp.sum(ratio_out / col_out_new, axis=1), expert_scalars[2], D * FF)
    new_first = weight_first + factor_first[:, None, None] * grad_first * lax.rsqrt(
        row_in_new[:, :, None] * col_in_new[:, None, :] / mean_in[:, None, None]
    )
    new_second = weight_second + factor_second[:, None, None] * grad_second * lax.rsqrt(
        row_out_new[:, :, None] * col_out_new[:, None, :] / mean_out[:, None, None]
    )
    return (
        block_out,
        grad_tokens,
        jnp.stack(dense_rms),
        jnp.stack([rms_first, rms_second], axis=1),
        part_g1,
        new_g1,
        v_attn_new,
        part_g2,
        new_g2,
        v_moe_new,
        part_qkv,
        new_qkv,
        row_qkv_new,
        col_qkv_new,
        part_proj,
        new_proj,
        row_proj_new,
        col_proj_new,
        part_router,
        new_router,
        row_router_new,
        col_router_new,
        grad_first,
        new_first,
        row_in_new,
        col_in_new,
        grad_second,
        new_second,
        row_out_new,
        col_out_new,
    )


def solution(mesh):
    return jax.shard_map(
        local,
        mesh=mesh,
        in_specs=(
            P(("expert", "shard"), None),
            P(("expert", "shard"), None),
            P(("expert", "shard"), None),
            P("shard"),
            P("shard", None),
            P("shard", None),
            P("shard"),
            P("shard", None),
            P("expert", None, "shard"),
            P("expert", "shard", None),
            P("shard"),
            P("shard"),
            P("shard"),
            P(),
            P("shard"),
            P(),
            P("shard"),
            P(),
            P("expert", None),
            P("expert", "shard"),
            P("expert", "shard"),
            P("expert", None),
        ),
        out_specs=(
            P(("expert", "shard"), None),
            P(("expert", "shard"), None),
            P(),
            P("expert", None),
            P("shard"),
            P("shard"),
            P("shard"),
            P("shard"),
            P("shard"),
            P("shard"),
            P("shard", None),
            P("shard", None),
            P("shard"),
            P(),
            P("shard", None),
            P("shard", None),
            P("shard"),
            P(),
            P("shard", None),
            P("shard", None),
            P("shard"),
            P(),
            P("expert", None, "shard"),
            P("expert", None, "shard"),
            P("expert", None),
            P("expert", "shard"),
            P("expert", "shard", None),
            P("expert", "shard", None),
            P("expert", "shard"),
            P("expert", None),
        ),
        check_vma=False,
    )
```

```python
import functools

import jax
import jax.numpy as jnp
from jax import lax
from jax.experimental import pallas as pl
from jax.experimental.pallas import tpu as pltpu
from jax.sharding import PartitionSpec as P

D = 768
HEADS = 12
HEAD = 64
FF = 3072
SEQ = 197


PRECISE = lax.Precision.HIGHEST
EPS_NORM = 1e-06
EPS_SQUARE = 1e-30
RATE = 0.3
DECAY = 0.5
CLIP = 0.05


GELU_A = 0.7978845608028654
GELU_B = 0.044715


def normalize(values):
    center = values - jnp.mean(values, axis=-1, keepdims=True)
    inv_root = lax.rsqrt(jnp.mean(center * center, axis=-1, keepdims=True) + EPS_NORM)
    return (center * inv_root, inv_root)


def norm_back(grad, normed, inv_root, gain):
    scaled = grad * gain
    grad_in = inv_root * (
        scaled
        - jnp.mean(scaled, axis=-1, keepdims=True)
        - normed * jnp.mean(scaled * normed, axis=-1, keepdims=True)
    )
    return (grad_in, jnp.sum(grad * normed, axis=0))


def gelu_tanh(values):
    return jax.nn.gelu(values, approximate=True)


def general(
    tokens,
    routes,
    cotangent,
    gain_attn,
    w_qkv,
    w_proj,
    gain_moe,
    w_router,
    w_in,
    w_out,
):
    gain_first, qkv_full, proj_full, gain_second, router_full = (
        lax.all_gather(gain_attn, "shard", axis=0, tiled=True),
        lax.all_gather(w_qkv, "shard", axis=0, tiled=True),
        lax.all_gather(w_proj, "shard", axis=0, tiled=True),
        lax.all_gather(gain_moe, "shard", axis=0, tiled=True),
        lax.all_gather(w_router, "shard", axis=0, tiled=True),
    )
    first_full, second_full = (
        lax.all_gather(w_in, "shard", axis=2, tiled=True),
        lax.all_gather(w_out, "shard", axis=1, tiled=True),
    )
    row_count = tokens.shape[0]
    image_count = row_count // SEQ
    expert_count = router_full.shape[1]
    per_device = w_in.shape[0]
    axis_count = lax.axis_size("expert")
    capacity = ((3 * row_count + expert_count - 1) // expert_count + 7) // 8 * 8
    score_scale = HEAD ** (-0.5)
    tok_float = tokens.astype(jnp.float32)
    gain_one = gain_first.astype(jnp.float32)
    gain_two = gain_second.astype(jnp.float32)
    attn_hat, attn_inv = normalize(tok_float)
    attn_low = (attn_hat * gain_one).astype(jnp.bfloat16)
    qkv_low = jnp.dot(attn_low, qkv_full, preferred_element_type=jnp.float32).astype(jnp.bfloat16)
    qkv_split = qkv_low.reshape(image_count, SEQ, 3, HEADS, HEAD)
    query_part = qkv_split[:, :, 0]
    key_part = qkv_split[:, :, 1]
    value_part = qkv_split[:, :, 2]
    scores = (
        jnp.einsum("ishd,ithd->ihst", query_part, key_part, preferred_element_type=jnp.float32)
        * score_scale
    )
    log_total = jax.nn.logsumexp(scores, axis=-1, keepdims=True)
    soft_low = jnp.exp(scores - log_total).astype(jnp.bfloat16)
    attended = (
        jnp.einsum("ihst,ithd->ishd", soft_low, value_part, preferred_element_type=jnp.float32)
        .reshape(row_count, D)
        .astype(jnp.bfloat16)
    )
    hidden = tok_float + jnp.dot(attended, proj_full, preferred_element_type=jnp.float32)
    moe_hat, moe_inv = normalize(hidden)
    moe_low = (moe_hat * gain_two).astype(jnp.bfloat16)
    logits = jnp.dot(moe_low, router_full, preferred_element_type=jnp.float32)
    labels = jnp.arange(expert_count, dtype=jnp.int32)
    route_hits = (routes[:, :, None] == labels[None, None, :]).astype(jnp.float32)
    chosen = jnp.sum(route_hits * logits[:, None, :], axis=2)
    gates = jax.nn.softmax(chosen, axis=-1)
    flat_routes = routes.reshape(-1)
    earlier = (jnp.arange(row_count)[:, None] > jnp.arange(row_count)[None, :]).astype(jnp.bfloat16)
    before = jnp.dot(
        earlier, jnp.sum(route_hits, axis=1).astype(jnp.bfloat16), preferred_element_type=jnp.float32
    )
    slot_rank = jnp.sum(route_hits * before[:, None, :], axis=2).astype(jnp.int32).reshape(-1)
    slot_dest = flat_routes * capacity + slot_rank
    pair_index = jnp.arange(2 * row_count, dtype=jnp.int32)
    slot_pair = (
        jnp.full((expert_count * capacity,), 2 * row_count, jnp.int32).at[slot_dest].set(pair_index)
    )
    slot_token = slot_pair // 2
    zero_row = jnp.zeros((1, D), jnp.bfloat16)
    send_rows = jnp.concatenate([moe_low, zero_row], axis=0)[slot_token].reshape(
        axis_count, per_device, capacity, D
    )
    received = lax.all_to_all(send_rows, "expert", split_axis=0, concat_axis=0, tiled=True)
    pre_gelu = jnp.einsum(
        "sekd,edf->sekf", received, first_full, preferred_element_type=jnp.float32
    )
    activated = gelu_tanh(pre_gelu).astype(jnp.bfloat16)
    expert_out = jnp.einsum(
        "sekf,efd->sekd", activated, second_full, preferred_element_type=jnp.float32
    ).astype(jnp.bfloat16)
    back_rows = lax.all_to_all(expert_out, "expert", split_axis=0, concat_axis=0, tiled=True)
    back_rows, received, pre_gelu, activated = (back_rows, received, pre_gelu, activated)
    picked = (
        back_rows.reshape(expert_count * capacity, D)[slot_dest]
        .reshape(row_count, 2, D)
        .astype(jnp.float32)
    )
    block_out = (hidden + jnp.sum(gates[:, :, None] * picked, axis=1)).astype(jnp.bfloat16)
    grad_out = cotangent.astype(jnp.float32)
    grad_picked = (gates[:, :, None] * grad_out[:, None, :]).astype(jnp.bfloat16)
    grad_gates = jnp.sum(grad_out[:, None, :] * picked, axis=2)
    grad_chosen = gates * (grad_gates - jnp.sum(gates * grad_gates, axis=1, keepdims=True))
    grad_logits = jnp.sum(route_hits * grad_chosen[:, :, None], axis=1)
    grad_send = jnp.concatenate([grad_picked.reshape(2 * row_count, D), zero_row], axis=0)[
        slot_pair
    ].reshape(axis_count, per_device, capacity, D)
    grad_recv = lax.all_to_all(grad_send, "expert", split_axis=0, concat_axis=0, tiled=True)
    grad_act = jnp.einsum(
        "sekd,efd->sekf", grad_recv, second_full, preferred_element_type=jnp.float32
    )
    unused, gelu_pull = jax.vjp(gelu_tanh, pre_gelu)
    grad_pre = gelu_pull(grad_act)[0].astype(jnp.bfloat16)
    grad_rows = jnp.einsum(
        "sekf,edf->sekd", grad_pre, first_full, preferred_element_type=jnp.float32
    ).astype(jnp.bfloat16)
    grad_back = lax.all_to_all(grad_rows, "expert", split_axis=0, concat_axis=0, tiled=True)
    grad_first = jnp.einsum(
        "sekd,sekf->edf", received, grad_pre, preferred_element_type=jnp.float32
    )
    grad_second = jnp.einsum(
        "sekf,sekd->efd", activated, grad_recv, preferred_element_type=jnp.float32
    )
    grad_first, grad_second = (
        lax.psum_scatter(grad_first, "shard", scatter_dimension=2, tiled=True),
        lax.psum_scatter(grad_second, "shard", scatter_dimension=1, tiled=True),
    )
    returned = (
        grad_back.reshape(expert_count * capacity, D)[slot_dest]
        .reshape(row_count, 2, D)
        .astype(jnp.float32)
    )
    router_float = router_full.astype(jnp.float32)
    grad_moe = jnp.sum(returned, axis=1) + jnp.einsum(
        "te,de->td", grad_logits, router_float, precision=PRECISE
    )
    grad_router = jnp.einsum(
        "td,te->de", moe_low.astype(jnp.float32), grad_logits, precision=PRECISE
    )
    grad_from_moe, grad_g2 = norm_back(grad_moe, moe_hat, moe_inv, gain_two)
    grad_hidden = grad_out + grad_from_moe
    grad_low = grad_hidden.astype(jnp.bfloat16)
    grad_proj = jnp.einsum("tc,td->cd", attended, grad_low, preferred_element_type=jnp.float32)
    grad_att = (
        jnp.einsum("td,cd->tc", grad_low, proj_full, preferred_element_type=jnp.float32)
        .astype(jnp.bfloat16)
        .reshape(image_count, SEQ, HEADS, HEAD)
    )
    scores_again = (
        jnp.einsum("ishd,ithd->ihst", query_part, key_part, preferred_element_type=jnp.float32)
        * score_scale
    )
    soft_again = jnp.exp(scores_again - log_total)
    soft_again_low = soft_again.astype(jnp.bfloat16)
    grad_soft = jnp.einsum(
        "ishd,ithd->ihst", grad_att, value_part, preferred_element_type=jnp.float32
    )
    grad_value = jnp.einsum(
        "ihst,ishd->ithd", soft_again_low, grad_att, preferred_element_type=jnp.float32
    )
    row_delta = jnp.sum(soft_again * grad_soft, axis=-1, keepdims=True)
    grad_scores = (soft_again * (grad_soft - row_delta)).astype(jnp.bfloat16)
    grad_query = (
        jnp.einsum("ihst,ithd->ishd", grad_scores, key_part, preferred_element_type=jnp.float32)
        * score_scale
    )
    grad_key = (
        jnp.einsum("ihst,ishd->ithd", grad_scores, query_part, preferred_element_type=jnp.float32)
        * score_scale
    )
    grad_qkv_low = (
        jnp.stack([grad_query, grad_key, grad_value], axis=2)
        .reshape(row_count, 3 * D)
        .astype(jnp.bfloat16)
    )
    grad_qkv = jnp.einsum("tc,td->cd", attn_low, grad_qkv_low, preferred_element_type=jnp.float32)
    grad_attn_in = jnp.einsum(
        "td,cd->tc", grad_qkv_low, qkv_full, preferred_element_type=jnp.float32
    )
    grad_from_attn, grad_g1 = norm_back(grad_attn_in, attn_hat, attn_inv, gain_one)
    grad_tokens = grad_hidden + grad_from_attn
    dense_grads = (grad_g1, grad_qkv, grad_proj, grad_g2, grad_router)
    dense_total = lax.psum(
        (dense_grads[0], dense_grads[1], dense_grads[2], dense_grads[3], dense_grads[4]), "expert"
    )
    dense_parts = (
        lax.psum_scatter(dense_total[0], "shard", scatter_dimension=0, tiled=True),
        lax.psum_scatter(dense_total[1], "shard", scatter_dimension=0, tiled=True),
        lax.psum_scatter(dense_total[2], "shard", scatter_dimension=0, tiled=True),
        lax.psum_scatter(dense_total[3], "shard", scatter_dimension=0, tiled=True),
        lax.psum_scatter(dense_total[4], "shard", scatter_dimension=0, tiled=True),
    )
    return block_out, grad_tokens, dense_parts, (grad_first, grad_second)


SEQ_PAD = 224
MESH = pl.DeviceIdType.MESH
VMEM_LIMIT = 62 * 1024 * 1024
BF = jnp.bfloat16
F32 = jnp.float32


def mm(a, b):
    return lax.dot_general(a, b, (((1,), (0,)), ((), ())), preferred_element_type=F32)


def mm_nt(a, b):
    return lax.dot_general(a, b, (((1,), (1,)), ((), ())), preferred_element_type=F32)


def mm_tn(a, b):
    return lax.dot_general(a, b, (((0,), (0,)), ((), ())), preferred_element_type=F32)


def remote(src, dst, send, recv, device):
    return pltpu.make_async_remote_copy(
        src_ref=src, dst_ref=dst, send_sem=send, recv_sem=recv, device_id=device, device_id_type=MESH
    )


def greet(devices):
    barrier = pltpu.get_barrier_semaphore()
    for device in devices:
        pl.semaphore_signal(barrier, inc=1, device_id=device, device_id_type=MESH)
    pl.semaphore_wait(barrier, len(devices))


class Place:
    def __init__(self):
        expert = lax.axis_index("expert")
        self.shard = lax.axis_index("shard")
        self.z, self.core = expert // 2, expert % 2
        self.number = self.z * 4 + self.shard
        self.sibling = (self.z * 2 + 1 - self.core, self.shard)

    def plane(self, step):
        return (self.z // 2 + step // 2) % 2 * 2 + (self.z + step) % 2

    def peer(self, number):
        return (number // 4 * 2 + self.core, number % 4)

    def peers(self):
        return [self.peer((self.number + d) % 16) for d in range(1, 16)]

    def mates(self):
        return [(self.z * 2 + self.core, (self.shard + d) % 4) for d in range(1, 4)]


class Quarters:
    def __init__(self, me, source, place, send, recv, local, pass_on):
        self.me, self.source, self.place = me, source, place
        self.sems = send, recv, local, pass_on

    def outgoing(self, act):
        me, (send, recv, local, _) = self.me, self.sems
        core = me.shard % 2
        for i in range(2):
            chip = 2 * me.core + i
            own = (core == me.core) & (chip == me.shard)

            @pl.when(jnp.logical_not(own))
            def _():
                act(
                    remote(
                        self.source.at[i], self.place(me.shard), send.at[i], recv.at[me.shard // 2],
                        (me.z * 2 + core, chip),
                    )
                )

            @pl.when(own)
            def _():
                act(pltpu.make_async_copy(self.source.at[i], self.place(me.shard), local))

    def start(self):
        self.outgoing(lambda cp: cp.start())

    def handed_on(self, q):
        pass_on = self.sems[3]
        return remote(self.place(q), self.place(q), pass_on.at[0, q // 2], pass_on.at[1, q // 2], self.me.sibling)

    def forward(self):
        me, (send, recv, local, _) = self.me, self.sems
        for n in range(2):
            q = 2 * n + me.core
            here = (me.shard // 2 == me.core) & (me.shard == q)

            @pl.when(jnp.logical_not(here))
            def _():
                remote(self.source.at[0], self.place(q), send.at[0], recv.at[n], me.sibling).wait_recv()

            @pl.when(here)
            def _():
                pltpu.make_async_copy(self.source.at[0], self.place(q), local).wait()

            self.handed_on(q).start()

    def finish(self):
        me, (send, recv, _, _) = self.me, self.sems
        core = me.shard % 2
        for i in range(2):
            chip = 2 * me.core + i

            @pl.when(jnp.logical_not((core == me.core) & (chip == me.shard)))
            def _():
                remote(self.source.at[i], self.place(me.shard), send.at[i], recv.at[0], me.sibling).wait_send()

        for n in range(2):
            self.handed_on(2 * n + me.core).wait_send()
            self.handed_on(2 * n + 1 - me.core).wait_recv()


def split3(rows):
    high = rows.astype(BF)
    rest = rows - high.astype(F32)
    low = rest.astype(BF)
    last = (rest - low.astype(F32)).astype(BF)
    return high, low, last


def three_rows(row):
    high, low, last = split3(row)
    index = lax.broadcasted_iota(jnp.int32, (8, row.shape[1]), 0)
    out = jnp.where(index == 0, high.astype(F32), 0.0)
    out = jnp.where(index == 1, low.astype(F32), out)
    return jnp.where(index == 2, last.astype(F32), out).astype(BF)


def norm_stats(values):
    center = values - jnp.mean(values, axis=-1, keepdims=True)
    inv = lax.rsqrt(jnp.mean(center * center, axis=-1, keepdims=True) + EPS_NORM)
    return center * inv, inv


def fill_hits(ranks, plane, hits, cap):
    slot = lax.broadcasted_iota(jnp.int32, (cap, hits.shape[1]), 0)
    for k in range(4):
        row = ranks[pl.ds(plane * 4 + k, 1), :]
        hits[k * cap : (k + 1) * cap, :] = jnp.where(slot == row, 1.0, 0.0).astype(BF)


def kernel_a(
    cap, tok, cot, rt, dsh, w1, w2,
    qkv_out, att_out, hid_out, lse, gate_t, ranks, aux, dense_out, xsend_out, gsend, cotr, wfull, wfull2, xfar,
    qkv, att, hid, dense, xsend, ssem, csend, low, hits, tri, dsem, dfsem, csem, wsem, wloc, wrecv, fsem, wsem2, wloc2, wrecv2, fsem2, osem, xsem,
):
    me = Place()
    z, c, s = me.z, me.core, me.shard
    rows = tok.shape[0]
    images = rows // SEQ_PAD
    other = [(z * 2 + 1 - c, t) for t in range(4)]
    greet(me.peers() + other)

    quarter = dsh.shape[0]
    half = quarter // 2
    dense_copies = []
    for d in range(1, 4):
        cp = remote(
            dsh.at[pl.ds(pl.multiple_of(c * half, half), half)],
            dense.at[pl.ds(pl.multiple_of(s * quarter + c * half, half), half)],
            dsem.at[0, d], dsem.at[1, d], (z * 2 + c, (s + d) % 4),
        )
        cp.start()
        dense_copies.append(cp)
    dense[pl.ds(pl.multiple_of(s * quarter, quarter), quarter), :] = dsh[...]

    expert_row = lax.broadcasted_iota(jnp.int32, (16, rows), 0)
    hit = (expert_row == rt[0:1, :]) | (expert_row == rt[1:2, :])
    earlier = lax.broadcasted_iota(jnp.int32, (rows, rows), 0) < lax.broadcasted_iota(jnp.int32, (rows, rows), 1)
    tri[...] = jnp.where(earlier, 1.0, 0.0).astype(BF)
    before = mm(jnp.where(hit, 1.0, 0.0).astype(BF), tri[...])
    ranks[...] = jnp.where(hit, before, -1.0).astype(jnp.int32)

    def cot_copy(p):
        return remote(
            csend.at[pl.ds(pl.multiple_of(p * cap, cap), cap)],
            cotr.at[pl.ds(pl.multiple_of(me.number * cap, cap), cap)],
            csem.at[0, p], csem.at[1, me.number], me.peer(p),
        )

    own = pl.multiple_of(me.number * cap, cap)
    own_copy = pltpu.make_async_copy(csend.at[pl.ds(own, cap)], cotr.at[pl.ds(own, cap)], osem)

    @pl.loop(0, 4)
    def _(step):
        plane = me.plane(3 - step)
        fill_hits(ranks, plane, hits, cap)
        csend[pl.ds(pl.multiple_of(plane * 4 * cap, 4 * cap), 4 * cap), :] = mm(hits[...], cot[...]).astype(BF)
        for k in range(4):
            p = plane * 4 + k

            @pl.when(p != me.number)
            def _():
                cot_copy(p).start()

            @pl.when(p == me.number)
            def _():
                own_copy.start()

    forwards = []
    for d in range(1, 4):
        dense_copies[d - 1].wait()
        source = (s - d + 4) % 4
        place = pl.ds(pl.multiple_of(source * quarter + c * half, half), half)
        cp = remote(dense.at[place], dense.at[place], dfsem.at[0, d], dfsem.at[1, d], me.sibling)
        cp.start()
        forwards.append(cp)

    in_quarters = Quarters(me, w1, lambda q: wfull.at[q], wsem, wrecv, wloc, fsem)
    out_quarters = Quarters(me, w2, lambda q: wfull2.at[q], wsem2, wrecv2, wloc2, fsem2)

    for cp in forwards:
        cp.wait()
    in_quarters.start()
    out_quarters.start()

    flat = jnp.transpose(dense[:, 3072:3200].astype(F32))
    aux[...] = flat[0:32, :]

    @pl.loop(0, images)
    def _(i):
        r = pl.ds(pl.multiple_of(i * SEQ_PAD, SEQ_PAD), SEQ_PAD)
        hat, _unused = norm_stats(tok[r, :].astype(F32))
        low[r, :] = (hat * aux[16:17, :]).astype(BF)

    @pl.loop(0, 3)
    def _(n):
        columns = pl.ds(pl.multiple_of(n * D, D), D)
        qkv[:, columns] = mm(low[...], dense[:, columns]).astype(BF)

    attention_forward(qkv, att, lse, images)

    wproj = dense.at[:, 2304:3072]
    @pl.loop(0, images)
    def _(i):
        r = pl.ds(pl.multiple_of(i * SEQ_PAD, SEQ_PAD), SEQ_PAD)
        hidden = tok[r, :].astype(F32) + mm(att[r, :], wproj[...])
        hid[r, :] = hidden
        hat, _unused = norm_stats(hidden)
        low[r, :] = (hat * aux[17:18, :]).astype(BF)

    logits = mm_nt(aux[0:16, :].astype(BF), low[...])
    masked = jnp.where(hit, logits, -1e30)
    weights = jnp.where(hit, jnp.exp(masked - jnp.max(masked, axis=0, keepdims=True)), 0.0)
    gate_t[...] = weights / jnp.maximum(jnp.sum(weights, axis=0, keepdims=True), 0.5)
    gsend[...] = jnp.zeros_like(gsend)

    far = me.plane(3)

    def far_copy(k):
        return remote(
            xsend.at[pl.ds(pl.multiple_of((far * 4 + k) * cap, cap), cap)],
            xfar.at[pl.ds(pl.multiple_of(s * cap, cap), cap)],
            xsem.at[0, k], xsem.at[1, s], me.peer(far * 4 + k),
        )

    @pl.loop(0, 4)
    def _(step):
        plane = me.plane(3 - step)
        fill_hits(ranks, plane, hits, cap)
        xsend[pl.ds(pl.multiple_of(plane * 4 * cap, 4 * cap), 4 * cap), :] = mm(hits[...], low[...]).astype(BF)

        @pl.when(step == 0)
        def _():
            for k in range(4):
                far_copy(k).start()

        for k in range(4):
            row = mm_nt(three_rows(gate_t[pl.ds(plane * 4 + k, 1), :]), hits[k * cap : (k + 1) * cap, :])
            gsend[plane * 4 + k, :, 0:cap] = jnp.broadcast_to(jnp.sum(row, axis=0, keepdims=True), (8, cap))

    saves = [
        pltpu.make_async_copy(held, place, ssem.at[n])
        for n, (held, place) in enumerate(
            ((qkv, qkv_out), (att, att_out), (hid, hid_out), (dense, dense_out), (xsend, xsend_out))
        )
    ]
    for cp in saves:
        cp.start()

    in_quarters.forward()
    out_quarters.forward()
    in_quarters.finish()
    out_quarters.finish()
    for d in range(1, 16):
        p = (me.number + d) % 16
        cot_copy(p).wait_send()
        remote(
            csend.at[pl.ds(0, cap)], cotr.at[pl.ds(0, cap)], csem.at[0, p], csem.at[1, p], me.peer(p)
        ).wait_recv()
    own_copy.wait()
    for k in range(4):
        far_copy(k).wait_send()
        remote(
            xsend.at[pl.ds(0, cap)], xfar.at[pl.ds(k * cap, cap)], xsem.at[0, k], xsem.at[1, k], me.peer(far * 4 + k)
        ).wait_recv()
    for cp in saves:
        cp.wait()


def attention_forward(qkv, att, lse, images):
    first = lax.broadcasted_iota(jnp.int32, (SEQ_PAD, 128), 1) < HEAD
    lane = lax.broadcasted_iota(jnp.int32, (SEQ_PAD, 128), 1)
    real = lax.broadcasted_iota(jnp.int32, (SEQ_PAD, SEQ_PAD), 1) < SEQ
    lse[...] = jnp.zeros_like(lse)

    @pl.loop(0, HEADS // 2)
    def _(pair):
        for i in range(images):
            r = slice(i * SEQ_PAD, (i + 1) * SEQ_PAD)
            cols = [pl.ds(pl.multiple_of(part * D + pair * 128, 128), 128) for part in range(3)]
            q, k, v = (qkv[r, cols[part]] for part in range(3))
            outs, lses = [], []
            for h in range(2):
                mine = first if h == 0 else jnp.logical_not(first)
                qh = (jnp.where(mine, q.astype(F32), 0.0) * 0.125).astype(BF)
                scores = jnp.where(real, mm_nt(qh, k), -1e30)
                top = jnp.max(scores, axis=1, keepdims=True)
                weights = jnp.exp(scores - top)
                total = jnp.sum(weights, axis=1, keepdims=True)
                lses.append(top + jnp.log(total))
                outs.append(mm((weights * (1.0 / total)).astype(BF), v))
            att[r, pl.ds(pl.multiple_of(pair * 128, 128), 128)] = jnp.where(first, outs[0], outs[1]).astype(BF)
            old = lse[r, :]
            lse[r, :] = jnp.where(lane == 2 * pair, lses[0], jnp.where(lane == 2 * pair + 1, lses[1], old))


def kernel_e(
    cap, xsend, gsend, cotr, wfull, wfull2, xfar,
    outs, ginh, ginb, ggb, gw, outn,
    w1v, w2v, xr, gcot, gater, act, gpre, acc, stage, ggs, gcol,
    xsem, gsem, rsem, ggsem, lsem, wlsem, stsem, nsem,
):
    me = Place()
    z, c, s = me.z, me.core, me.shard
    greet(me.peers())
    block = 4 * cap

    def part(ref, p):
        return ref.at[pl.ds(pl.multiple_of(p * cap, cap), cap)]

    def x_copy(p):
        return remote(part(xsend, p), part(xr, me.number), xsem.at[0, p], xsem.at[1, me.number], me.peer(p))

    def g_copy(p):
        return remote(gsend.at[p], gater.at[me.number], gsem.at[0, p], gsem.at[1, me.number], me.peer(p))

    def r_copy(p):
        return remote(part(ginh, p), part(ginb, me.number), rsem.at[0, p], rsem.at[1, me.number], me.peer(p))

    def n_copy(p):
        return remote(part(outs, p), part(outn, me.number), nsem.at[0, p], nsem.at[1, me.number], me.peer(p))

    def gg_copy(p):
        return remote(ggs.at[p], ggb.at[me.number], ggsem.at[0, p], ggsem.at[1, me.number], me.peer(p))

    local_copies = [
        pltpu.make_async_copy(part(xsend, me.number), part(xr, me.number), lsem.at[0]),
        pltpu.make_async_copy(gsend.at[me.number], gater.at[me.number], lsem.at[1]),
        pltpu.make_async_copy(cotr, gcot, lsem.at[2]),
    ]
    own_r = pltpu.make_async_copy(part(ginh, me.number), part(ginb, me.number), lsem.at[3])
    own_g = pltpu.make_async_copy(ggs.at[me.number], ggb.at[me.number], lsem.at[4])
    own_n = pltpu.make_async_copy(part(outs, me.number), part(outn, me.number), lsem.at[5])
    far = me.plane(3)
    far_rows = pl.ds(pl.multiple_of(far * block, block), block)
    w_copies = [
        pltpu.make_async_copy(wfull, w1v, wlsem.at[0]), pltpu.make_async_copy(xfar, xr.at[far_rows], wlsem.at[5])
    ] + [pltpu.make_async_copy(wfull2.at[f], w2v.at[pl.ds(f * D, D)], wlsem.at[1 + f]) for f in range(4)]
    for step in (2, 1, 0):
        for k in range(4):
            p = me.plane(step) * 4 + k

            @pl.when(p != me.number)
            def _():
                x_copy(p).start()

    for d in range(1, 16):
        g_copy((me.number + d) % 16).start()
    for cp in local_copies + w_copies:
        cp.start()
    ggs[...] = jnp.zeros_like(ggs)
    for cp in local_copies + w_copies:
        cp.wait()

    eye = lax.broadcasted_iota(jnp.int32, (cap, cap), 0) == lax.broadcasted_iota(jnp.int32, (cap, cap), 1)

    def recv_block(plane):
        for k in range(4):
            p = plane * 4 + k

            @pl.when(p != me.number)
            def _():
                @pl.when(plane != far)
                def _():
                    remote(part(xsend, p), part(xr, p), xsem.at[0, p], xsem.at[1, p], me.peer(p)).wait_recv()

                remote(gsend.at[p], gater.at[p], gsem.at[0, p], gsem.at[1, p], me.peer(p)).wait_recv()

    def stage_out(plane, which):
        return pltpu.make_async_copy(
            stage.at[which], (outs if which == 0 else ginh).at[pl.ds(pl.multiple_of(plane * block, block), block)],
            stsem.at[which],
        )

    def first_half(step):
        plane = me.plane(step)
        recv_block(plane)
        r = pl.ds(pl.multiple_of(plane * block, block), block)

        @pl.loop(0, 4)
        def _(f):
            for n in range(3):
                cols = pl.ds(pl.multiple_of(f * D + n * 256, 256), 256)
                pre = mm(xr[r, :], w1v[f, :, n * 256 : (n + 1) * 256])
                square = pre * pre
                t = jnp.tanh(pre * (GELU_A + GELU_A * GELU_B * square))
                half = 0.5 + 0.5 * t
                act[r, cols] = (pre * half).astype(BF)
                slope = half + (0.5 * pre) * (1.0 - t * t) * (GELU_A + 3.0 * GELU_A * GELU_B * square)
                gpre[r, cols] = slope.astype(BF)

    @pl.loop(0, 4)
    def _(turn):
        step = (turn + 3) % 4
        first_half(step)
        plane = me.plane(step)
        r = pl.ds(pl.multiple_of(plane * block, block), block)
        acc[...] = mm(act[r, :], w2v[...])

        for k in range(4):
            row = gater[plane * 4 + k, 0:1, 0:cap]
            column = jnp.sum(jnp.where(eye, row, 0.0), axis=1, keepdims=True)
            gcol[k * cap : (k + 1) * cap, :] = jnp.broadcast_to(column, (cap, 128))

        for k in range(4):
            rk = pl.ds(pl.multiple_of(plane * block + k * cap, cap), cap)
            kk = slice(k * cap, (k + 1) * cap)
            out = acc[kk, :].astype(BF).astype(F32)
            gate = gcol[kk, 0:1]
            g = gcot[rk, :].astype(F32)
            dots = jnp.sum(g * out, axis=1, keepdims=True)
            row = jnp.sum(jnp.where(eye, dots, 0.0), axis=0, keepdims=True)
            ggs[plane * 4 + k, :, 0:cap] = jnp.broadcast_to(row, (8, cap))
            stage[0, kk, :] = (gate * out).astype(BF)
            gcot[rk, :] = (gate * g).astype(BF)
        stage_out(plane, 0).start()

        @pl.loop(0, 4)
        def _(f):
            for n in range(3):
                cols = pl.ds(pl.multiple_of(f * D + n * 256, 256), 256)
                ga = mm_nt(gcot[r, :], w2v[cols, :])
                gpre[r, cols] = (ga * gpre[r, cols].astype(F32)).astype(BF)

        acc[...] = mm_nt(gpre[r, 0:D], w1v[0])
        for f in range(1, 4):
            acc[...] += mm_nt(gpre[r, f * D : (f + 1) * D], w1v[f])
        stage[1] = acc[...].astype(BF)
        stage_out(plane, 1).start()
        stage_out(plane, 1).wait()
        for k in range(4):
            p = plane * 4 + k

            @pl.when(p != me.number)
            def _():
                r_copy(p).start()
                gg_copy(p).start()

            @pl.when(p == me.number)
            def _():
                own_r.start()
                own_g.start()

        stage_out(plane, 0).wait()

        @pl.when(step < 2)
        def _():
            for k in range(4):
                p = plane * 4 + k

                @pl.when(p != me.number)
                def _():
                    n_copy(p).start()

                @pl.when(p == me.number)
                def _():
                    own_n.start()


    @pl.loop(0, 4)
    def _(f):
        cols = pl.ds(pl.multiple_of(f * D, D), D)
        w1v[f] = mm_tn(xr[...], gpre[:, cols]).astype(BF)
        w2v[cols, :] = mm_tn(act[:, cols], gcot[...]).astype(BF)

    out_w = [pltpu.make_async_copy(w1v, gw.at[0], wlsem.at[0])] + [
        pltpu.make_async_copy(w2v.at[pl.ds(f * D, D)], gw.at[1, f], wlsem.at[1 + f]) for f in range(4)
    ]
    for cp in out_w:
        cp.start()
    for d in range(1, 16):
        p = (me.number + d) % 16

        @pl.when(p // 4 != far)
        def _():
            x_copy(p).wait_send()

        g_copy(p).wait_send()
        r_copy(p).wait_send()
        gg_copy(p).wait_send()
        remote(part(ginh, p), part(ginb, p), rsem.at[0, p], rsem.at[1, p], me.peer(p)).wait_recv()
        remote(ggs.at[p], ggb.at[p], ggsem.at[0, p], ggsem.at[1, p], me.peer(p)).wait_recv()
    own_r.wait()
    own_g.wait()
    own_n.wait()
    for step in range(2):
        for k in range(4):
            p = me.plane(step) * 4 + k

            @pl.when(p != me.number)
            def _():
                n_copy(p).wait_send()
                remote(part(outs, p), part(outn, p), nsem.at[0, p], nsem.at[1, p], me.peer(p)).wait_recv()

    for cp in out_w:
        cp.wait()


def attention_backward(qkv, gatt, lse, gqkv, images, group):
    first = lax.broadcasted_iota(jnp.int32, (SEQ_PAD, 128), 1) < HEAD
    lane = lax.broadcasted_iota(jnp.int32, (SEQ_PAD, 128), 1)
    real = lax.broadcasted_iota(jnp.int32, (SEQ_PAD, SEQ_PAD), 1) < SEQ

    @pl.loop(0, 2)
    def _(near):
        pair = 2 * group + near
        for i in range(images):
            r = slice(i * SEQ_PAD, (i + 1) * SEQ_PAD)
            cols = [pl.ds(pl.multiple_of(part * D + pair * 128, 128), 128) for part in range(3)]
            q, k, v = (qkv[r, cols[part]] for part in range(3))
            g = gatt[r, pl.ds(pl.multiple_of(pair * 128, 128), 128)]
            logs = lse[r, :]
            parts = []
            for h in range(2):
                mine = first if h == 0 else jnp.logical_not(first)
                qh = (jnp.where(mine, q.astype(F32), 0.0) * 0.125).astype(BF)
                gh = jnp.where(mine, g.astype(F32), 0.0).astype(BF)
                log = jnp.sum(jnp.where(lane == 2 * pair + h, logs, 0.0), axis=1, keepdims=True)
                probs = jnp.where(real, jnp.exp(mm_nt(qh, k) - log), 0.0)
                grad_probs = mm_nt(gh, v)
                low = probs.astype(BF)
                delta = jnp.sum(probs * grad_probs, axis=1, keepdims=True)
                grad_scores = (probs * (grad_probs - delta)).astype(BF)
                parts.append((mm(grad_scores, k) * 0.125, mm_tn(grad_scores, q) * 0.125, mm_tn(low, g)))
            for part in range(3):
                place = pl.ds(pl.multiple_of(group * D + part * 256 + near * 128, 128), 128)
                gqkv[r, place] = jnp.where(first, parts[0][part], parts[1][part]).astype(BF)


def kernel_b(
    cap, tok, cot, aux, lse, gate_t, ranks, ggb, dense_in, qkv_in, att_in, hid_in, ginb, outs, gw, outn,
    block_out, gtok, ghat, extra, outb, eg,
    dense, qkv, att, hid, hsem, rowsv, hits, gmoe, low, glow, gatt, gqkv, gd, ra, rb, sc, rc, exs, exl, gx, own_w, ggt,
    osem, lsem, wxsem, wsem, wload, wlocal, asem, bsem, zsem, fsem, esem, xsem,
):
    me = Place()
    z, c, s = me.z, me.core, me.shard
    rows = tok.shape[0]
    images = rows // SEQ_PAD
    block = 4 * cap
    quarter, wide, deep = D // 4, D // 2, D // 16
    greet(me.peers() + [(z * 2 + 1 - c, t) for t in range(4)])

    def part(ref, p):
        return ref.at[pl.ds(pl.multiple_of(p * cap, cap), cap)]

    def o_copy(p):
        return remote(part(outs, p), part(outb, me.number), osem.at[0, p], osem.at[1, me.number], me.peer(p))

    load_in = pltpu.make_async_copy(ginb, rowsv, lsem.at[0])
    load_in.start()
    held = [
        pltpu.make_async_copy(place, ref, hsem.at[n])
        for n, (place, ref) in enumerate(((hid_in, hid), (att_in, att), (dense_in, dense), (qkv_in, qkv)))
    ]
    swap = [remote(gw.at[1 - c, t], gx.at[t], wxsem.at[0, t], wxsem.at[1, t], me.sibling) for t in range(4)]
    for cp in swap:
        cp.start()

    def send_outs(step):
        for k in range(4):
            o_copy(me.plane(step) * 4 + k).start()

    send_outs(3)
    send_outs(2)
    for cp in held:
        cp.start()

    load_in.wait()
    gmoe[...] = jnp.zeros_like(gmoe)

    @pl.loop(0, 4)
    def _(plane):
        fill_hits(ranks, plane, hits, cap)
        for k in range(4):
            rows8 = three_rows(ggb[plane * 4 + k, 0:1, 0:cap])
            row = mm(rows8, hits[k * cap : (k + 1) * cap, :])
            ggt[pl.ds(plane * 4 + k, 1), :] = jnp.sum(row, axis=0, keepdims=True)
        r = pl.ds(pl.multiple_of(plane * block, block), block)
        gmoe[...] += mm_tn(hits[...], rowsv[r, :])

    for cp in held:
        cp.wait()
    gates = gate_t[...]
    grad_gates = ggt[...]
    grad_logits = gates * (grad_gates - jnp.sum(gates * grad_gates, axis=0, keepdims=True))
    gl_high = grad_logits.astype(BF)
    gl_low = (grad_logits - gl_high.astype(F32)).astype(BF)

    @pl.loop(0, images)
    def _(i):
        r = pl.ds(pl.multiple_of(i * SEQ_PAD, SEQ_PAD), SEQ_PAD)
        hat, _unused = norm_stats(hid[r, :])
        low[r, :] = (hat * aux[17:18, :]).astype(BF)

    router = aux[0:16, :].astype(BF)
    gmoe[...] += mm_tn(gl_high, router) + mm_tn(gl_low, router)
    exs[0, 0:16, :] = mm(gl_high, low[...]) + mm(gl_low, low[...])
    exs[0, 16:32, :] = jnp.zeros((16, D), F32)

    @pl.loop(0, images)
    def _(i):
        r = pl.ds(pl.multiple_of(i * SEQ_PAD, SEQ_PAD), SEQ_PAD)
        hat, inv = norm_stats(hid[r, :])
        w = gmoe[r, :]
        scaled = w * aux[17:18, :]
        back = inv * (
            scaled - jnp.mean(scaled, axis=-1, keepdims=True) - hat * jnp.mean(scaled * hat, axis=-1, keepdims=True)
        )
        grad = cot[r, :].astype(F32) + back
        gtok[r, :] = grad
        glow[r, :] = grad.astype(BF)
        exs[0, 17:18, :] += jnp.sum(w * hat, axis=0, keepdims=True)
        hat, _unused = norm_stats(tok[r, :].astype(F32))
        low[r, :] = (hat * aux[16:17, :]).astype(BF)

    def put(group, value):
        for t in range(4):
            for h in range(2):
                gd[group, t, h] = value[t * quarter : (t + 1) * quarter, h * wide : (h + 1) * wide].astype(BF)

    def stage_a(g):
        return [
            remote(gd.at[g, t, 1 - c], ra.at[g, t], asem.at[0, g, t], asem.at[1, g, t], me.sibling) for t in range(4)
        ]

    def stage_b(g):
        return [
            remote(
                gd.at[g, (s + d) % 4, c], rb.at[g, d], bsem.at[0, g, d], bsem.at[1, g, d], (z * 2 + c, (s + d) % 4)
            )
            for d in range(1, 4)
        ]

    def stage_c(g):
        return [
            remote(
                sc.at[g, pl.ds(pl.multiple_of((z + d) % 4 * deep, deep), deep)], rc.at[g, d],
                zsem.at[0, g, d], zsem.at[1, g, d], ((z + d) % 4 * 2 + c, s),
            )
            for d in range(1, 4)
        ]

    my_rows = pl.ds(pl.multiple_of(z * deep, deep), deep)

    def stage_d(g):
        return [
            remote(
                ghat.at[g, c, my_rows], ghat.at[g, c, my_rows],
                fsem.at[0, g, d], fsem.at[1, g, d], ((z + d) % 4 * 2 + c, s),
            )
            for d in range(1, 4)
        ]

    def stage_e(g):
        return [remote(ghat.at[g, c], ghat.at[g, c], esem.at[0, g], esem.at[1, g], me.sibling)]

    def start(copies):
        for cp in copies:
            cp.start()

    def finish(copies):
        for cp in copies:
            cp.wait()

    def to_b(g):
        finish(stage_a(g))
        for t in range(4):
            gd[g, t, c] = (gd[g, t, c].astype(F32) + ra[g, t].astype(F32)).astype(BF)
        start(stage_b(g))

    def to_c(g):
        finish(stage_b(g))
        sc[g] = (
            (gd[g, s, c].astype(F32) + rb[g, 1].astype(F32)) + (rb[g, 2].astype(F32) + rb[g, 3].astype(F32))
        ).astype(BF)
        start(stage_c(g))

    def to_d(g):
        finish(stage_c(g))
        ghat[g, c, my_rows, :] = (
            (sc[g, my_rows, :].astype(F32) + rc[g, 1].astype(F32)) + (rc[g, 2].astype(F32) + rc[g, 3].astype(F32))
        ).astype(BF)
        start(stage_d(g))

    def to_e(g):
        finish(stage_d(g))
        start(stage_e(g))

    put(3, mm_tn(att[...], glow[...]))
    start(stage_a(3))
    gatt[...] = mm_nt(glow[...], dense[:, 2304:3072]).astype(BF)

    def owner_copy(t):
        return remote(
            gx.at[t], eg.at[s % 2, c], wsem.at[0, t], wsem.at[1, s % 2 * 2 + c], (z * 2 + s // 2, t)
        )

    mine_local = s // 2 == c
    owner_local = pltpu.make_async_copy(gx.at[s], eg.at[s % 2, c], wlocal)
    def to_owner(t):
        load = pltpu.make_async_copy(gw.at[c, t], own_w, wload)
        load.start()
        load.wait()
        remote(gw.at[1 - c, t], gx.at[t], wxsem.at[0, t], wxsem.at[1, t], me.sibling).wait()
        gx[t] = (gx[t].astype(F32) + own_w[...].astype(F32)).astype(BF)

        @pl.when(jnp.logical_not(mine_local & (s == t)))
        def _():
            owner_copy(t).start()

        @pl.when(mine_local & (s == t))
        def _():
            owner_local.start()

    for d in (1, 2, 3, 0):
        to_owner((s + d) % 4)
    to_b(3)
    for g in range(3):
        attention_backward(qkv, gatt, lse, gqkv, images, g)
        put(g, mm_tn(low[...], gqkv[:, g * D : (g + 1) * D]))
        start(stage_a(g))
        partial = [
            mm_nt(gqkv[:, g * D + 256 * n : g * D + 256 * (n + 1)], dense[:, n * D + g * 256 : n * D + (g + 1) * 256])
            for n in range(3)
        ]
        if g == 0:
            gmoe[...] = (partial[0] + partial[1]) + partial[2]
        else:
            gmoe[...] += (partial[0] + partial[1]) + partial[2]
            to_b(g - 1)

    @pl.loop(0, images)
    def _(i):
        r = pl.ds(pl.multiple_of(i * SEQ_PAD, SEQ_PAD), SEQ_PAD)
        hat, inv = norm_stats(tok[r, :].astype(F32))
        w = gmoe[r, :]
        scaled = w * aux[16:17, :]
        gtok[r, :] += inv * (
            scaled - jnp.mean(scaled, axis=-1, keepdims=True) - hat * jnp.mean(scaled * hat, axis=-1, keepdims=True)
        )
        exs[0, 16:17, :] += jnp.sum(w * hat, axis=0, keepdims=True)

    def add_outputs(source, step):
        plane = me.plane(step)
        r = pl.ds(pl.multiple_of(plane * block, block), block)
        load = pltpu.make_async_copy(source.at[r], rowsv.at[r], lsem.at[0])
        load.start()
        fill_hits(ranks, plane, hits, cap)
        load.wait()
        gmoe[...] += mm_tn(hits[...], rowsv[r, :])

    to_b(2)
    x_first = remote(exs.at[0], exl.at[0], xsem.at[0, 0], xsem.at[1, 0], me.sibling)
    x_first.start()
    gmoe[...] = hid[...]
    add_outputs(outn, 0)
    add_outputs(outn, 1)
    to_c(3)
    x_first.wait()
    exs[1] = exs[0] + exl[0]
    exl[1 + s] = exs[1]
    x_second = [
        remote(exs.at[1], exl.at[1 + s], xsem.at[0, d], xsem.at[1, d], (z * 2 + c, (s + d) % 4)) for d in range(1, 4)
    ]
    start(x_second)
    to_c(0)
    to_c(1)
    to_c(2)
    finish(x_second)
    exs[2] = (exl[1] + exl[2]) + (exl[3] + exl[4])
    exl[5 + z] = exs[2]
    x_third = [
        remote(exs.at[2], exl.at[5 + z], xsem.at[0, 3 + d], xsem.at[1, 3 + d], ((z + d) % 4 * 2 + c, s))
        for d in range(1, 4)
    ]
    start(x_third)
    for g in (3, 0, 1, 2):
        to_d(g)
    finish(x_third)
    extra[...] = (exl[5] + exl[6]) + (exl[7] + exl[8])
    for g in (3, 0, 1, 2):
        to_e(g)

    for step in (2, 3):
        for k in range(4):
            p = me.plane(step) * 4 + k
            o_copy(p).wait_send()
            remote(part(outs, p), part(outb, p), osem.at[0, p], osem.at[1, p], me.peer(p)).wait_recv()
        add_outputs(outb, step)

    block_out[...] = gmoe[...].astype(BF)

    for t in range(4):
        @pl.when(jnp.logical_not(mine_local & (s == t)))
        def _():
            owner_copy(t).wait_send()

        @pl.when(mine_local & (s == t))
        def _():
            owner_local.wait()

    for i in range(2):
        for a in range(2):
            own = (a == c) & (s == 2 * c + i)

            @pl.when(jnp.logical_not(own))
            def _():
                remote(gx.at[0], eg.at[i, a], wsem.at[0, 0], wsem.at[1, i * 2 + a], me.sibling).wait_recv()

    for g in range(4):
        finish(stage_e(g))


def lane_sums(values, count):
    lane = lax.broadcasted_iota(jnp.int32, (1, count), 1)
    out = jnp.zeros((1, count), F32)
    for n, value in enumerate(values):
        out = jnp.where(lane == n, value, out)
    return out


def total(values):
    return jnp.sum(jnp.sum(values, axis=1, keepdims=True), axis=0, keepdims=True)


def set_columns(ref, columns):
    lane = lax.broadcasted_iota(jnp.int32, ref.shape, 1)
    out = jnp.zeros(ref.shape, F32)
    for n, column in enumerate(columns):
        out = jnp.where(lane == n, column, out)
    ref[...] = out


def pick(row, n):
    lane = lax.broadcasted_iota(jnp.int32, row.shape, 1)
    return jnp.sum(jnp.where(lane == n, row, 0.0), axis=1, keepdims=True)


def mean_square(square_sum, weight_sum, size):
    rms = jnp.sqrt(square_sum * (1.0 / size))
    return rms, -RATE * jnp.sqrt(weight_sum * (1.0 / size)) / jnp.maximum(CLIP, rms)


def kernel_s(
    eg, ghat, extra, w1, w2, dsh, gains, moments, rows3, row_router, v_gain,
    mine_new, v_new, rows3_new, row_router_new, moments_new, sums, sums_r,
    egv, tall, turned, stats, landed, stats_r, landed_r, dgrad,
    isem, xsem, rsem,
):
    me = Place()
    z, c, s = me.z, me.core, me.shard
    quarter = dsh.shape[0]
    load = pltpu.make_async_copy(eg, egv, isem)
    load.start()
    greet(me.mates())

    read_dense(ghat, dgrad)
    mine = jnp.zeros((32, quarter), F32)
    for t in range(4):
        mine = mine + jnp.where(s == t, extra[:, t * quarter : (t + 1) * quarter], 0.0)
    mine_new[...] = mine
    router = mine[0:16, :]
    gain = mine[16:18, :]
    v = DECAY * v_gain[...] + (1.0 - DECAY) * (gain * gain + EPS_SQUARE)
    v_new[...] = v
    raw_gain = gain * lax.rsqrt(v)
    gain_weight = gains[...].astype(F32)
    gain_square = jnp.sum(raw_gain * raw_gain, axis=1, keepdims=True)
    gain_size = jnp.sum(gain_weight * gain_weight, axis=1, keepdims=True)
    router_square = router * router
    router_row = DECAY * row_router[...] + (1.0 - DECAY) * (
        jnp.sum(router_square, axis=0, keepdims=True) * (1.0 / 16) + EPS_SQUARE
    )
    row_router_new[...] = router_row
    set_columns(
        stats_r,
        [
            jnp.sum(router_square, axis=1, keepdims=True) + quarter * EPS_SQUARE,
            jnp.sum(router_square * (1.0 / router_row), axis=1, keepdims=True),
        ],
    )
    router_weight = dsh[:, 4 * D : 4 * D + 16].astype(F32)
    qkv_square = dgrad[:, : 3 * D] * dgrad[:, : 3 * D]
    proj_square = dgrad[:, 3 * D :] * dgrad[:, 3 * D :]
    row_qkv = DECAY * rows3[:, 0:1] + (1.0 - DECAY) * (
        jnp.sum(qkv_square, axis=1, keepdims=True) * (1.0 / (3 * D)) + EPS_SQUARE
    )
    row_proj = DECAY * rows3[:, 1:2] + (1.0 - DECAY) * (
        jnp.sum(proj_square, axis=1, keepdims=True) * (1.0 / D) + EPS_SQUARE
    )
    rows3_new[...] = jnp.where(lax.broadcasted_iota(jnp.int32, rows3_new.shape, 1) == 0, row_qkv, row_proj)
    inv_qkv, inv_proj = 1.0 / row_qkv, 1.0 / row_proj
    for g in range(4):
        square, inv = (qkv_square[:, g * D : (g + 1) * D], inv_qkv) if g < 3 else (proj_square, inv_proj)
        stats[8 + g : 9 + g, :] = jnp.sum(square, axis=0, keepdims=True) + quarter * EPS_SQUARE
        stats[12 + g : 13 + g, :] = jnp.sum(square * inv, axis=0, keepdims=True)
    dense_weight = dsh[:, : 4 * D].astype(F32)
    sizes = [
        total(row_qkv), total(row_proj), total(router_row),
        total(dense_weight[:, : 3 * D] * dense_weight[:, : 3 * D]),
        total(dense_weight[:, 3 * D :] * dense_weight[:, 3 * D :]),
        total(router_weight * router_weight),
        gain_square[0:1], gain_square[1:2], gain_size[0:1], gain_size[1:2],
    ]

    tall[...] = jnp.zeros_like(tall)
    turned[...] = jnp.zeros_like(turned)
    turned[0:8, :] = moments[...]
    moment_columns = jnp.transpose(turned[...])
    load.wait()
    columns = []
    for i in range(2):
        grad = egv[i, 0].astype(F32)
        square = grad * grad
        col = DECAY * moments[2 + i : 3 + i, :] + (1.0 - DECAY) * (
            jnp.sum(square, axis=0, keepdims=True) * (1.0 / D) + EPS_SQUARE
        )
        moments_new[2 + i : 3 + i, :] = col
        columns.append(jnp.sum(square, axis=1, keepdims=True) + D * EPS_SQUARE)
        columns.append(jnp.sum(square * (1.0 / col), axis=1, keepdims=True))
        weight = w1[i].astype(F32)
        sizes.append(total(weight * weight))
    for i in range(2):
        grad = egv[i, 1].astype(F32)
        square = grad * grad
        row = DECAY * moment_columns[:, 4 + i : 5 + i] + (1.0 - DECAY) * (
            jnp.sum(square, axis=1, keepdims=True) * (1.0 / D) + EPS_SQUARE
        )
        columns.append(row)
        stats[4 + i : 5 + i, :] = jnp.sum(square, axis=0, keepdims=True) + D * EPS_SQUARE
        stats[6 + i : 7 + i, :] = jnp.sum(square * (1.0 / row), axis=0, keepdims=True)
        weight = w2[i].astype(F32)
        sizes.append(total(weight * weight))
        sizes.append(total(row))
    set_columns(tall, columns)
    flat = jnp.transpose(tall[...])
    for n, m in ((0, 0), (2, 1), (1, 2), (3, 3)):
        stats[m : m + 1, :] = flat[n : n + 1, :]
    moments_new[0:2, :] = flat[4:6, :]
    moments_new[4:8, :] = jnp.zeros((4, D), F32)
    stats[16:24, :] = jnp.zeros((8, D), F32)
    stats[16:17, :] = lane_sums(sizes, D)

    landed[s] = stats[...]
    landed_r[s] = stats_r[...]
    copies = []
    for d in range(1, 4):
        mate = (z * 2 + c, (s + d) % 4)
        copies.append(remote(stats, landed.at[s], xsem.at[0, d], xsem.at[1, d], mate))
        copies.append(remote(stats_r, landed_r.at[s], rsem.at[0, d], rsem.at[1, d], mate))
    for cp in copies:
        cp.start()
    for cp in copies:
        cp.wait()
    sums[...] = (landed[0] + landed[1]) + (landed[2] + landed[3])
    sums_r[...] = (landed_r[0] + landed_r[1]) + (landed_r[2] + landed_r[3])


def read_dense(ghat, dgrad):
    for g in range(4):
        for n in range(6):
            column = 3 * D + 128 * n if g == 3 else n // 2 * D + g * 256 + n % 2 * 128
            dgrad[:, column : column + 128] = ghat[g, n // 3, :, n % 3 * 128 : n % 3 * 128 + 128].astype(F32)


def kernel_u(
    eg, ghat, mine, w1, w2, dsh, gains, moments, moments_mid, rows3, row_router, cols, col_router, v, sums, sums_r,
    g_first, g_second, n_first, n_second, dense_rms, expert_rms, n_gain, g_qkv, n_qkv, g_proj, n_proj, n_router,
    cols_new, col_router_new, row_in_new, col_out_new,
    egv, grads, news, turned, tall_d, dgrad,
    isem, gsem, nsem,
):
    quarter = dsh.shape[0]
    load = pltpu.make_async_copy(eg, egv, isem)
    load.start()
    read_dense(ghat, dgrad)
    g_qkv[...] = dgrad[:, : 3 * D]
    g_proj[...] = dgrad[:, 3 * D :]
    router, gain = mine[0:16, :], mine[16:18, :]
    raw_gain = gain * lax.rsqrt(v[...])
    gain_weight = gains[...].astype(F32)
    router_row = row_router[...]
    router_weight = dsh[:, 4 * D : 4 * D + 16].astype(F32)
    row_qkv, row_proj = rows3[:, 0:1], rows3[:, 1:2]
    scalars = sums[16:17, :]
    one = lambda n: pick(scalars, n)
    load.wait()

    hidden = 4.0 * D
    row_in = DECAY * moments[0:2, :] + (1.0 - DECAY) * (sums[0:2, :] * (1.0 / hidden))
    row_in_new[...] = row_in
    col_out = DECAY * moments[6:8, :] + (1.0 - DECAY) * (sums[4:6, :] * (1.0 / hidden))
    col_out_new[...] = col_out
    turned[...] = jnp.zeros_like(turned)
    turned[0:2, :] = row_in
    turned[2:4, :] = moments_mid[0:2, :]
    back = jnp.transpose(turned[...])
    rms_all = []
    for i in range(2):
        r = row_in[i : i + 1, :]
        mean = jnp.sum(r, axis=1, keepdims=True) * (1.0 / D)
        raw = mean * jnp.sum(sums[2 + i : 3 + i, :] / r, axis=1, keepdims=True)
        rms, factor = mean_square(raw, one(10 + i), D * hidden)
        rms_all.append(rms)
        left = factor * lax.rsqrt(back[:, i : i + 1] / mean)
        grads[i] = egv[i, 0].astype(F32)
        pltpu.make_async_copy(grads.at[i], g_first.at[i], gsem.at[i]).start()
        news[i] = w1[i].astype(F32) + grads[i] * left * lax.rsqrt(moments_mid[2 + i : 3 + i, :])
        pltpu.make_async_copy(news.at[i], n_first.at[i], nsem.at[i]).start()
    for i in range(2):
        col = col_out[i : i + 1, :]
        mean = one(13 + 2 * i) * (1.0 / hidden)
        raw = mean * jnp.sum(sums[6 + i : 7 + i, :] / col, axis=1, keepdims=True)
        rms, factor = mean_square(raw, one(12 + 2 * i), D * hidden)
        rms_all.append(rms)
        left = factor * lax.rsqrt(back[:, 2 + i : 3 + i] / mean)
        grads[2 + i] = egv[i, 1].astype(F32)
        pltpu.make_async_copy(grads.at[2 + i], g_second.at[i], gsem.at[2 + i]).start()
        news[2 + i] = w2[i].astype(F32) + grads[2 + i] * left * lax.rsqrt(col)
        pltpu.make_async_copy(news.at[2 + i], n_second.at[i], nsem.at[2 + i]).start()
    expert_rms[...] = lane_sums(rms_all, 128)

    rms_g1, factor_g1 = mean_square(one(6), one(8), D)
    rms_g2, factor_g2 = mean_square(one(7), one(9), D)
    upper = lax.broadcasted_iota(jnp.int32, gain.shape, 0) == 0
    n_gain[...] = gain_weight + jnp.where(upper, factor_g1, factor_g2) * raw_gain
    col_dense = []
    for g in range(4):
        col = DECAY * cols[g : g + 1, :] + (1.0 - DECAY) * (sums[8 + g : 9 + g, :] * (1.0 / D))
        cols_new[g : g + 1, :] = col
        col_dense.append(col)
    mean_qkv, mean_proj, mean_router = one(0) * (1.0 / D), one(1) * (1.0 / D), one(2) * (1.0 / D)
    ratio = [jnp.sum(sums[12 + g : 13 + g, :] / col_dense[g], axis=1, keepdims=True) for g in range(4)]
    rms_qkv, factor_qkv = mean_square(mean_qkv * (ratio[0] + ratio[1] + ratio[2]), one(3), 3 * D * D)
    rms_proj, factor_proj = mean_square(mean_proj * ratio[3], one(4), D * D)
    left_qkv = factor_qkv * lax.rsqrt(row_qkv / mean_qkv)
    left_proj = factor_proj * lax.rsqrt(row_proj / mean_proj)
    for g in range(4):
        part = slice(g * D, (g + 1) * D)
        new = dsh[:, part].astype(F32) + dgrad[:, part] * (left_qkv if g < 3 else left_proj) * lax.rsqrt(col_dense[g])
        if g < 3:
            n_qkv[:, part] = new
        else:
            n_proj[...] = new
    col = DECAY * col_router[...] + (1.0 - DECAY) * (sums_r[:, 0:1] * (1.0 / D))
    col_router_new[...] = col
    raw_router = mean_router * jnp.sum(sums_r[:, 1:2] / col, axis=0, keepdims=True)
    rms_router, factor_router = mean_square(raw_router, one(5), 16 * D)
    tall_d[...] = jnp.zeros_like(tall_d)
    tall_d[0:16, 0:quarter] = router * (factor_router * lax.rsqrt(router_row / mean_router)) * lax.rsqrt(col)
    n_router[...] = router_weight + jnp.transpose(tall_d[...])[0:quarter, 0:16]
    dense_rms[...] = lane_sums([rms_g1, rms_g2, rms_qkv, rms_proj, rms_router], 128)
    for i in range(2):
        pltpu.make_async_copy(news.at[i], n_first.at[i], nsem.at[i]).wait()
        pltpu.make_async_copy(news.at[2 + i], n_second.at[i], nsem.at[2 + i]).wait()
        pltpu.make_async_copy(grads.at[i], g_first.at[i], gsem.at[i]).wait()
        pltpu.make_async_copy(grads.at[2 + i], g_second.at[i], gsem.at[2 + i]).wait()


def params(number):
    return pltpu.CompilerParams(collective_id=number, has_side_effects=True, vmem_limit_bytes=VMEM_LIMIT)


def dma(*shape):
    return pltpu.SemaphoreType.DMA(shape)


def fast(
    tokens, routes, cotangent, gain_attn, w_qkv, w_proj, gain_moe, w_router, w_in, w_out,
    v_attn, v_moe, row_qkv, col_qkv, row_proj, col_proj, row_router, col_router, row_in, col_in, row_out, col_out,
):
    count = tokens.shape[0]
    images = count // SEQ
    rows = images * SEQ_PAD
    experts = w_router.shape[1]
    cap = ((3 * count + experts - 1) // experts + 15) // 16 * 16
    slots = experts * cap
    vmem = pl.BlockSpec(memory_space=pltpu.VMEM)
    hbm = pl.BlockSpec(memory_space=pl.ANY)
    shape = jax.ShapeDtypeStruct

    def padded(array, value=0):
        array = array.reshape(images, SEQ, array.shape[1])
        array = jnp.pad(array, ((0, 0), (0, SEQ_PAD - SEQ), (0, 0)), constant_values=value)
        return array.reshape(rows, array.shape[2])

    tok = padded(tokens)
    cot = padded(cotangent)
    rt = padded(routes, -1).T
    quarter = w_qkv.shape[0]
    small = jnp.concatenate([w_router, gain_attn[:, None], gain_moe[:, None]], axis=1)
    small = jnp.pad(small, ((0, 0), (0, 128 - small.shape[1])))
    dsh = jnp.concatenate([w_qkv, w_proj, small], axis=1)
    wide = dsh.shape[1]

    qkv, att, hid, lse, gate_t, ranks, aux, dense, xsend, gsend, cotr, wfull, wfull2, xfar = pl.pallas_call(
        functools.partial(kernel_a, cap),
        out_shape=(
            shape((rows, 3 * D), BF), shape((rows, D), BF), shape((rows, D), F32), shape((rows, 128), F32),
            shape((16, rows), F32), shape((16, rows), jnp.int32), shape((32, D), F32), shape((D, wide), BF),
            shape((slots, D), BF), shape((16, 8, 256), F32), shape((slots, D), BF), shape((4, D, D), BF),
            shape((4, D, D), BF), shape((4 * cap, D), BF),
        ),
        in_specs=[vmem] * 4 + [hbm] * 2,
        out_specs=(hbm,) * 3 + (vmem,) * 4 + (hbm,) * 2 + (vmem,) + (hbm,) * 4,
        scratch_shapes=[
            pltpu.VMEM((rows, 3 * D), BF), pltpu.VMEM((rows, D), BF), pltpu.VMEM((rows, D), F32),
            pltpu.VMEM((D, wide), BF), pltpu.VMEM((slots, D), BF), dma(5),
            pltpu.VMEM((slots, D), BF), pltpu.VMEM((rows, D), BF), pltpu.VMEM((4 * cap, rows), BF),
            pltpu.VMEM((rows, rows), BF), dma(2, 4), dma(2, 4), dma(2, 16), dma(2), dma(), dma(2), dma(2, 2),
            dma(2), dma(), dma(2), dma(2, 2), dma(), dma(2, 4),
        ],
        compiler_params=params(1),
        name="forward",
    )(tok, cot, rt, dsh, w_in, w_out)

    outs, ginh, ginb, ggb, gw, outn = pl.pallas_call(
        functools.partial(kernel_e, cap),
        out_shape=(
            shape((slots, D), BF), shape((slots, D), BF), shape((slots, D), BF), shape((16, 8, 256), F32),
            shape((2, 4, D, D), BF), shape((slots, D), BF),
        ),
        in_specs=[hbm, vmem, hbm, hbm, hbm, hbm],
        out_specs=(hbm, hbm, hbm, vmem, hbm, hbm),
        scratch_shapes=[
            pltpu.VMEM((4, D, D), BF), pltpu.VMEM((FF, D), BF), pltpu.VMEM((slots, D), BF), pltpu.VMEM((slots, D), BF),
            pltpu.VMEM((16, 8, 256), F32), pltpu.VMEM((slots, FF), BF), pltpu.VMEM((slots, FF), BF),
            pltpu.VMEM((4 * cap, D), F32), pltpu.VMEM((2, 4 * cap, D), BF),
            pltpu.VMEM((16, 8, 256), F32), pltpu.VMEM((4 * cap, 128), F32),
            dma(2, 16), dma(2, 16), dma(2, 16), dma(2, 16), dma(6), dma(6), dma(2), dma(2, 16),
        ],
        compiler_params=params(2),
        name="experts",
    )(xsend, gsend, cotr, wfull, wfull2, xfar)

    block_out, gtok, ghat, extra, outb, eg = pl.pallas_call(
        functools.partial(kernel_b, cap),
        out_shape=(
            shape((rows, D), BF), shape((rows, D), F32), shape((4, 2, quarter, D // 2), BF), shape((32, D), F32),
            shape((slots, D), BF), shape((2, 2, D, D), BF),
        ),
        in_specs=[vmem] * 7 + [hbm] * 8,
        out_specs=(vmem,) * 4 + (hbm,) * 2,
        scratch_shapes=[
            pltpu.VMEM((D, wide), BF), pltpu.VMEM((rows, 3 * D), BF), pltpu.VMEM((rows, D), BF),
            pltpu.VMEM((rows, D), F32), dma(4), pltpu.VMEM((slots, D), BF), pltpu.VMEM((4 * cap, rows), BF), pltpu.VMEM((rows, D), F32),
            pltpu.VMEM((rows, D), BF), pltpu.VMEM((rows, D), BF), pltpu.VMEM((rows, D), BF),
            pltpu.VMEM((rows, 3 * D), BF), pltpu.VMEM((4, 4, 2, quarter, D // 2), BF),
            pltpu.VMEM((4, 4, quarter, D // 2), BF), pltpu.VMEM((4, 4, quarter, D // 2), BF),
            pltpu.VMEM((4, quarter, D // 2), BF), pltpu.VMEM((4, 4, quarter // 4, D // 2), BF),
            pltpu.VMEM((3, 32, D), F32), pltpu.VMEM((9, 32, D), F32), pltpu.VMEM((4, D, D), BF),
            pltpu.VMEM((D, D), BF), pltpu.VMEM((16, rows), F32),
            dma(2, 16), dma(2), dma(2, 4), dma(2, 4), dma(), dma(), dma(2, 4, 4), dma(2, 4, 4), dma(2, 4, 4),
            dma(2, 4, 4), dma(2, 4), dma(2, 7),
        ],
        compiler_params=params(3),
        name="backward",
    )(tok, cot, aux, lse, gate_t, ranks, ggb, dense, qkv, att, hid, ginb, outs, gw, outn)

    def unpadded(array):
        return array.reshape(images, SEQ_PAD, D)[:, :SEQ].reshape(count, D)

    gains = jnp.stack([gain_attn, gain_moe])
    moments = jnp.concatenate([row_in, col_in, row_out, col_out])
    mine, v_new, rows_new, row_router_new, moments_mid, sums, sums_r = pl.pallas_call(
        kernel_s,
        out_shape=(
            shape((32, quarter), F32), shape((2, quarter), F32), shape((quarter, 2), F32), shape((1, quarter), F32),
            shape((8, D), F32), shape((24, D), F32), shape((16, 128), F32),
        ),
        in_specs=[hbm] + [vmem] * 10,
        out_specs=(vmem,) * 7,
        scratch_shapes=[
            pltpu.VMEM((2, 2, D, D), BF), pltpu.VMEM((D, 128), F32), pltpu.VMEM((128, D), F32),
            pltpu.VMEM((24, D), F32), pltpu.VMEM((4, 24, D), F32), pltpu.VMEM((16, 128), F32),
            pltpu.VMEM((4, 16, 128), F32), pltpu.VMEM((quarter, 4 * D), F32), dma(), dma(2, 4), dma(2, 4),
        ],
        compiler_params=params(4),
        name="update_sums",
    )(
        eg, ghat, extra, w_in, w_out, dsh, gains, moments, jnp.stack([row_qkv, row_proj], axis=1), row_router[None],
        jnp.stack([v_attn, v_moe]),
    )
    (
        g_first, g_second, n_first, n_second, dense_rms, expert_rms, n_gain, g_qkv, n_qkv, g_proj, n_proj, n_router,
        cols_new, col_router_new, row_in_new, col_out_new,
    ) = pl.pallas_call(
        kernel_u,
        out_shape=(
            shape((2, D, D), F32), shape((2, D, D), F32), shape((2, D, D), F32), shape((2, D, D), F32),
            shape((1, 128), F32), shape((1, 128), F32), shape((2, quarter), F32),
            shape((quarter, 3 * D), F32), shape((quarter, 3 * D), F32),
            shape((quarter, D), F32), shape((quarter, D), F32), shape((quarter, 16), F32),
            shape((4, D), F32), shape((16, 1), F32), shape((2, D), F32), shape((2, D), F32),
        ),
        in_specs=[hbm] + [vmem] * 15,
        out_specs=(hbm,) * 4 + (vmem,) * 12,
        scratch_shapes=[
            pltpu.VMEM((2, 2, D, D), BF), pltpu.VMEM((4, D, D), F32), pltpu.VMEM((4, D, D), F32),
            pltpu.VMEM((128, D), F32), pltpu.VMEM((128, 256), F32), pltpu.VMEM((quarter, 4 * D), F32),
            dma(), dma(4), dma(4),
        ],
        compiler_params=pltpu.CompilerParams(vmem_limit_bytes=VMEM_LIMIT),
        name="update",
    )(
        eg, ghat, mine, w_in, w_out, dsh, gains, moments, moments_mid, rows_new, row_router_new,
        jnp.concatenate([col_qkv, col_proj]).reshape(4, D), col_router[:, None], v_new, sums, sums_r,
    )
    return (
        unpadded(block_out), unpadded(gtok), dense_rms[0, :5], expert_rms[0, :4].reshape(2, 2).T,
        mine[16], n_gain[0], v_new[0], mine[17], n_gain[1], v_new[1],
        g_qkv, n_qkv, rows_new[:, 0], cols_new[:3].reshape(3 * D),
        g_proj, n_proj, rows_new[:, 1], cols_new[3],
        mine[:16].T, n_router, row_router_new[0], col_router_new[:, 0],
        g_first, n_first, row_in_new, moments_mid[2:4],
        g_second, n_second, moments_mid[0:2], col_out_new,
    )


def local(
    tokens, routes, cotangent, gain_attn, w_qkv, w_proj, gain_moe, w_router, w_in, w_out,
    v_attn, v_moe, row_qkv, col_qkv, row_proj, col_proj, row_router, col_router, row_in, col_in, row_out, col_out,
):
    if (
        lax.axis_size("shard") == 4
        and lax.axis_size("expert") == 8
        and w_in.shape == w_out.shape == (2, D, D)
        and tokens.shape[0] % SEQ == 0
    ):
        return fast(
            tokens, routes, cotangent, gain_attn, w_qkv, w_proj, gain_moe, w_router, w_in, w_out,
            v_attn, v_moe, row_qkv, col_qkv, row_proj, col_proj, row_router, col_router, row_in, col_in, row_out, col_out,
        )
    block_out, grad_tokens, dense_parts, expert_parts = general(
        tokens, routes, cotangent, gain_attn, w_qkv, w_proj, gain_moe, w_router, w_in, w_out
    )
    part_g1, part_qkv, part_proj, part_g2, part_router = dense_parts
    grad_first, grad_second = expert_parts
    expert_count = part_router.shape[1]
    weight_g1 = gain_attn.astype(jnp.float32)
    weight_g2 = gain_moe.astype(jnp.float32)
    dense = (
        (part_qkv, w_qkv.astype(jnp.float32), row_qkv, col_qkv),
        (part_proj, w_proj.astype(jnp.float32), row_proj, col_proj),
        (part_router, w_router.astype(jnp.float32), row_router, col_router),
    )
    weight_first = w_in.astype(jnp.float32)
    weight_second = w_out.astype(jnp.float32)
    v_attn_new = DECAY * v_attn + (1.0 - DECAY) * (part_g1 * part_g1 + EPS_SQUARE)
    v_moe_new = DECAY * v_moe + (1.0 - DECAY) * (part_g2 * part_g2 + EPS_SQUARE)
    raw_g1 = part_g1 * lax.rsqrt(v_attn_new)
    raw_g2 = part_g2 * lax.rsqrt(v_moe_new)
    dense_rows, dense_sums = [], []
    for grad, weight, row, col in dense:
        square = grad * grad
        row_new = DECAY * row + (1.0 - DECAY) * jnp.mean(square + EPS_SQUARE, axis=1)
        dense_rows.append(row_new)
        dense_sums.append(
            (
                jnp.sum(square + EPS_SQUARE, axis=0),
                jnp.sum(square / row_new[:, None], axis=0),
                jnp.stack([jnp.sum(row_new), jnp.sum(weight * weight)]),
            )
        )
    square_first = grad_first * grad_first
    square_second = grad_second * grad_second
    col_in_new = DECAY * col_in + (1.0 - DECAY) * jnp.mean(square_first + EPS_SQUARE, axis=1)
    row_out_new = DECAY * row_out + (1.0 - DECAY) * jnp.mean(square_second + EPS_SQUARE, axis=2)
    gain_sums = jnp.stack(
        [
            jnp.sum(raw_g1 * raw_g1),
            jnp.sum(raw_g2 * raw_g2),
            jnp.sum(weight_g1 * weight_g1),
            jnp.sum(weight_g2 * weight_g2),
        ]
    )
    expert_sums = (
        jnp.sum(square_first + EPS_SQUARE, axis=2),
        jnp.sum(square_first / col_in_new[:, None, :], axis=2),
        jnp.sum(square_second + EPS_SQUARE, axis=1),
        jnp.sum(square_second / row_out_new[:, :, None], axis=1),
        jnp.stack(
            [
                jnp.sum(weight_first * weight_first, axis=(1, 2)),
                jnp.sum(row_out_new, axis=1),
                jnp.sum(weight_second * weight_second, axis=(1, 2)),
            ]
        ),
    )
    expert_sums = lax.psum(expert_sums, "shard")
    dense_sums, gain_sums = lax.psum((dense_sums, gain_sums), "shard")

    def step(square_sum, weight_sum, size):
        rms = jnp.sqrt(square_sum / size)
        return rms, -RATE * jnp.sqrt(weight_sum / size) / jnp.maximum(CLIP, rms)

    rms_g1, factor_g1 = step(gain_sums[0], gain_sums[2], D)
    rms_g2, factor_g2 = step(gain_sums[1], gain_sums[3], D)
    new_g1 = weight_g1 + factor_g1 * raw_g1
    new_g2 = weight_g2 + factor_g2 * raw_g2
    dense_new, dense_cols, dense_rms = [], [], [rms_g1, rms_g2]
    for (grad, weight, _, col), row_new, (col_sum, ratio_sum, both) in zip(dense, dense_rows, dense_sums):
        col_new = DECAY * col + (1.0 - DECAY) * (col_sum / D)
        row_mean = both[0] / D
        rms, factor = step(row_mean * jnp.sum(ratio_sum / col_new), both[1], grad.shape[1] * D)
        raw = grad * lax.rsqrt(row_new[:, None] * col_new[None, :] / row_mean)
        dense_new.append(weight + factor * raw)
        dense_cols.append(col_new)
        dense_rms.append(rms)
    new_qkv, new_proj, new_router = dense_new
    row_qkv_new, row_proj_new, row_router_new = dense_rows
    col_qkv_new, col_proj_new, col_router_new = dense_cols
    row_in_sum, ratio_in, col_out_sum, ratio_out, expert_scalars = expert_sums
    row_in_new = DECAY * row_in + (1.0 - DECAY) * (row_in_sum / FF)
    col_out_new = DECAY * col_out + (1.0 - DECAY) * (col_out_sum / FF)
    mean_in = jnp.mean(row_in_new, axis=1)
    mean_out = expert_scalars[1] / FF
    rms_first, factor_first = step(mean_in * jnp.sum(ratio_in / row_in_new, axis=1), expert_scalars[0], D * FF)
    rms_second, factor_second = step(mean_out * jnp.sum(ratio_out / col_out_new, axis=1), expert_scalars[2], D * FF)
    new_first = weight_first + factor_first[:, None, None] * grad_first * lax.rsqrt(
        row_in_new[:, :, None] * col_in_new[:, None, :] / mean_in[:, None, None]
    )
    new_second = weight_second + factor_second[:, None, None] * grad_second * lax.rsqrt(
        row_out_new[:, :, None] * col_out_new[:, None, :] / mean_out[:, None, None]
    )
    return (
        block_out,
        grad_tokens,
        jnp.stack(dense_rms),
        jnp.stack([rms_first, rms_second], axis=1),
        part_g1,
        new_g1,
        v_attn_new,
        part_g2,
        new_g2,
        v_moe_new,
        part_qkv,
        new_qkv,
        row_qkv_new,
        col_qkv_new,
        part_proj,
        new_proj,
        row_proj_new,
        col_proj_new,
        part_router,
        new_router,
        row_router_new,
        col_router_new,
        grad_first,
        new_first,
        row_in_new,
        col_in_new,
        grad_second,
        new_second,
        row_out_new,
        col_out_new,
    )


def solution(mesh):
    return jax.shard_map(
        local,
        mesh=mesh,
        in_specs=(
            P(("expert", "shard"), None),
            P(("expert", "shard"), None),
            P(("expert", "shard"), None),
            P("shard"),
            P("shard", None),
            P("shard", None),
            P("shard"),
            P("shard", None),
            P("expert", None, "shard"),
            P("expert", "shard", None),
            P("shard"),
            P("shard"),
            P("shard"),
            P(),
            P("shard"),
            P(),
            P("shard"),
            P(),
            P("expert", None),
            P("expert", "shard"),
            P("expert", "shard"),
            P("expert", None),
        ),
        out_specs=(
            P(("expert", "shard"), None),
            P(("expert", "shard"), None),
            P(),
            P("expert", None),
            P("shard"),
            P("shard"),
            P("shard"),
            P("shard"),
            P("shard"),
            P("shard"),
            P("shard", None),
            P("shard", None),
            P("shard"),
            P(),
            P("shard", None),
            P("shard", None),
            P("shard"),
            P(),
            P("shard", None),
            P("shard", None),
            P("shard"),
            P(),
            P("expert", None, "shard"),
            P("expert", None, "shard"),
            P("expert", None),
            P("expert", "shard"),
            P("expert", "shard", None),
            P("expert", "shard", None),
            P("expert", "shard"),
            P("expert", None),
        ),
        check_vma=False,
    )
```
